32 devices in a mesh: dp: 8 (over y, x, core), tensor: 4 (over z).
Axes of the slice: x: 2, y: 2, z: 4, core: 2. Of those that a mesh axis runs over, the one named last changes fastest.
Arguments:
- inputs: bfloat16 [2, 8, 1024, 1024], P(None, 'dp', 'tensor'), may hold values from -6 to 6
- cotangent: bfloat16 [2, 8, 1024, 1024], P(None, 'dp', 'tensor'), may hold values from -6 to 6
- attention_in: float32 [1024, 3, 1024], P('dp', None, 'tensor'), may hold values from -0.1875 to 0.1875
- attention_out: float32 [1024, 1024], P('dp', 'tensor'), may hold values from -3 to 3
- expand_weight: float32 [1024, 2, 2624], P('dp', None, 'tensor'), may hold values from -0.1875 to 0.1875
- contract_weight: float32 [1024, 2624], P('dp', 'tensor'), may hold values from -0.125 to 0.125
- norm_gains: float32 [2, 1024], P(None, 'dp'), may hold values from 0.5 to 1.5
- attention_in_first: float32 [1024, 3, 1024], P('dp', None, 'tensor'), may hold values from -64 to 64
- attention_in_second: float32 [1024, 3, 1024], P('dp', None, 'tensor'), may hold values from 163.84 to 655.36
- attention_out_first: float32 [1024, 1024], P('dp', 'tensor'), may hold values from -6 to 6
- attention_out_second: float32 [1024, 1024], P('dp', 'tensor'), may hold values from 1.6 to 6.4
- expand_first: float32 [1024, 2, 2624], P('dp', None, 'tensor'), may hold values from -32 to 32
- expand_second: float32 [1024, 2, 2624], P('dp', None, 'tensor'), may hold values from 40.96 to 163.84
- contract_first: float32 [1024, 2624], P('dp', 'tensor'), may hold values from -40 to 40
- contract_second: float32 [1024, 2624], P('dp', 'tensor'), may hold values from 65.536 to 262.144
- gains_first: float32 [2, 1024], P(None, 'dp'), may hold values from -80 to 80
- gains_second: float32 [2, 1024], P(None, 'dp'), may hold values from 327.68 to 1310.72
Outputs:
- layer_output: bfloat16 [2, 8, 1024, 1024], P(None, 'dp', 'tensor')
- input_gradient: bfloat16 [2, 8, 1024, 1024], P(None, 'dp', 'tensor')
- attention_in_new: float32 [1024, 3, 1024], P('dp', None, 'tensor')
- attention_in_first_new: float32 [1024, 3, 1024], P('dp', None, 'tensor')
- attention_in_second_new: float32 [1024, 3, 1024], P('dp', None, 'tensor')
- attention_out_new: float32 [1024, 1024], P('dp', 'tensor')
- attention_out_first_new: float32 [1024, 1024], P('dp', 'tensor')
- attention_out_second_new: float32 [1024, 1024], P('dp', 'tensor')
- expand_new: float32 [1024, 2, 2624], P('dp', None, 'tensor')
- expand_first_new: float32 [1024, 2, 2624], P('dp', None, 'tensor')
- expand_second_new: float32 [1024, 2, 2624], P('dp', None, 'tensor')
- contract_new: float32 [1024, 2624], P('dp', 'tensor')
- contract_first_new: float32 [1024, 2624], P('dp', 'tensor')
- contract_second_new: float32 [1024, 2624], P('dp', 'tensor')
- gains_new: float32 [2, 1024], P(None, 'dp')
- gains_first_new: float32 [2, 1024], P(None, 'dp')
- gains_second_new: float32 [2, 1024], P(None, 'dp')
The draws below stay inside these ranges and needn't reach their ends.
All inputs are finite; a program needn't handle non-finite values.
Results may differ from the reference program's by a relative error of at most 0.02.
Values may be sent and summed in bfloat16 or wider, within the bound.
No kernel may reach another device: no remote copies, remote signals or barrier semaphores. Data moves between devices by JAX's collectives and lax.ppermute only.
A program may use at most 192 MiB of HBM per device.

```python
import math
import jax
import jax.numpy as jnp
from jax import lax

D = 1024
H = 16
DH = 64
FF = 2624
SEQ = 1024
MICRO = 2
STEP = 10
GROUPS = 8
TOKENS = 16384


def with_spikes(values, rng, source, target, shards_of, factor):
    def block_of(dim):
        return (jnp.arange(values.shape[dim]) // (values.shape[dim] // shards_of)).reshape((-1,) + (1,) * (values.ndim - 1 - dim))

    near = jax.random.permutation(rng, shards_of)[block_of(target)]
    far = (block_of(target) + shards_of // 2) % shards_of
    return jnp.where((block_of(source) == near) | (block_of(source) == far), factor * values, values)


def shard_levels(key, shape, split, smallest, high):
    factor_of, own = 1.0, jax.random.fold_in(key, 6)
    for dim, blocks in split:
        heights = jnp.exp(jax.random.uniform(jax.random.fold_in(own, dim), (blocks,), jnp.float32, smallest / len(split), high / len(split)))
        factor_of = factor_of * jnp.repeat(heights, shape[dim] // blocks).reshape([-1 if axis == dim else 1 for axis in range(len(shape))])
    return factor_of


def gaussian(own_key, dims, deviation, limit, cuts=(), dtype=jnp.bfloat16):
    gain = shard_levels(own_key, dims, cuts, -0.22, 0.18) if cuts else 1.0
    entries = jax.random.normal(own_key, dims, jnp.float32) * deviation * gain
    return jnp.minimum(jnp.maximum(entries, -limit), limit).astype(dtype)


def bell_draw_with(key, dims, deviation, reach, pieces, heavy, held_as=jnp.bfloat16):
    entries = deviation * jax.random.normal(key, dims, jnp.float32)
    if pieces:
        entries = entries * shard_levels(key, dims, pieces, -0.22, 0.18)
    return jnp.clip(with_spikes(entries, jax.random.fold_in(key, 3), *heavy), -reach, reach).astype(held_as)


def setup_inputs(seed: int = 0) -> dict:
    splits = jax.random.split(jax.random.key(seed), 18)
    inputs = gaussian(splits[0], (MICRO, GROUPS, SEQ, D), 1.0, 6.0, ((1, 8), (2, 4)))
    cotangent = bell_draw_with(splits[1], (MICRO, GROUPS, SEQ, D), 1.0, 6.0, ((1, 8), (2, 4)), (1, 3, 8, 2.0))
    attention_in = gaussian(splits[2], (D, 3, H * DH), D ** -0.5, 0.1875, ((0, 8), (2, 4)), jnp.float32)
    attention_out = gaussian(splits[3], (D, H * DH), (max(1, 4 * H * DH // SEQ)) ** -0.5, 3.0, ((0, 8), (1, 4)), jnp.float32)
    expand_weight = gaussian(splits[4], (D, 2, FF), D ** -0.5, 0.1875, ((0, 8), (2, 4)), jnp.float32)
    contract_weight = gaussian(splits[5], (D, FF), FF ** -0.5, 0.125, ((0, 8), (1, 4)), jnp.float32)
    norm_gains = jnp.clip(1.0 + 0.1 * jax.random.normal(splits[6], (2, D), jnp.float32), 0.5, 1.5)
    attention_in_first = gaussian(splits[7], (D, 3, H * DH), (0.08 * TOKENS ** 0.5), 64.0, ((0, 8), (2, 4)), jnp.float32)
    attention_in_second = jnp.clip(jnp.exp(math.log(655.36) - 1.3862944 * jax.random.uniform(splits[8], (D, 3, H * DH), jnp.float32) ** shard_levels(splits[8], (D, 3, H * DH), ((0, 8), (2, 4)), -0.2, 0.2)), 163.84, 655.36)
    attention_out_first = gaussian(splits[9], (D, H * DH), (0.25 * (TOKENS / SEQ) ** 0.5), 6.0, ((0, 8), (1, 4)), jnp.float32)
    attention_out_second = jnp.clip(jnp.exp(math.log(6.4) - 1.3862944 * jax.random.uniform(splits[10], (D, H * DH), jnp.float32) ** shard_levels(splits[10], (D, H * DH), ((0, 8), (1, 4)), -0.2, 0.2)), 1.6, 6.4)
    expand_first = gaussian(splits[11], (D, 2, FF), (0.04 * TOKENS ** 0.5), 32.0, ((0, 8), (2, 4)), jnp.float32)
    expand_second = jnp.clip(jnp.exp(math.log(163.84) - 1.3862944 * jax.random.uniform(splits[12], (D, 2, FF), jnp.float32) ** shard_levels(splits[12], (D, 2, FF), ((0, 8), (2, 4)), -0.2, 0.2)), 40.96, 163.84)
    contract_first = gaussian(splits[13], (D, FF), (0.05 * TOKENS ** 0.5), 40.0, ((0, 8), (1, 4)), jnp.float32)
    contract_second = jnp.clip(jnp.exp(math.log(262.144) - 1.3862944 * jax.random.uniform(splits[14], (D, FF), jnp.float32) ** shard_levels(splits[14], (D, FF), ((0, 8), (1, 4)), -0.2, 0.2)), 65.536, 262.144)
    gains_first = gaussian(splits[15], (2, D), (0.11 * TOKENS ** 0.5), 80.0, ((1, 8),), jnp.float32)
    gains_second = jnp.clip(jnp.exp(math.log(1310.72) - 1.3862944 * jax.random.uniform(splits[16], (2, D), jnp.float32) ** shard_levels(splits[16], (2, D), ((1, 8),), -0.2, 0.2)), 327.68, 1310.72)
    return dict(inputs=inputs, cotangent=cotangent, attention_in=attention_in, attention_out=attention_out, expand_weight=expand_weight, contract_weight=contract_weight, norm_gains=norm_gains, attention_in_first=attention_in_first, attention_in_second=attention_in_second, attention_out_first=attention_out_first, attention_out_second=attention_out_second, expand_first=expand_first, expand_second=expand_second, contract_first=contract_first, contract_second=contract_second, gains_first=gains_first, gains_second=gains_second)


@jax.custom_vjp
def low(v):
    return lax.optimization_barrier(v.astype(jnp.bfloat16)).astype(jnp.float32)

@jax.custom_vjp
def low_back(v):
    return v

def low_keep(v):
    return (low(v), None)

def low_pass(kept, grad):
    return (grad,)

def back_keep(v):
    return (v, None)

def back_low(kept, grad):
    return (low(grad),)
low.defvjp(low_keep, low_pass)
low_back.defvjp(back_keep, back_low)
epsilon_norm = 1e-05
rope_theta = 160000.0
beta_first = 0.9
beta_second = 0.98
epsilon_adam = 1e-06
weight_decay = 1e-05
highest = lax.Precision.HIGHEST

def layer_norm(values):
    centered = values - lax.optimization_barrier(jnp.mean(values, axis=-1, keepdims=True))
    variance = lax.optimization_barrier(jnp.mean(centered * centered, axis=-1, keepdims=True))
    return centered * lax.rsqrt(variance + epsilon_norm)

def rotary_tables(seq_length, head_size):
    positions = jnp.arange(seq_length).astype(jnp.float32)
    exponents = jnp.arange(0, head_size, 2).astype(jnp.float32) / head_size
    angles = positions[:, None] * jnp.power(rope_theta, -exponents)[None, :]
    angles = jnp.concatenate([angles, angles], axis=-1)
    return (jnp.cos(angles), jnp.sin(angles))

def rotate(values, cosine, sine):
    half_size = values.shape[-1] // 2
    turned = jnp.concatenate([-values[..., half_size:], values[..., :half_size]], axis=-1)
    return values * cosine[:, None, :] + turned * sine[:, None, :]

def attend_block(query_block, key_rows, value_rows):
    scores = low_back(jnp.einsum('qhd,khd->hqk', query_block, key_rows, precision=highest) * DH ** (-0.5))
    soft_weights = low(jax.nn.softmax(scores, axis=-1))
    return jnp.einsum('hqk,khd->qhd', soft_weights, value_rows, precision=highest)

def attention(queries, key_rows, value_rows):
    block_rows = min(512, SEQ)

    def one_block(query_block):
        return attend_block(query_block, key_rows, value_rows)
    blocks_out = lax.map(jax.checkpoint(one_block), queries.reshape(SEQ // block_rows, block_rows, H, DH))
    return blocks_out.reshape(SEQ, H * DH)

def layer(sequence, attn_in, attn_out, expand, contract, gains):
    gain_low = low(gains)
    normed = low(layer_norm(sequence) * gain_low[0])
    mixed_rows = low_back(jnp.dot(normed, low(attn_in).reshape(D, 3 * H * DH), precision=highest))
    mixed_rows = mixed_rows.reshape(SEQ, 3, H, DH)
    cosine, sine = rotary_tables(SEQ, DH)
    queries = low(rotate(mixed_rows[:, 0], cosine, sine))
    key_rows = low(rotate(mixed_rows[:, 1], cosine, sine))
    value_rows = low(mixed_rows[:, 2])
    attended = low_back(low(attention(queries, key_rows, value_rows)))
    branch = low_back(jnp.dot(attended, low(attn_out).T, precision=highest))
    middle = sequence + branch
    normed_two = low(layer_norm(middle) * gain_low[1])
    lifted = low_back(jnp.dot(normed_two, low(expand).reshape(D, 2 * FF), precision=highest))
    hidden = low(jax.nn.gelu(lifted[:, :FF], approximate=False) * lifted[:, FF:])
    branch_two = low_back(jnp.dot(hidden, low(contract).T, precision=highest))
    return middle + branch_two

def adamw_update(weight, first_moment, second_moment, gradient, step_rate):
    first_new = beta_first * first_moment + (1.0 - beta_first) * gradient
    second_new = beta_second * second_moment + (1.0 - beta_second) * gradient * gradient
    first_hat = first_new / (1.0 - beta_first ** STEP)
    second_hat = second_new / (1.0 - beta_second ** STEP)
    weight_new = weight - step_rate * (first_hat / (jnp.sqrt(second_hat) + epsilon_adam) + weight_decay * weight)
    return (weight_new, first_new, second_new)

def reference(inputs, cotangent, attention_in, attention_out, expand_weight, contract_weight, norm_gains, attention_in_first, attention_in_second, attention_out_first, attention_out_second, expand_first, expand_second, contract_first, contract_second, gains_first, gains_second):
    seq_count = MICRO * GROUPS
    flat_inputs = inputs.reshape(seq_count, SEQ, D).astype(jnp.float32)
    flat_cotangent = cotangent.reshape(seq_count, SEQ, D).astype(jnp.float32)
    weights = (attention_in, attention_out, expand_weight, contract_weight, norm_gains)

    def one_sequence(totals, sequence_pair):
        sequence, sequence_grad = sequence_pair
        result, backward = jax.vjp(layer, sequence, *weights)
        grad_list = backward(sequence_grad)
        totals = tuple((summed + fresh_grad for summed, fresh_grad in zip(totals, grad_list[1:])))
        return (totals, (result.astype(jnp.bfloat16), grad_list[0].astype(jnp.bfloat16)))
    zeros_start = tuple((jnp.zeros(weight.shape, jnp.float32) for weight in weights))
    totals, (outputs, input_grads) = lax.scan(one_sequence, zeros_start, (flat_inputs, flat_cotangent))
    step_rates = (2.5 * D ** (-0.5), 2.5 * max(1, 4 * H * DH // SEQ) ** (-0.5), 2.5 * D ** (-0.5), 2.5 * FF ** (-0.5), 0.25)
    qkv_new = adamw_update(attention_in, attention_in_first, attention_in_second, totals[0], step_rates[0])
    out_new = adamw_update(attention_out, attention_out_first, attention_out_second, totals[1], step_rates[1])
    expand_new = adamw_update(expand_weight, expand_first, expand_second, totals[2], step_rates[2])
    contract_new = adamw_update(contract_weight, contract_first, contract_second, totals[3], step_rates[3])
    gains_new = adamw_update(norm_gains, gains_first, gains_second, totals[4], step_rates[4])
    return (outputs.reshape(MICRO, GROUPS, SEQ, D), input_grads.reshape(MICRO, GROUPS, SEQ, D), qkv_new[0], qkv_new[1], qkv_new[2], out_new[0], out_new[1], out_new[2], expand_new[0], expand_new[1], expand_new[2], contract_new[0], contract_new[1], contract_new[2], gains_new[0], gains_new[1], gains_new[2])
```

```python
import jax
import jax.numpy as jnp
from jax import lax
from jax.experimental import pallas as pl
from jax.experimental.pallas import tpu as pltpu
from jax.sharding import PartitionSpec as P

D = 1024
H = 16
DH = 64
FF = 2624
SEQ = 1024
STEP = 10

epsilon_norm = 1e-05
rope_theta = 160000.0
beta_first = 0.9
beta_second = 0.98
epsilon_adam = 1e-06
weight_decay = 1e-05

AXES = ("dp", "tensor")
bf16 = jnp.bfloat16
f32 = jnp.float32


def dot_nt(left, right):
    return lax.dot_general(left, right, (((1,), (1,)), ((), ())), preferred_element_type=f32)


def dot_tn(left, right):
    return lax.dot_general(left, right, (((0,), (0,)), ((), ())), preferred_element_type=f32)


def dot_nn(left, right):
    return jnp.dot(left, right, preferred_element_type=f32)


def adamw_update(weight, first_moment, second_moment, gradient, step_rate):
    first_new = beta_first * first_moment + (1.0 - beta_first) * gradient
    second_new = beta_second * second_moment + (1.0 - beta_second) * gradient * gradient
    first_hat = first_new / (1.0 - beta_first**STEP)
    second_hat = second_new / (1.0 - beta_second**STEP)
    weight_new = weight - step_rate * (
        first_hat / (jnp.sqrt(second_hat) + epsilon_adam) + weight_decay * weight
    )
    return (weight_new, first_new, second_new)


def swap_halves(values):
    lane = lax.broadcasted_iota(jnp.int32, values.shape, 1)
    return jnp.where(
        lane % DH < DH // 2,
        pltpu.roll(values, values.shape[1] - DH // 2, 1),
        pltpu.roll(values, DH // 2, 1),
    )


def qkv_kernel(own_ref, oth_ref, w_own_ref, w_oth_ref, cos_ref, sin_ref, q_ref, kv_ref):
    mixed = dot_nt(own_ref[...], w_own_ref[0]) + dot_nt(oth_ref[...], w_oth_ref[0])
    cosine, sine = cos_ref[...], sin_ref[...]
    query, key = mixed[:, :128], mixed[:, 128:256]
    query = query * cosine + swap_halves(query) * sine
    key = key * cosine + swap_halves(key) * sine
    q_ref[...] = query.astype(bf16) * bf16(DH**-0.5)
    kv_ref[:, :128] = key.astype(bf16)
    kv_ref[:, 128:] = mixed[:, 256:].astype(bf16)


def qkv_call(own, oth, w_own, w_oth, cosine, sine):
    rows = own.shape[0]
    blocks = w_own.shape[0]
    whole = lambda a: pl.BlockSpec(a.shape, lambda z: (0, 0))
    weight = pl.BlockSpec((1,) + w_own.shape[1:], lambda z: (z, 0, 0))
    return pl.pallas_call(
        qkv_kernel,
        grid=(blocks,),
        in_specs=[whole(own), whole(oth), weight, weight, whole(cosine), whole(sine)],
        out_specs=[
            pl.BlockSpec((rows, 128), lambda z: (0, z)),
            pl.BlockSpec((rows, 256), lambda z: (0, z)),
        ],
        out_shape=[
            jax.ShapeDtypeStruct((rows, blocks * 128), bf16),
            jax.ShapeDtypeStruct((rows, blocks * 256), bf16),
        ],
        compiler_params=pltpu.CompilerParams(vmem_limit_bytes=40 << 20),
        cost_estimate=pl.CostEstimate(
            flops=2 * rows * w_own.shape[1] * blocks * 2 * own.shape[1],
            bytes_accessed=4 * w_own.size + 8 * own.size,
            transcendentals=0,
        ),
        name="qkv_projection",
    )(own, oth, w_own, w_oth, cosine, sine)


def attend_kernel(q_ref, kv_own_ref, kv_oth_ref, out_ref, lse_ref):
    query = q_ref[...]
    key = jnp.concatenate([kv_own_ref[:, :128], kv_oth_ref[:, :128]], axis=0)
    value = jnp.concatenate([kv_own_ref[:, 128:], kv_oth_ref[:, 128:]], axis=0)
    value_t = value.astype(f32).T.astype(bf16)
    lane = lax.broadcasted_iota(jnp.int32, query.shape, 1)
    outs = []
    for head in range(2):
        query_head = jnp.where(lane // DH == head, query, jnp.zeros_like(query))
        scores = dot_nt(key, query_head)
        peak = jnp.max(scores, axis=0, keepdims=True)
        weights = jnp.exp(scores - peak)
        total = jnp.sum(weights, axis=0, keepdims=True)
        out = dot_nn(value_t[head * DH : (head + 1) * DH], weights.astype(bf16))
        outs.append(out / total)
        lse_ref[0, head : head + 1, :] = peak + jnp.log(total)
    out_ref[...] = jnp.concatenate(outs, axis=0).T.astype(bf16)


def attend_call(query, kv_own, kv_oth):
    rows = query.shape[0]
    blocks = query.shape[1] // 128
    kv_spec = pl.BlockSpec((rows, 256), lambda z: (0, z))
    q_spec = pl.BlockSpec((rows, 128), lambda z: (0, z))
    return pl.pallas_call(
        attend_kernel,
        grid=(blocks,),
        in_specs=[q_spec, kv_spec, kv_spec],
        out_specs=[q_spec, pl.BlockSpec((1, 2, rows), lambda z: (z, 0, 0))],
        out_shape=[
            jax.ShapeDtypeStruct(query.shape, bf16),
            jax.ShapeDtypeStruct((blocks, 2, rows), f32),
        ],
        compiler_params=pltpu.CompilerParams(vmem_limit_bytes=48 << 20),
        cost_estimate=pl.CostEstimate(
            flops=16 * rows * 2 * rows * 128 * blocks,
            bytes_accessed=12 * rows * 128 * blocks,
            transcendentals=4 * rows * rows * blocks,
        ),
        name="attention_forward",
    )(query, kv_own, kv_oth)


def attend_back_kernel(
    q_ref, kv_own_ref, kv_oth_ref, grad_ref, out_ref, lse_ref, cos_ref, sin_ref,
    dq_ref, dkv_own_ref, dkv_oth_ref,
):
    query, grad = q_ref[...], grad_ref[...]
    rows = query.shape[0]
    key = jnp.concatenate([kv_own_ref[:, :128], kv_oth_ref[:, :128]], axis=0)
    value = jnp.concatenate([kv_own_ref[:, 128:], kv_oth_ref[:, 128:]], axis=0)
    key_t = key.astype(f32).T.astype(bf16)
    product_t = (grad.astype(f32) * out_ref[...].astype(f32)).T
    lane = lax.broadcasted_iota(jnp.int32, query.shape, 1)
    grad_key = jnp.zeros((2 * rows, 128), f32)
    grad_value = jnp.zeros((2 * rows, 128), f32)
    grad_queries = []
    for head in range(2):
        mine = lane // DH == head
        query_head = jnp.where(mine, query, jnp.zeros_like(query))
        grad_head = jnp.where(mine, grad, jnp.zeros_like(grad))
        delta = jnp.sum(product_t[head * DH : (head + 1) * DH], axis=0, keepdims=True)
        weights = jnp.exp(dot_nt(key, query_head) - lse_ref[0, head : head + 1, :])
        grad_soft = dot_nt(value, grad_head)
        grad_scores = (weights * (grad_soft - delta)).astype(bf16)
        grad_value += dot_nn(weights.astype(bf16), grad_head)
        grad_key += dot_nn(grad_scores, query_head)
        grad_queries.append(dot_nn(key_t[head * DH : (head + 1) * DH], grad_scores))
    grad_query = jnp.concatenate(grad_queries, axis=0).T * (DH**-0.5)
    cosine, sine = cos_ref[...], sin_ref[...]
    dq_ref[...] = (grad_query * cosine - swap_halves(grad_query) * sine).astype(bf16)
    dkv_own_ref[:, :128] = grad_key[:rows]
    dkv_own_ref[:, 128:] = grad_value[:rows]
    dkv_oth_ref[:, :128] = grad_key[rows:].astype(bf16)
    dkv_oth_ref[:, 128:] = grad_value[rows:].astype(bf16)


def attend_back_call(query, kv_own, kv_oth, grad, out, lse, cosine, sine):
    rows = query.shape[0]
    blocks = query.shape[1] // 128
    kv_spec = pl.BlockSpec((rows, 256), lambda z: (0, z))
    q_spec = pl.BlockSpec((rows, 128), lambda z: (0, z))
    whole = lambda a: pl.BlockSpec(a.shape, lambda z: (0, 0))
    return pl.pallas_call(
        attend_back_kernel,
        grid=(blocks,),
        in_specs=[
            q_spec, kv_spec, kv_spec, q_spec, q_spec,
            pl.BlockSpec((1, 2, rows), lambda z: (z, 0, 0)), whole(cosine), whole(sine),
        ],
        out_specs=[q_spec, kv_spec, kv_spec],
        out_shape=[
            jax.ShapeDtypeStruct(query.shape, bf16),
            jax.ShapeDtypeStruct(kv_own.shape, f32),
            jax.ShapeDtypeStruct(kv_own.shape, bf16),
        ],
        compiler_params=pltpu.CompilerParams(vmem_limit_bytes=56 << 20),
        cost_estimate=pl.CostEstimate(
            flops=40 * rows * 2 * rows * 128 * blocks,
            bytes_accessed=30 * rows * 128 * blocks,
            transcendentals=4 * rows * rows * blocks,
        ),
        name="attention_backward",
    )(query, kv_own, kv_oth, grad, out, lse, cosine, sine)


def join_kernel(dq_ref, own_ref, got_ref, cos_ref, sin_ref, mixed_ref):
    total = own_ref[...] + got_ref[...].astype(f32)
    key = total[:, :128]
    mixed_ref[:, :128] = dq_ref[...]
    mixed_ref[:, 128:256] = (key * cos_ref[...] - swap_halves(key) * sin_ref[...]).astype(bf16)
    mixed_ref[:, 256:] = total[:, 128:].astype(bf16)


def join_call(dq, dkv_own, dkv_got, cosine, sine):
    rows = dq.shape[0]
    blocks = dq.shape[1] // 128
    spec = lambda width: pl.BlockSpec((rows, width), lambda z: (0, z))
    whole = lambda a: pl.BlockSpec(a.shape, lambda z: (0, 0))
    return pl.pallas_call(
        join_kernel,
        grid=(blocks,),
        in_specs=[spec(128), spec(256), spec(256), whole(cosine), whole(sine)],
        out_specs=spec(384),
        out_shape=jax.ShapeDtypeStruct((rows, 384 * blocks), bf16),
        cost_estimate=pl.CostEstimate(
            flops=rows * 384 * blocks, bytes_accessed=10 * rows * 256 * blocks, transcendentals=0
        ),
        name="grad_mixed",
    )(dq, dkv_own, dkv_got, cosine, sine)


def norm_stats(halves):
    width = sum(h.shape[1] for h in halves)
    mean = sum(jnp.sum(h, axis=1, keepdims=True) for h in halves) / width
    centered = [h - mean for h in halves]
    variance = sum(jnp.sum(c * c, axis=1, keepdims=True) for c in centered) / width
    return mean, lax.rsqrt(variance + epsilon_norm)


def norm_back(grads, halves, mean, scale, gains):
    width = sum(h.shape[1] for h in halves)
    hats = [(h - mean) * scale for h in halves]
    gain_grads = [jnp.sum(g * n, axis=0) for g, n in zip(grads, hats)]
    errors = [g * gain[None, :] for g, gain in zip(grads, gains)]
    average = sum(jnp.sum(e, axis=1, keepdims=True) for e in errors) / width
    along = sum(jnp.sum(e * n, axis=1, keepdims=True) for e, n in zip(errors, hats)) / width
    return [scale * (e - average - n * along) for e, n in zip(errors, hats)], gain_grads


def make_per_device(dp, tensor):
    count = dp * tensor
    chips = dp // 2
    chip_bits = chips.bit_length() - 1

    def permute(value, pairs):
        return lax.ppermute(value, AXES, pairs)

    def exchange(value, mask):
        return permute(value, [(i, i ^ mask) for i in range(count)])

    def over_chip(value, bit):
        return exchange(value, (2 * tensor) << bit)

    def over_core(value):
        return exchange(value, tensor)

    def spread_pairs(r, k):
        pairs = []
        for i in range(count):
            z = i % tensor
            core = (i // tensor) % 2
            chip = i // (2 * tensor)
            a, b = z // 2, z % 2
            pairs.append((i, (chip * 2 + (k ^ b)) * tensor + (r ^ a) * 2 + core))
        return pairs

    combos = [(r, k) for r in range(2) for k in range(2)]

    def gather_chunks(chunks):
        if chip_bits != 2:
            results = []
            for chunk in chunks:
                current = jnp.stack([chunk] + [exchange(chunk, k) for k in range(1, tensor)])[None]
                for bit in range(chip_bits):
                    current = jnp.concatenate([current, over_chip(current, bit)], axis=0)
                current = current.transpose(1, 2, 0, 3)
                current = current.reshape(current.shape[:2] + (-1,))
                results.append((current, over_core(current)))
            return results
        total = len(chunks)
        column, near, far, owned, results = ({} for _ in range(5))
        before = None
        for slot in range(total + 3):
            inputs = {}
            if slot < total:
                inputs["a"] = chunks[slot]
            if 0 <= slot - 1 < total:
                inputs["b"] = column[slot - 1]
            if 0 <= slot - 2 < total:
                x_got, y_got = near[slot - 2]
                inputs["c"] = (x_got[: tensor // 2], y_got[tensor // 2 :])
            if 0 <= slot - 3 < total:
                inputs["d"] = owned[slot - 3]
            if before is not None:
                inputs, before = lax.optimization_barrier((inputs, before))
            outputs = {}
            if "c" in inputs:
                outputs["c"] = (over_chip(inputs["c"][0], 1), over_chip(inputs["c"][1], 0))
            if "b" in inputs:
                outputs["b"] = (over_chip(inputs["b"], 0), over_chip(inputs["b"], 1))
            if "a" in inputs:
                outputs["a"] = [exchange(inputs["a"], k) for k in range(1, tensor)]
            if "d" in inputs:
                outputs["d"] = over_core(inputs["d"])
            if "a" in inputs:
                column[slot] = jnp.stack([inputs["a"]] + outputs["a"])
            if "b" in inputs:
                near[slot - 1] = outputs["b"]
            if "c" in inputs:
                k = slot - 2
                diagonal = jnp.concatenate(outputs["c"], axis=0)
                owned[k] = jnp.concatenate([column[k], near[k][0], near[k][1], diagonal], axis=-1)
            if "d" in inputs:
                results[slot - 3] = (inputs["d"], outputs["d"])
            before = outputs
        return [results[k] for k in range(total)]

    def low_sum(left, right):
        return (left.astype(f32) + right.astype(f32)).astype(bf16)

    def reduce_chunk(own, other):
        block = own.shape[-1] // chips
        total = low_sum(own, over_core(other))
        parts = [total[..., j * block : (j + 1) * block] for j in range(chips)]
        if chip_bits != 2:
            current = jnp.stack(parts)
            for bit in reversed(range(chip_bits)):
                half = current.shape[0] // 2
                current = low_sum(current[:half], over_chip(current[half:], bit))
            mine = current[0]
        else:
            mine, x_part, y_part, diagonal = parts
            half = tensor // 2
            to_y = over_chip(diagonal[:half], 0)
            to_x = over_chip(diagonal[half:], 1)
            y_part = jnp.concatenate([low_sum(y_part[:half], to_y), y_part[half:]], axis=0)
            x_part = jnp.concatenate([x_part[:half], low_sum(x_part[half:], to_x)], axis=0)
            x_got, y_got = over_chip(x_part, 0), over_chip(y_part, 1)
            mine = (mine.astype(f32) + x_got.astype(f32) + y_got.astype(f32)).astype(bf16)
        result = mine[0].astype(f32)
        for k in range(1, tensor):
            result = result + exchange(mine[k], k).astype(f32)
        return result

    def per_device(
        inputs,
        cotangent,
        attention_in,
        attention_out,
        expand_weight,
        contract_weight,
        norm_gains,
        attention_in_first,
        attention_in_second,
        attention_out_first,
        attention_out_second,
        expand_first,
        expand_second,
        contract_first,
        contract_second,
        gains_first,
        gains_second,
    ):
        block = attention_in.shape[0]
        head_columns = attention_in.shape[2]
        hidden_local = expand_weight.shape[2]
        local_rows = inputs.shape[2]
        piece = local_rows // 2
        width = inputs.shape[3]
        me_dp = lax.axis_index("dp")
        me_z = lax.axis_index("tensor")
        core = me_dp % 2
        z_high, z_low = me_z // 2, me_z % 2

        order = [(j % chips) * 2 + j // chips for j in range(dp)]

        def to_relative(values):
            pieces = [
                lax.dynamic_slice_in_dim(values, (me_dp ^ o) * block, block, values.ndim - 1)
                for o in order
            ]
            return (
                jnp.concatenate(pieces[:chips], axis=-1),
                jnp.concatenate(pieces[chips:], axis=-1),
            )

        def from_relative(own, other):
            both = jnp.concatenate([own, other], axis=-1)
            pieces = []
            for i in range(dp):
                relative = me_dp ^ i
                j = (relative % 2) * chips + relative // 2
                pieces.append(lax.dynamic_slice_in_dim(both, j * block, block, both.ndim - 1))
            return jnp.concatenate(pieces, axis=-1)

        def spread(values):
            got = []
            for r, k in combos:
                part = lax.dynamic_index_in_dim(values[:, 0], r ^ z_high, 0, keepdims=False)
                part = lax.dynamic_slice_in_dim(part, (k ^ z_low) * piece, piece, 0)
                got.append(permute(part, spread_pairs(r, k)))
            return jnp.concatenate(got, axis=0)

        def collect(values):
            back = []
            for index, (r, k) in enumerate(combos):
                part = values[index * piece : (index + 1) * piece]
                back.append(permute(part, [(b, a) for a, b in spread_pairs(r, k)]))
            back = jnp.stack(back)
            rows = []
            for m in range(2):
                halves = [
                    lax.dynamic_index_in_dim(
                        back, (m ^ z_high) * 2 + (h ^ z_low), 0, keepdims=False
                    )
                    for h in range(2)
                ]
                rows.append(jnp.concatenate(halves, axis=0))
            return jnp.stack(rows)[:, None]

        low_in = attention_in.astype(bf16).reshape(block, 3, 2, head_columns // 2)
        low_in = low_in.transpose(2, 1, 3, 0).reshape(2, -1, block)
        low_out = attention_out.astype(bf16).T
        low_expand = expand_weight.astype(bf16).transpose(1, 2, 0)
        low_contract = contract_weight.astype(bf16).T
        gathered = gather_chunks(
            [low_in[0], low_in[1], low_out, low_expand[0], low_expand[1], low_contract]
        )
        w_in = gathered[:2]
        flat = lambda a: a.reshape(-1, a.shape[-1])
        w_out, w_up, w_gate, w_down = [tuple(flat(h) for h in pair) for pair in gathered[2:]]
        gains = lax.all_gather(norm_gains.astype(bf16), "dp", axis=1, tiled=True).astype(f32)
        gain_own, gain_oth = to_relative(gains)
        gain_one = (gain_own[0], gain_oth[0])
        gain_two = (gain_own[1], gain_oth[1])

        starts = [((r ^ z_high) * 2 + (k ^ core)) * local_rows + core * piece for r, k in combos]
        positions = jnp.concatenate([s + jnp.arange(piece) for s in starts]).astype(f32)
        exponents = jnp.arange(0, DH, 2).astype(f32) / DH
        angles = positions[:, None] * jnp.power(rope_theta, -exponents)[None, :]
        cosine, sine = jnp.cos(angles), jnp.sin(angles)
        cosine = jnp.concatenate([cosine] * 4, axis=-1)
        sine = jnp.concatenate([-sine, sine] * 2, axis=-1)

        sequence = to_relative(spread(inputs))
        sequence = [h.astype(f32) for h in sequence]
        mean_one, scale_one = norm_stats(sequence)
        normed = [
            ((h - mean_one) * scale_one * g[None, :]).astype(bf16)
            for h, g in zip(sequence, gain_one)
        ]
        queries, kv_own, kv_oth, attended, lse = [], [], [], [], []
        for p in range(2):
            q, kv = qkv_call(*normed, *w_in[p], cosine, sine)
            got = over_core(kv)
            out, totals = attend_call(q, kv, got)
            queries.append(q)
            kv_own.append(kv)
            kv_oth.append(got)
            attended.append(out)
            lse.append(totals)
        rows = attended[0].shape[0]
        attended_all = jnp.stack([a.reshape(rows, tensor, -1) for a in attended], axis=2)
        attended_all = attended_all.reshape(rows, -1)
        middle = [s + dot_nn(attended_all, w) for s, w in zip(sequence, w_out)]
        mean_two, scale_two = norm_stats(middle)
        normed_two = [
            ((h - mean_two) * scale_two * g[None, :]).astype(bf16)
            for h, g in zip(middle, gain_two)
        ]
        lifted_in = dot_nt(normed_two[0], w_up[0]) + dot_nt(normed_two[1], w_up[1])
        lifted_gate = dot_nt(normed_two[0], w_gate[0]) + dot_nt(normed_two[1], w_gate[1])
        phi = 0.5 * (1.0 + lax.erf(lifted_in * (0.5**0.5)))
        gelu = lifted_in * phi
        hidden = (gelu * lifted_gate).astype(bf16)
        slope = phi + lifted_in * jnp.exp(-0.5 * lifted_in * lifted_in) * 0.3989422804014327
        to_gate = gelu.astype(bf16)
        to_in = (lifted_gate * slope).astype(bf16)
        outputs = [
            (m + dot_nn(hidden, w)).astype(bf16) for m, w in zip(middle, w_down)
        ]
        layer_output = collect(from_relative(*outputs))

        grad_rows = to_relative(spread(cotangent))

        def shards(left, right):
            grads = dot_tn(left, right).astype(bf16)
            return grads.reshape(tensor, -1, grads.shape[-1])

        grad_down = reduce_chunk(*[shards(hidden, g) for g in grad_rows])
        grad_hidden = dot_nt(grad_rows[0], w_down[0]) + dot_nt(grad_rows[1], w_down[1])
        grad_in = (grad_hidden * to_in.astype(f32)).astype(bf16)
        grad_gate = (grad_hidden * to_gate.astype(f32)).astype(bf16)
        grad_up = reduce_chunk(*[shards(grad_in, n) for n in normed_two])
        grad_gates = reduce_chunk(*[shards(grad_gate, n) for n in normed_two])
        grad_two = [dot_nn(grad_in, u) + dot_nn(grad_gate, g) for u, g in zip(w_up, w_gate)]
        back_two, gain_two_grad = norm_back(grad_two, middle, mean_two, scale_two, gain_two)
        grad_middle = [g.astype(f32) + b for g, b in zip(grad_rows, back_two)]
        middle_low = [g.astype(bf16) for g in grad_middle]
        grad_out = reduce_chunk(*[shards(attended_all, m) for m in middle_low])
        grad_attended = dot_nt(middle_low[0], w_out[0]) + dot_nt(middle_low[1], w_out[1])
        grad_attended = grad_attended.astype(bf16).reshape(rows, tensor, 2, -1)
        grad_in_parts, grad_one = [], [0.0, 0.0]
        for p in range(2):
            dq, dkv, dkv_far = attend_back_call(
                queries[p],
                kv_own[p],
                kv_oth[p],
                grad_attended[:, :, p].reshape(rows, -1),
                attended[p],
                lse[p],
                cosine,
                sine,
            )
            grad_mixed = join_call(dq, dkv, over_core(dkv_far), cosine, sine)
            grad_in_parts.append(reduce_chunk(*[shards(grad_mixed, n) for n in normed]))
            grad_one = [g + dot_nn(grad_mixed, flat(w)) for g, w in zip(grad_one, w_in[p])]
        back_one, gain_one_grad = norm_back(grad_one, sequence, mean_one, scale_one, gain_one)
        input_grads = [(g + b).astype(bf16) for g, b in zip(grad_middle, back_one)]
        input_gradient = collect(from_relative(*input_grads))

        gain_grads = jnp.stack(
            [from_relative(*gain_one_grad), from_relative(*gain_two_grad)]
        )
        gain_total = lax.psum(gain_grads, AXES)
        gain_total = lax.dynamic_slice_in_dim(gain_total, me_dp * block, block, 1)
        grad_qkv = jnp.stack([g.reshape(3, -1, block) for g in grad_in_parts], axis=1)
        grad_qkv = grad_qkv.reshape(3, head_columns, block).transpose(2, 0, 1)
        grad_expand = jnp.stack([grad_up, grad_gates]).transpose(2, 0, 1)
        step_rates = (
            2.5 * D ** (-0.5),
            2.5 * max(1, 4 * H * DH // SEQ) ** (-0.5),
            2.5 * D ** (-0.5),
            2.5 * FF ** (-0.5),
            0.25,
        )
        qkv_new = adamw_update(
            attention_in, attention_in_first, attention_in_second, grad_qkv, step_rates[0]
        )
        out_new = adamw_update(
            attention_out, attention_out_first, attention_out_second, grad_out.T, step_rates[1]
        )
        expand_new = adamw_update(
            expand_weight, expand_first, expand_second, grad_expand, step_rates[2]
        )
        contract_new = adamw_update(
            contract_weight, contract_first, contract_second, grad_down.T, step_rates[3]
        )
        gains_new = adamw_update(norm_gains, gains_first, gains_second, gain_total, step_rates[4])
        return (
            layer_output,
            input_gradient,
            *qkv_new,
            *out_new,
            *expand_new,
            *contract_new,
            *gains_new,
        )

    return per_device


def solution(mesh):
    activation = P(None, "dp", "tensor", None)
    cube = P("dp", None, "tensor")
    flat = P("dp", "tensor")
    gain = P(None, "dp")
    return jax.shard_map(
        make_per_device(mesh.shape["dp"], mesh.shape["tensor"]),
        mesh=mesh,
        in_specs=(
            activation, activation, cube, flat, cube, flat, gain,
            cube, cube, flat, flat, cube, cube, flat, flat, gain, gain,
        ),
        out_specs=(
            activation, activation, cube, cube, cube, flat, flat, flat,
            cube, cube, cube, flat, flat, flat, gain, gain, gain,
        ),
        check_vma=False,
    )
```

```python
import jax
import jax.numpy as jnp
from jax import lax
from jax.experimental import pallas as pl
from jax.experimental.pallas import tpu as pltpu
from jax.sharding import PartitionSpec as P

D = 1024
H = 16
DH = 64
FF = 2624
SEQ = 1024
STEP = 10

epsilon_norm = 1e-05
rope_theta = 160000.0
beta_first = 0.9
beta_second = 0.98
epsilon_adam = 1e-06
weight_decay = 1e-05

AXES = ("dp", "tensor")
bf16 = jnp.bfloat16
f32 = jnp.float32


def dot_nt(left, right):
    return lax.dot_general(left, right, (((1,), (1,)), ((), ())), preferred_element_type=f32)


def dot_tn(left, right):
    return lax.dot_general(left, right, (((0,), (0,)), ((), ())), preferred_element_type=f32)


def dot_nn(left, right):
    return jnp.dot(left, right, preferred_element_type=f32)


def adamw_update(weight, first_moment, second_moment, gradient, step_rate):
    first_new = beta_first * first_moment + (1.0 - beta_first) * gradient
    second_new = beta_second * second_moment + (1.0 - beta_second) * gradient * gradient
    first_hat = first_new / (1.0 - beta_first**STEP)
    second_hat = second_new / (1.0 - beta_second**STEP)
    weight_new = weight - step_rate * (
        first_hat / (jnp.sqrt(second_hat) + epsilon_adam) + weight_decay * weight
    )
    return (weight_new, first_new, second_new)


def whole(array):
    return pl.BlockSpec(array.shape, lambda i, rank=array.ndim: (0,) * rank)


def by_block(array):
    return pl.BlockSpec((1,) + array.shape[1:], lambda z: (z, 0, 0))


def by_rows(array, steps):
    return pl.BlockSpec((array.shape[0] // steps, array.shape[1]), lambda i: (i, 0))


def like(shape, dtype=bf16):
    return jax.ShapeDtypeStruct(shape, dtype)


microseconds = {
    "feature_order": 3.0,
    "first_norm": 4.0,
    "qkv_projection": 6.0,
    "attention_forward": 9.0,
    "attention_output": 2.5,
    "second_norm": 4.0,
    "expand": 12.0,
    "contract": 5.0,
    "layer_output": 2.0,
    "weight_gradient": 5.0,
    "grad_lifted": 6.0,
    "grad_normed_two": 8.0,
    "second_norm_gradient": 5.0,
    "grad_attended": 2.5,
    "attention_backward": 14.0,
    "grad_normed_one": 6.0,
    "first_norm_gradient": 3.0,
}


def cost(name):
    return pl.CostEstimate(
        flops=int(microseconds[name] * 0.35e9),
        bytes_accessed=int(microseconds[name] * 1.2e6),
        transcendentals=0,
    )


def call(kernel, name, grid, in_specs, out_specs, out_shape, scratch=()):
    return pl.pallas_call(
        kernel,
        grid=grid,
        in_specs=in_specs,
        out_specs=out_specs,
        out_shape=out_shape,
        scratch_shapes=list(scratch),
        compiler_params=pltpu.CompilerParams(vmem_limit_bytes=28 << 20),
        cost_estimate=cost(name),
        name=name,
    )


def swap_halves(values):
    lane = lax.broadcasted_iota(jnp.int32, values.shape, 1)
    return jnp.where(
        lane % DH < DH // 2,
        pltpu.roll(values, values.shape[1] - DH // 2, 1),
        pltpu.roll(values, DH // 2, 1),
    )


def normalize(values):
    centered = values - jnp.mean(values, axis=1, keepdims=True)
    scale = lax.rsqrt(jnp.mean(centered * centered, axis=1, keepdims=True) + epsilon_norm)
    return centered * scale, scale


def unnormalize(grads, values, gain):
    hats, scale = normalize(values)
    gain_grad = jnp.sum(grads * hats, axis=0, keepdims=True)
    errors = grads * gain
    average = jnp.mean(errors, axis=1, keepdims=True)
    along = jnp.mean(errors * hats, axis=1, keepdims=True)
    return scale * (errors - average - hats * along), gain_grad


def pick(ref, index_ref):
    count = index_ref.shape[0]
    if count == 1:
        return ref[...]
    block = ref.shape[1] // count
    parts = [ref[:, pl.ds(pl.multiple_of(index_ref[j] * block, block), block)] for j in range(count)]
    return jnp.concatenate(parts, axis=1)


scalars = pl.BlockSpec(memory_space=pltpu.SMEM)


def order_call(values, index):
    def kernel(index_ref, in_ref, out_ref):
        out_ref[...] = pick(in_ref, index_ref)

    tile = by_rows(values, 2)
    return call(
        kernel, "feature_order", (2,), [scalars, tile], tile, like(values.shape, values.dtype)
    )(index, values)


def norm_call(x, gains, index):
    def kernel(index_ref, x_ref, gain_ref, x_out_ref, out_ref):
        values = pick(x_ref, index_ref)
        x_out_ref[...] = values
        hats, _ = normalize(values.astype(f32))
        out_ref[...] = (hats * gain_ref[0:1, :]).astype(bf16)

    tile = by_rows(x, 4)
    return call(
        kernel, "first_norm", (4,), [scalars, tile, whole(gains)], [tile] * 2, [like(x.shape)] * 2
    )(index, x, gains)


def qkv_call(x, w_query, query_start, w_key_value, cosine, sine):
    rows, blocks = x.shape[0], w_query.shape[0]

    def kernel(x_ref, wq_ref, wkv_ref, cos_ref, sin_ref, q_ref, k_ref, v_ref):
        w = jnp.concatenate([wq_ref[0, query_start:], wkv_ref[0, :256]], axis=0)
        mixed = dot_nt(x_ref[...], w)
        cosine, sine = cos_ref[...], sin_ref[...]
        query, key = mixed[:, :128], mixed[:, 128:256]
        query = query * cosine + swap_halves(query) * sine
        key = key * cosine + swap_halves(key) * sine
        q_ref[0] = query.astype(bf16) * bf16(DH**-0.5)
        k_ref[0] = key.astype(bf16)
        v_ref[0] = mixed[:, 256:].astype(bf16)

    out = like((blocks, rows, 128))
    return call(
        kernel,
        "qkv_projection",
        (blocks,),
        [whole(x), by_block(w_query), by_block(w_key_value), whole(cosine), whole(sine)],
        [by_block(out)] * 3,
        [out] * 3,
    )(x, w_query, w_key_value, cosine, sine)


def pair_specs(array, first, halves):
    rows = array.shape[1]
    return (
        pl.BlockSpec((1, rows // halves, array.shape[2]), lambda z, i: (first + z, i, 0)),
        pl.BlockSpec((1, rows, array.shape[2]), lambda z, i: (first + z, 0, 0)),
    )


def attend_call(query, key, value, first, count):
    rows = query.shape[1]

    def kernel(q_ref, k_ref, v_ref, out_ref, lse_ref):
        query, key = q_ref[0], k_ref[0]
        value_t = v_ref[0].astype(f32).T.astype(bf16)
        lane = lax.broadcasted_iota(jnp.int32, query.shape, 1)
        outs = []
        for head in range(2):
            query_head = jnp.where(lane // DH == head, query, jnp.zeros_like(query))
            scores = dot_nt(key, query_head)
            peak = jnp.max(scores, axis=0, keepdims=True)
            weights = jnp.exp(scores - peak)
            total = jnp.sum(weights, axis=0, keepdims=True)
            out = dot_nn(value_t[head * DH : (head + 1) * DH], weights.astype(bf16))
            outs.append(out / total)
            lse_ref[0, head : head + 1, :] = peak + jnp.log(total)
        out_ref[0] = jnp.concatenate(outs, axis=0).T.astype(bf16)

    half, full = pair_specs(query, first, 2)
    out_half, _ = pair_specs(query, 0, 2)
    lse = pl.BlockSpec((1, 2, rows // 2), lambda z, i: (z, 0, i))
    return call(
        kernel,
        "attention_forward",
        (count, 2),
        [half, full, full],
        [out_half, lse],
        [like((count, rows, 128)), like((count, 2, rows), f32)],
    )(query, key, value)


def attend_back_call(query, key, value, grad, out, lse, cosine, sine, first, count):
    rows = query.shape[1]

    def kernel(
        q_ref, k_ref, v_ref, grad_ref, out_ref, lse_ref, cos_ref, sin_ref, dq_ref, dkv_ref,
        key_total, value_total,
    ):
        step = pl.program_id(1)
        query, key, value, grad = q_ref[0], k_ref[0], v_ref[0], grad_ref[0]
        key_t = key.astype(f32).T.astype(bf16)
        product_t = (grad.astype(f32) * out_ref[0].astype(f32)).T
        lane = lax.broadcasted_iota(jnp.int32, query.shape, 1)
        grad_key = jnp.zeros((rows, 128), f32)
        grad_value = jnp.zeros((rows, 128), f32)
        grad_queries = []
        for head in range(2):
            mine = lane // DH == head
            query_head = jnp.where(mine, query, jnp.zeros_like(query))
            grad_head = jnp.where(mine, grad, jnp.zeros_like(grad))
            delta = jnp.sum(product_t[head * DH : (head + 1) * DH], axis=0, keepdims=True)
            weights = jnp.exp(dot_nt(key, query_head) - lse_ref[0, head : head + 1, :])
            grad_soft = dot_nt(value, grad_head)
            grad_scores = (weights * (grad_soft - delta)).astype(bf16)
            grad_value += dot_nn(weights.astype(bf16), grad_head)
            grad_key += dot_nn(grad_scores, query_head)
            grad_queries.append(dot_nn(key_t[head * DH : (head + 1) * DH], grad_scores))
        half = query.shape[0]
        grad_query = jnp.concatenate(grad_queries, axis=0).T * (DH**-0.5)
        start = pl.multiple_of(step * half, half)
        cosine, sine = cos_ref[pl.ds(start, half), :], sin_ref[pl.ds(start, half), :]
        dq_ref[0] = (grad_query * cosine - swap_halves(grad_query) * sine).astype(bf16)

        @pl.when(step == 0)
        def _():
            key_total[...] = grad_key
            value_total[...] = grad_value

        @pl.when(step == 1)
        def _():
            total = key_total[...] + grad_key
            back = total * cos_ref[...] - swap_halves(total) * sin_ref[...]
            dkv_ref[0, :, :128] = back.astype(bf16)
            dkv_ref[0, :, 128:] = (value_total[...] + grad_value).astype(bf16)

    half, full = pair_specs(query, first, 2)
    out_half, _ = pair_specs(query, 0, 2)
    lse_spec = pl.BlockSpec((1, 2, rows // 2), lambda z, i: (z, 0, i))
    table = pl.BlockSpec(cosine.shape, lambda z, i: (0, 0))
    return call(
        kernel,
        "attention_backward",
        (count, 2),
        [half, full, full, half, out_half, lse_spec, table, table],
        [out_half, pl.BlockSpec((1, rows, 256), lambda z, i: (z, 0, 0))],
        [like((count, rows, 128)), like((count, rows, 256))],
        [pltpu.VMEM((rows, 128), f32)] * 2,
    )(query, key, value, grad, out, lse, cosine, sine)


def lanes_of(refs):
    return jnp.concatenate([r[j] for r in refs for j in range(r.shape[0])], axis=1)


def blocks_by_rows(array, steps):
    return pl.BlockSpec(
        (array.shape[0], array.shape[1] // steps, array.shape[2]), lambda i: (0, i, 0)
    )


def rows_of(ref, start, stop):
    if start == 0 and stop == ref.shape[1]:
        return ref[...].reshape(-1, ref.shape[2])
    return jnp.concatenate([ref[z, start:stop] for z in range(ref.shape[0])], axis=0)


def attention_output_call(att, w, start):
    rows = att[0].shape[1]

    def kernel(*refs):
        *att_refs, w_ref, out_ref = refs
        out_ref[...] = dot_nn(lanes_of(att_refs), rows_of(w_ref, start, w_ref.shape[1])).astype(bf16)

    out = like((rows, w.shape[2]))
    return call(
        kernel,
        "attention_output",
        (2,),
        [blocks_by_rows(a, 2) for a in att] + [whole(w)],
        by_rows(out, 2),
        out,
    )(*att, w)


def swapped_rows(array):
    return pl.BlockSpec((array.shape[0] // 4, array.shape[1]), lambda i: ((i + 2) % 4, 0))


def middle_call(x, part, got, gains):
    def kernel(x_ref, part_ref, got_ref, gain_ref, mid_ref, out_ref):
        middle = x_ref[...].astype(f32) + (part_ref[...].astype(f32) + got_ref[...].astype(f32))
        mid_ref[...] = middle
        hats, _ = normalize(middle)
        out_ref[...] = (hats * gain_ref[1:2, :]).astype(bf16)

    tile = by_rows(x, 4)
    return call(
        kernel,
        "second_norm",
        (4,),
        [tile, tile, swapped_rows(got), whole(gains)],
        [tile, tile],
        [like(x.shape, f32), like(x.shape)],
    )(x, part, got, gains)


def lift_call(x, up, gate):
    hidden = up.shape[0] * up.shape[1]

    def kernel(x_ref, up_ref, gate_ref, hid_ref, to_in_ref, to_gate_ref):
        x = x_ref[...]
        w_up, w_gate = (r[...].reshape(hidden, -1) for r in (up_ref, gate_ref))
        for start in range(0, hidden, 512):
            part = slice(start, min(start + 512, hidden))
            lifted = dot_nt(x, w_up[part])
            gate = dot_nt(x, w_gate[part])
            phi = 0.5 * (1.0 + lax.erf(lifted * (0.5**0.5)))
            gelu = lifted * phi
            slope = phi + lifted * jnp.exp(-0.5 * lifted * lifted) * 0.3989422804014327
            hid_ref[:, part] = (gelu * gate).astype(bf16)
            to_in_ref[:, part] = (gate * slope).astype(bf16)
            to_gate_ref[:, part] = gelu.astype(bf16)

    out = like((x.shape[0], hidden))
    return call(
        kernel,
        "expand",
        (2,),
        [by_rows(x, 2), whole(up), whole(gate)],
        [by_rows(out, 2)] * 3,
        [out] * 3,
    )(x, up, gate)


def lower_call(hidden, w, middle):
    rows, width = middle.shape

    def kernel(hid_ref, w_ref, mid_ref, own_ref, oth_ref):
        total = dot_nn(hid_ref[...], w_ref[...].reshape(-1, width))

        @pl.when(pl.program_id(0) == 1)
        def _():
            own_ref[...] = mid_ref[...] + total

        @pl.when(pl.program_id(0) == 0)
        def _():
            oth_ref[...] = total.astype(bf16)

    first = pl.BlockSpec((rows // 2, width), lambda i: (0, 0))
    return call(
        kernel,
        "contract",
        (2,),
        [pl.BlockSpec((rows // 2, hidden.shape[1]), lambda i: (1 - i, 0)), whole(w), first],
        [first, first],
        [like((rows // 2, width), f32), like((rows // 2, width))],
    )(hidden, w, middle)


def output_call(own, got, index):
    def kernel(index_ref, own_ref, got_ref, out_ref):
        out_ref[...] = (pick(own_ref, index_ref) + pick(got_ref, index_ref).astype(f32)).astype(bf16)

    tile = by_rows(own, 2)
    return call(kernel, "layer_output", (2,), [scalars, tile, tile], tile, like(own.shape))(
        index, own, got
    )


def weight_gradient_call(lefts, right, blocks, split, extra=None):
    flat = lefts[0].ndim == 2
    columns = lefts[0].shape[1] // blocks if flat else lefts[0].shape[2]
    more = [] if extra is None else [extra]
    lead = sum(e.shape[0] for e in more)
    height = lead + columns
    width = right.shape[1]
    half = blocks // 2

    def kernel(*refs):
        left_refs = refs[: len(lefts)]
        right_ref = refs[len(lefts)]
        extra_refs = refs[len(lefts) + 1 : len(lefts) + 1 + len(more)]
        outs = refs[len(lefts) + 1 + len(more) :]
        left = left_refs[0][...] if flat else lanes_of(left_refs)

        def put(ref, place, values, part):
            ref[place, lead:] = values
            for e in extra_refs:
                ref[place, :lead] = e[:, part]

        for start in range(0, width, 512):
            grads = dot_tn(left, right_ref[:, start : start + 512]).astype(bf16)
            for z in range(blocks):
                block = grads[z * columns : (z + 1) * columns]
                if not split:
                    put(outs[0], (z, slice(start, start + 512)), block, None)
                    continue
                mine, x_rest, y_rest, to_x, to_y = outs
                for j in range(start // 256, start // 256 + 2):
                    part = slice(256 * j, 256 * j + 256)
                    values = block[:, 256 * j - start : 256 * j - start + 256]
                    if j == 0:
                        put(mine, z, values, part)
                    elif j == 1:
                        put(*((to_x, half + z) if z < half else (x_rest, z - half)), values, part)
                    elif j == 2:
                        put(*((y_rest, z) if z < half else (to_y, z)), values, part)
                    else:
                        put(*((to_x, z) if z < half else (to_y, z - half)), values, part)

    if split:
        out_shape = [like((n, height, width // 4)) for n in (blocks, half, half, blocks, blocks)]
    else:
        out_shape = [like((blocks, height, width))]

        def kernel(*refs):
            left_refs = refs[: len(lefts)]
            right_ref, out_ref = refs[len(lefts)], refs[-1]
            left = left_refs[0][...] if flat else lanes_of(left_refs)
            grads = dot_tn(left, right_ref[...]).astype(bf16)
            for z in range(blocks):
                out_ref[z, lead:] = grads[z * columns : (z + 1) * columns]
                if more:
                    out_ref[z, :lead] = refs[len(lefts) + 1][...]

    return call(
        kernel,
        "weight_gradient",
        (1,),
        [whole(a) for a in (*lefts, right, *more)],
        [whole(o) for o in out_shape],
        out_shape,
    )(*lefts, right, *more)


def hidden_back_call(dy, w, to_in, to_gate):
    hidden = to_in.shape[1]

    def kernel(dy_ref, w_ref, to_in_ref, to_gate_ref, in_ref, gate_ref):
        w = w_ref[...].reshape(hidden, -1)
        for start in range(0, hidden, 512):
            part = slice(start, min(start + 512, hidden))
            grad = dot_nt(dy_ref[...], w[part])
            in_ref[:, part] = (grad * to_in_ref[:, part].astype(f32)).astype(bf16)
            gate_ref[:, part] = (grad * to_gate_ref[:, part].astype(f32)).astype(bf16)

    tile = by_rows(to_in, 2)
    return call(
        kernel,
        "grad_lifted",
        (2,),
        [by_rows(dy, 2), whole(w), tile, tile],
        [tile, tile],
        [like(to_in.shape)] * 2,
    )(dy, w, to_in, to_gate)


def two_part_call(grad_in, grad_gate, up, gate):
    width = up.shape[2]

    def kernel(in_ref, gate_ref, up_ref, w_gate_ref, out_ref):
        total = dot_nn(in_ref[...], up_ref[...].reshape(-1, width))
        total += dot_nn(gate_ref[...], w_gate_ref[...].reshape(-1, width))
        out_ref[...] = total.astype(bf16)

    out = like((grad_in.shape[0], width))
    return call(
        kernel,
        "grad_normed_two",
        (2,),
        [by_rows(grad_in, 2), by_rows(grad_gate, 2), whole(up), whole(gate)],
        by_rows(out, 2),
        out,
    )(grad_in, grad_gate, up, gate)


def two_back_call(part, got, middle, dy, gains):
    rows, width = middle.shape

    def kernel(part_ref, got_ref, mid_ref, dy_ref, gain_ref, grad_ref, low_ref, gain_grad_ref):
        i = pl.program_id(0)
        grads = part_ref[...].astype(f32) + got_ref[...].astype(f32)
        back, gain_grad = unnormalize(grads, mid_ref[...], gain_ref[1:2, :])
        grad = dy_ref[...].astype(f32) + back
        low_ref[...] = grad.astype(bf16)

        @pl.when(i == 0)
        def _():
            gain_grad_ref[...] = jnp.zeros_like(gain_grad_ref)

        @pl.when(i < 2)
        def _():
            grad_ref[...] = grad
            gain_grad_ref[...] += jnp.broadcast_to(gain_grad, gain_grad_ref.shape)

    tile = by_rows(middle, 4)
    row = like((8, width), f32)
    return call(
        kernel,
        "second_norm_gradient",
        (4,),
        [tile, swapped_rows(got), tile, tile, whole(gains)],
        [
            pl.BlockSpec((rows // 4, width), lambda i: (jnp.minimum(i, 1), 0)),
            tile,
            whole(row),
        ],
        [like((rows // 2, width), f32), like(middle.shape), row],
    )(part, got, middle, dy, gains)


def att_grad_call(grad, w, start):
    blocks = w.shape[0]
    columns = w.shape[1] - start

    def kernel(g_ref, w_ref, out_ref):
        out = dot_nt(g_ref[...], rows_of(w_ref, start, w_ref.shape[1])).astype(bf16)
        for z in range(blocks):
            out_ref[z] = out[:, z * columns : (z + 1) * columns]

    out = like((blocks, grad.shape[0], columns))
    return call(
        kernel,
        "grad_attended",
        (2,),
        [by_rows(grad, 2), whole(w)],
        blocks_by_rows(out, 2),
        out,
    )(grad, w)


def one_part_call(queries, keys_values, w_query, query_start, w_key_value):
    rows, width = queries[0].shape[1], w_query.shape[2]
    count = len(queries)

    def kernel(*refs):
        left_refs = refs[: 2 * count]
        wq_ref, wkv_ref, own_ref, oth_ref = refs[2 * count :]
        left = lanes_of(left_refs)
        w = jnp.concatenate(
            [rows_of(wq_ref, query_start, wq_ref.shape[1]), rows_of(wkv_ref, 0, 256)], axis=0
        )
        total = dot_nn(left, w)

        @pl.when(pl.program_id(0) == 1)
        def _():
            own_ref[...] = total

        @pl.when(pl.program_id(0) == 0)
        def _():
            oth_ref[...] = total.astype(bf16)

    def half(array):
        shape = (array.shape[0], rows // 2, array.shape[2])
        return pl.BlockSpec(shape, lambda i: (0, 1 - i, 0))

    first = pl.BlockSpec((rows // 2, width), lambda i: (0, 0))
    return call(
        kernel,
        "grad_normed_one",
        (2,),
        [half(a) for a in (*queries, *keys_values)] + [whole(w_query), whole(w_key_value)],
        [first, first],
        [like((rows // 2, width), f32), like((rows // 2, width))],
    )(*queries, *keys_values, w_query, w_key_value)


def one_back_call(own, got, x, grad_middle, gains, gain_two, index):
    rows, width = own.shape

    def kernel(
        index_ref, own_ref, got_ref, x_ref, mid_ref, gain_ref, gain_two_ref, grad_ref, gain_grad_ref,
        total_ref, low_ref,
    ):
        i = pl.program_id(0)
        grads = own_ref[...] + got_ref[...].astype(f32)
        back, gain_grad = unnormalize(grads, x_ref[...].astype(f32), gain_ref[0:1, :])
        low_ref[...] = (mid_ref[...] + back).astype(bf16)
        grad_ref[...] = pick(low_ref, index_ref)

        @pl.when(i == 0)
        def _():
            total_ref[...] = gain_grad

        @pl.when(i == 1)
        def _():
            total = total_ref[...] + gain_grad
            row = lax.broadcasted_iota(jnp.int32, gain_grad_ref.shape, 0)
            both = jnp.where(row == 0, total, jnp.where(row == 1, gain_two_ref[0:1, :], 0.0))
            gain_grad_ref[...] = both.astype(bf16)

    tile = by_rows(own, 2)
    x_tile = pl.BlockSpec((rows // 2, width), lambda i: (i, 0))
    gain_grads = like((16, width))
    return call(
        kernel,
        "first_norm_gradient",
        (2,),
        [scalars, tile, tile, x_tile, tile, whole(gains), whole(gain_two)],
        [tile, whole(gain_grads)],
        [like(own.shape), gain_grads],
        [pltpu.VMEM((1, width), f32), pltpu.VMEM((rows // 2, width), bf16)],
    )(index, own, got, x, grad_middle, gains, gain_two)


def make_per_device(dp, tensor):
    count = dp * tensor
    chips = dp // 2
    chip_bits = chips.bit_length() - 1
    square = chip_bits == 2
    half = tensor // 2

    def permute(value, pairs):
        return lax.ppermute(value, AXES, pairs)

    def exchange(value, mask):
        return permute(value, [(i, i ^ mask) for i in range(count)])

    def over_chip(value, bit):
        return exchange(value, (2 * tensor) << bit)

    def over_core(value):
        pieces = max(1, value.size // (1 << 18))
        if value.ndim != 2 or value.shape[0] % (16 * pieces):
            pieces = 1
        rows = value.shape[0] // pieces
        got = [exchange(value[i * rows : (i + 1) * rows], tensor) for i in range(pieces)]
        return got[0] if pieces == 1 else jnp.concatenate(got, axis=0)

    def spread_pairs(r):
        pairs = []
        for i in range(count):
            z = i % tensor
            core = (i // tensor) % 2
            chip = i // (2 * tensor)
            pairs.append((i, (chip * 2 + z % 2) * tensor + (r ^ (z // 2)) * 2 + core))
        return pairs

    def by_column(blocks, me_z):
        for bit in range(tensor.bit_length() - 1):
            odd = (me_z >> bit) % 2 == 1
            blocks = [jnp.where(odd, blocks[k ^ (1 << bit)], blocks[k]) for k in range(tensor)]
        return blocks

    def gather_column(rows, me_z):
        return by_column([rows] + [exchange(rows, k) for k in range(1, tensor)], me_z)

    def gather_plane(columns):
        current = columns[None]
        for bit in range(chip_bits):
            current = jnp.concatenate([current, over_chip(current, bit)], axis=0)
        return current.transpose(1, 2, 0, 3).reshape(columns.shape[:2] + (-1,))

    def low_sum(*values):
        return sum(v.astype(f32) for v in values).astype(bf16)

    def reduce_plane(parts):
        current = parts
        for bit in reversed(range(chip_bits)):
            middle = current.shape[0] // 2
            current = low_sum(current[:middle], over_chip(current[middle:], bit))
        return current[0]

    def reduce_column(blocks):
        result = blocks[0].astype(f32)
        for k in range(1, tensor):
            result = result + exchange(blocks[k], k).astype(f32)
        return result

    def per_device(
        inputs,
        cotangent,
        attention_in,
        attention_out,
        expand_weight,
        contract_weight,
        norm_gains,
        attention_in_first,
        attention_in_second,
        attention_out_first,
        attention_out_second,
        expand_first,
        expand_second,
        contract_first,
        contract_second,
        gains_first,
        gains_second,
    ):
        block = attention_in.shape[0]
        head_columns = attention_in.shape[2]
        hidden_local = expand_weight.shape[2]
        local_rows = inputs.shape[2]
        me_dp = lax.axis_index("dp")
        me_z = lax.axis_index("tensor")
        core = me_dp % 2
        z_high = me_z // 2

        me_chip = me_dp // 2
        index = me_chip ^ jnp.arange(chips, dtype=jnp.int32)
        aligned = block % 128 == 0
        kernel_index = index if aligned else jnp.zeros((1,), jnp.int32)

        def outside(values):
            if aligned:
                return values
            shaped = values.reshape(values.shape[0], chips, 2 * block)
            return jnp.take(shaped, index, axis=1).reshape(values.shape)

        def spread(values, r):
            part = lax.dynamic_index_in_dim(values[:, 0], r ^ z_high, 0, keepdims=False)
            return permute(part, spread_pairs(r))

        def collect(values, r):
            part = values[r * local_rows : (r + 1) * local_rows]
            return permute(part, [(b, a) for a, b in spread_pairs(r)])

        def assemble(first, second):
            odd = z_high == 1
            return jnp.stack([jnp.where(odd, second, first), jnp.where(odd, first, second)])[:, None]

        row_starts = [
            ((r ^ z_high) * 2 + (core ^ c)) * local_rows for c in range(2) for r in range(2)
        ]
        positions = jnp.concatenate([s + jnp.arange(local_rows) for s in row_starts]).astype(f32)
        exponents = jnp.arange(0, DH, 2).astype(f32) / DH
        angles = positions[:, None] * jnp.power(rope_theta, -exponents)[None, :]
        cosine, sine = jnp.cos(angles), jnp.sin(angles)
        cosine = jnp.concatenate([cosine] * 4, axis=-1)
        sine = jnp.concatenate([-sine, sine] * 2, axis=-1)

        cut = (hidden_local // 2 + 15) // 16 * 16
        spare = 2 * cut - hidden_local
        head_cut = head_columns // 2
        low_in = attention_in.astype(bf16).reshape(block, 3, 2, head_cut).transpose(2, 1, 3, 0)
        low_out = attention_out.astype(bf16).reshape(block, 2, head_cut).transpose(1, 2, 0)
        low_expand = jnp.pad(expand_weight.astype(bf16).transpose(1, 2, 0), ((0, 0), (0, spare), (0, 0)))
        low_expand = low_expand.reshape(2, 2, cut, block).transpose(1, 0, 2, 3)
        low_contract = jnp.pad(contract_weight.astype(bf16).T, ((0, spare), (0, 0)))
        low_contract = low_contract.reshape(2, cut, block)
        low_gains = jnp.pad(norm_gains.astype(bf16), ((0, 14), (0, 0)))
        lead = low_gains.shape[0]
        both = jnp.concatenate(
            [
                jnp.stack([low_gains, low_gains]),
                low_in.reshape(2, -1, block),
                low_out,
                low_expand.reshape(2, -1, block),
                low_contract,
            ],
            axis=1,
        )
        sizes = [lead + head_cut, 3 * head_cut, cut, cut, cut]
        starts = [sum(sizes[:k]) for k in range(len(sizes) + 1)]
        last = len(sizes)
        first_core = core == 0

        def side_by_side(mine, got):
            return jnp.concatenate(
                [jnp.where(first_core, mine, got), jnp.where(first_core, got, mine)], axis=-1
            )

        state = {"tables": (cosine, sine), "x_in": inputs, "cot": cotangent, "both": both}
        held = []
        again = []

        def run(work):
            nonlocal state
            new = {}
            late = held[:]
            held[:] = again
            again.clear()
            work(state, new)
            for values in late:
                new.update(values)
            state.update(new)
            names = list(state)
            state = dict(zip(names, lax.optimization_barrier([state[n] for n in names])))

        def columns(s, new, first, count):
            low = s["low"][starts[first] : starts[first + count]]
            blocks = gather_column(low, me_z)
            for k in range(first, first + count):
                a, b = starts[k] - starts[first], starts[k + 1] - starts[first]
                new["column", k] = jnp.stack([block[a:b] for block in blocks])

        def plane(s, new, k):
            if not square:
                if k < last:
                    new["w", k] = gather_plane(s.pop(("column", k)))
                return
            sends, first_rows = ([], []), 0
            if k < last:
                column = s["column", k]
                first_rows = column.shape[0] * column.shape[1]
                for way in range(2):
                    sends[way].append(column.reshape(first_rows, -1))
            if k > 0:
                got = s["near", k - 1]
                rows = half * sizes[k - 1]
                sends[0].append(got[1][rows : 2 * rows])
                sends[1].append(got[0][:rows])
            got = tuple(over_chip(jnp.concatenate(sends[way], axis=0), way) for way in range(2))
            if k < last:
                new["near", k] = got
            if k > 0:
                shape = (tensor, sizes[k - 1], -1)
                rows = tensor * sizes[k - 1]
                x_got, y_got = s.pop(("near", k - 1))
                diagonal = jnp.concatenate([got[1][first_rows:], got[0][first_rows:]], axis=0)
                new["w", k - 1] = jnp.concatenate(
                    [
                        s.pop(("column", k - 1)),
                        x_got[:rows].reshape(shape),
                        y_got[:rows].reshape(shape),
                        diagonal.reshape(shape),
                    ],
                    axis=-1,
                )

        def f0(s, new):
            pair = s.pop("both")
            mine = jnp.where(first_core, pair[0], pair[1])
            got = over_core(jnp.where(first_core, pair[1], pair[0]))
            new["low"] = side_by_side(mine, got)

        run(f0)

        def f1(s, new):
            columns(s, new, 0, 1)
            late = lax.all_gather(s["low"][starts[3] :], "tensor", axis=0)
            again.append({("column", 3): late[:, : sizes[3]], ("column", 4): late[:, sizes[3] :]})

        run(f1)

        def f2(s, new):
            plane(s, new, 0)
            columns(s, new, 1, 1)

        run(f2)

        def f3(s, new):
            plane(s, new, 1)
            columns(s, new, 2, 1)
            new["x0"] = spread(s["x_in"], 0)

        run(f3)

        def f4(s, new):
            plane(s, new, 2)
            rows = jnp.concatenate([s.pop("x0"), spread(s.pop("x_in"), 1)], axis=0)
            new["x_own"] = rows

        run(f4)

        def f5(s, new):
            plane(s, new, 3)
            rows = s.pop("x_own")
            x_raw = jnp.concatenate([rows, over_core(rows)], axis=0)
            new["gains"] = s["w", 0][0, :lead].astype(f32)
            new["x"], new["normed"] = norm_call(outside(x_raw), new["gains"], kernel_index)
            query, key, value = qkv_call(new["normed"], s["w", 0], lead, s["w", 1], *s["tables"])
            new["qkv"] = (query, key, value)
            new["att", 0], new["lse", 0] = attend_call(query, key, value, 0, tensor // 2)
            new["y0"] = spread(s["cot"], 0)

        run(f5)

        def f6(s, new):
            plane(s, new, 4)
            new["att", 1], new["lse", 1] = attend_call(*s["qkv"], tensor // 2, tensor // 2)
            new["part"] = attention_output_call((s["att", 0], new["att", 1]), s["w", 1], 2 * head_cut)
            new["y_own"] = jnp.concatenate([s.pop("y0"), spread(s.pop("cot"), 1)], axis=0)

        run(f6)

        def f7(s, new):
            plane(s, new, 5)
            part, rows = s.pop("part"), s.pop("y_own")
            new["middle"], new["normed_two"] = middle_call(
                s["x"], part, over_core(part), s["gains"]
            )
            new["hidden"], new["to_in"], new["to_gate"] = lift_call(
                new["normed_two"], s["w", 2], s["w", 3]
            )
            y_raw = jnp.concatenate([rows, over_core(rows)], axis=0)
            new["dy"] = order_call(outside(y_raw), kernel_index)
            made(new, 0, [new["hidden"]], new["dy"])

        def made(new, k, lefts, right, extra=None):
            grads = weight_gradient_call(lefts, right, tensor, square and aligned, extra)
            if not square or not aligned:
                (full,) = grads
                grads = full.reshape(full.shape[:2] + (chips, -1)).transpose(2, 0, 1, 3)
            new["g", k] = grads

        def near(s, new, k):
            if not square:
                new["f", k] = [b for b in reduce_plane(s.pop(("g", k)))]
                return
            mine, x_rest, y_rest, to_x, to_y = s.pop(("g", k))
            x_got, y_got = over_chip(to_x, 0), over_chip(to_y, 1)
            new["n", k] = (
                low_sum(x_rest, y_got[:half]),
                low_sum(y_rest, x_got[:half]),
                mine,
                x_got,
                y_got,
            )

        def far(s, new, k):
            if not square:
                return
            x_second, y_second, mine, x_near, y_near = s.pop(("n", k))
            x_got, y_got = over_chip(x_second, 0), over_chip(y_second, 1)
            new["f", k] = [
                low_sum(mine[j], x_near[half + j], y_got[j]) for j in range(half)
            ] + [low_sum(mine[half + j], y_near[half + j], x_got[j]) for j in range(half)]

        def scatter(s, k):
            total = lax.psum_scatter(
                jnp.stack(s.pop(("f", k))), "tensor", scatter_dimension=0, tiled=False
            )
            held.append({("sum", k): total})

        def column(s, new, *chunks):
            blocks = [by_column(s.pop(("f", k)), me_z) for k in chunks]
            total = reduce_column([jnp.concatenate(b, axis=0) for b in zip(*blocks)])
            start = 0
            for k, b in zip(chunks, blocks):
                new["sum", k] = total[start : start + b[0].shape[0]].astype(bf16)
                start += b[0].shape[0]

        def trade(s, new, *chunks):
            sums = [s.pop(("sum", k)) for k in chunks]
            total = jnp.concatenate(sums, axis=0)
            mine = jnp.where(first_core, total[:, :block], total[:, block:])
            got = over_core(jnp.where(first_core, total[:, block:], total[:, :block]))
            start = 0
            for k, rows in zip(chunks, [a.shape[0] for a in sums]):
                a, b = mine[start : start + rows], got[start : start + rows]
                new["grad", k] = (
                    jnp.where(first_core, a, b).astype(f32),
                    jnp.where(first_core, b, a).astype(f32),
                )
                start += rows

        run(f7)

        def s1(s, new):
            near(s, new, 0)
            g_in, g_gate = hidden_back_call(s["dy"], s["w", 4], s.pop("to_in"), s.pop("to_gate"))
            new["g_gate"] = g_gate
            new["part"] = two_part_call(g_in, g_gate, s.pop(("w", 2)), s.pop(("w", 3)))
            made(new, 1, [g_in], s["normed_two"])
            new["low_own"], new["low_other"] = lower_call(
                s.pop("hidden"), s.pop(("w", 4)), s["middle"]
            )

        run(s1)

        def attention_back(s, new, p):
            new["dq", p], new["dkv", p] = attend_back_call(
                *s["qkv"], s["g_att"], s["att", p], s.pop(("lse", p)), *s["tables"],
                p * (tensor // 2), tensor // 2,
            )

        def s2(s, new):
            far(s, new, 0)
            near(s, new, 1)
            part = s.pop("part")
            new["grad_mid"], new["mid_low"], new["gain_two"] = two_back_call(
                part, over_core(part), s.pop("middle"), s.pop("dy"), s["gains"]
            )
            made(new, 2, [s.pop("g_gate")], s.pop("normed_two"))
            s["g_att"] = new["g_att"] = att_grad_call(new["mid_low"], s["w", 1], 2 * head_cut)
            attention_back(s, new, 0)
            new["out"] = outside(
                output_call(s.pop("low_own"), over_core(s.pop("low_other")), kernel_index)
            )

        run(s2)

        def s3(s, new):
            scatter(s, 0)
            far(s, new, 1)
            near(s, new, 2)
            attention_back(s, new, 1)
            made(new, 3, [s["att", 0], s["att", 1]], s["mid_low"])
            new["out0"] = collect(s["out"], 0)
            held.append({"out1": collect(s["out"], 1)})

        run(s3)

        def s4(s, new):
            scatter(s, 1)
            far(s, new, 2)
            near(s, new, 3)
            made(new, 4, [s["dkv", 0], s["dkv", 1]], s["normed"])
            new["own"], new["other"] = one_part_call(
                (s["dq", 0], s["dq", 1]), (s["dkv", 0], s["dkv", 1]), s["w", 0], lead, s["w", 1]
            )

        run(s4)

        def s5(s, new):
            scatter(s, 2)
            far(s, new, 3)
            near(s, new, 4)
            dx, gain_grads = one_back_call(
                s.pop("own"), over_core(s.pop("other")), s.pop("x"), s.pop("grad_mid"), s["gains"],
                s.pop("gain_two"), kernel_index,
            )
            new["dx"] = outside(dx)
            made(new, 5, [s["dq", 0], s["dq", 1]], s["normed"], gain_grads)

        run(s5)

        def s6(s, new):
            far(s, new, 4)
            near(s, new, 5)
            column(s, new, 3)
            held.append({"dx0": collect(s["dx"], 0), "dx1": collect(s["dx"], 1)})

        run(s6)

        def s7(s, new):
            far(s, new, 5)
            column(s, new, 4)
            trade(s, new, 0, 1, 2, 3)

        run(s7)

        def s8(s, new):
            column(s, new, 5)

        run(s8)

        def s9(s, new):
            trade(s, new, 4, 5)

        run(s9)

        layer_output = assemble(state["out0"], state["out1"])
        input_gradient = assemble(state["dx0"], state["dx1"])
        def joined(k, rows):
            return jnp.concatenate(state["grad", k], axis=0)[:rows]

        grad_down, grad_up, grad_gate = (joined(k, hidden_local) for k in range(3))
        grad_out = joined(3, head_columns)
        key_value = [g.reshape(2, head_cut, block) for g in state["grad", 4]]
        query = [g[lead:] for g in state["grad", 5]]
        grad_qkv = jnp.stack(
            [jnp.concatenate(query, axis=0)]
            + [jnp.concatenate([g[i] for g in key_value], axis=0) for i in range(2)]
        ).transpose(2, 0, 1)
        gain_total = sum(g[:2] for g in state["grad", 5])
        grad_expand = jnp.stack([grad_up, grad_gate]).transpose(2, 0, 1)
        step_rates = (
            2.5 * D ** (-0.5),
            2.5 * max(1, 4 * H * DH // SEQ) ** (-0.5),
            2.5 * D ** (-0.5),
            2.5 * FF ** (-0.5),
            0.25,
        )
        grad_qkv, grad_out, grad_expand, grad_down = lax.optimization_barrier(
            (grad_qkv, grad_out.T, grad_expand, grad_down.T)
        )
        qkv_new = adamw_update(
            attention_in, attention_in_first, attention_in_second, grad_qkv, step_rates[0]
        )
        out_new = adamw_update(
            attention_out, attention_out_first, attention_out_second, grad_out, step_rates[1]
        )
        expand_new = adamw_update(
            expand_weight, expand_first, expand_second, grad_expand, step_rates[2]
        )
        contract_new = adamw_update(
            contract_weight, contract_first, contract_second, grad_down, step_rates[3]
        )
        gains_new = adamw_update(norm_gains, gains_first, gains_second, gain_total, step_rates[4])
        return (
            layer_output,
            input_gradient,
            *qkv_new,
            *out_new,
            *expand_new,
            *contract_new,
            *gains_new,
        )

    return per_device


def solution(mesh):
    activation = P(None, "dp", "tensor", None)
    cube = P("dp", None, "tensor")
    flat = P("dp", "tensor")
    gain = P(None, "dp")
    return jax.shard_map(
        make_per_device(mesh.shape["dp"], mesh.shape["tensor"]),
        mesh=mesh,
        in_specs=(
            activation, activation, cube, flat, cube, flat, gain,
            cube, cube, flat, flat, cube, cube, flat, flat, gain, gain,
        ),
        out_specs=(
            activation, activation, cube, cube, cube, flat, flat, flat,
            cube, cube, cube, flat, flat, flat, gain, gain, gain,
        ),
        check_vma=False,
    )
```

```python
import jax
import jax.numpy as jnp
from jax import lax
from jax.experimental import pallas as pl
from jax.experimental.pallas import tpu as pltpu
from jax.sharding import PartitionSpec as P

D = 1024
H = 16
DH = 64
FF = 2624
SEQ = 1024
STEP = 10

epsilon_norm = 1e-05
rope_theta = 160000.0
beta_first = 0.9
beta_second = 0.98
epsilon_adam = 1e-06
weight_decay = 1e-05

AXES = ("dp", "tensor")
bf16 = jnp.bfloat16
f32 = jnp.float32


def dot_nt(left, right):
    return lax.dot_general(left, right, (((1,), (1,)), ((), ())), preferred_element_type=f32)


def dot_tn(left, right):
    return lax.dot_general(left, right, (((0,), (0,)), ((), ())), preferred_element_type=f32)


def dot_nn(left, right):
    return jnp.dot(left, right, preferred_element_type=f32)


def adamw_update(weight, first_moment, second_moment, gradient, step_rate):
    first_new = beta_first * first_moment + (1.0 - beta_first) * gradient
    second_new = beta_second * second_moment + (1.0 - beta_second) * gradient * gradient
    first_hat = first_new / (1.0 - beta_first**STEP)
    second_hat = second_new / (1.0 - beta_second**STEP)
    weight_new = weight - step_rate * (
        first_hat / (jnp.sqrt(second_hat) + epsilon_adam) + weight_decay * weight
    )
    return (weight_new, first_new, second_new)


def whole(array):
    return pl.BlockSpec(
        array.shape, lambda i, rank=array.ndim: (0,) * rank, pipeline_mode=pl.Buffered(1)
    )


def by_block(array):
    return pl.BlockSpec((1,) + array.shape[1:], lambda z: (z, 0, 0))


def by_rows(array, steps):
    return pl.BlockSpec((array.shape[0] // steps, array.shape[1]), lambda i: (i, 0))


def like(shape, dtype=bf16):
    return jax.ShapeDtypeStruct(shape, dtype)


def kept(array):
    return pltpu.HBM(array.shape, array.dtype)


microseconds = dict(
    feature_order=3.0,
    gathered_weight=3.0,
    gradient_sums=3.0,
    first_norm=4.0,
    qkv_projection=6.0,
    attention_forward=9.0,
    attention_output=2.5,
    second_norm=4.0,
    expand=12.0,
    contract=5.0,
    layer_output=2.0,
    weight_gradient=5.0,
    grad_lifted=6.0,
    grad_normed_two=8.0,
    second_norm_gradient=5.0,
    grad_attended=2.5,
    attention_backward=14.0,
    grad_normed_one=6.0,
    first_norm_gradient=3.0,
)


def cost(name):
    return pl.CostEstimate(
        flops=int(microseconds[name] * 0.35e9),
        bytes_accessed=int(microseconds[name] * 1.2e6),
        transcendentals=0,
    )


def call(kernel, name, grid, in_specs, out_specs, out_shape, scratch=()):
    return pl.pallas_call(
        kernel,
        grid=grid,
        in_specs=in_specs,
        out_specs=out_specs,
        out_shape=out_shape,
        scratch_shapes=list(scratch),
        compiler_params=pltpu.CompilerParams(vmem_limit_bytes=28 << 20),
        cost_estimate=cost(name),
        name=name,
    )


def swap_halves(values):
    lane = lax.broadcasted_iota(jnp.int32, values.shape, 1)
    return jnp.where(
        lane % DH < DH // 2,
        pltpu.roll(values, values.shape[1] - DH // 2, 1),
        pltpu.roll(values, DH // 2, 1),
    )


def normalize(values):
    centered = values - jnp.mean(values, axis=1, keepdims=True)
    scale = lax.rsqrt(jnp.mean(centered * centered, axis=1, keepdims=True) + epsilon_norm)
    return centered * scale, scale


def unnormalize(grads, values, gain):
    hats, scale = normalize(values)
    gain_grad = jnp.sum(grads * hats, axis=0, keepdims=True)
    errors = grads * gain
    average = jnp.mean(errors, axis=1, keepdims=True)
    along = jnp.mean(errors * hats, axis=1, keepdims=True)
    return scale * (errors - average - hats * along), gain_grad


def pick(ref, index_ref):
    count = index_ref.shape[0]
    if count == 1:
        return ref[...]
    block = ref.shape[1] // count
    parts = [ref[:, pl.ds(pl.multiple_of(index_ref[j] * block, block), block)] for j in range(count)]
    return jnp.concatenate(parts, axis=1)


def in_hbm(*arrays):
    return tuple(pltpu.with_memory_space_constraint(a, pltpu.HBM) for a in arrays)


scalars = pl.BlockSpec(memory_space=pltpu.SMEM)


def order_call(values, index):
    def kernel(index_ref, in_ref, out_ref):
        out_ref[...] = pick(in_ref, index_ref)

    tile = by_rows(values, 2)
    return call(
        kernel, "feature_order", (2,), [scalars, tile], tile, like(values.shape, values.dtype)
    )(index, values)


def norm_call(x, gains, index):
    def kernel(index_ref, x_ref, gain_ref, x_out_ref, out_ref):
        values = pick(x_ref, index_ref)
        x_out_ref[...] = values
        hats, _ = normalize(values.astype(f32))
        out_ref[...] = (hats * gain_ref[0:1, :]).astype(bf16)

    tile = by_rows(x, 4)
    return call(
        kernel, "first_norm", (4,), [scalars, tile, whole(gains)], [tile] * 2, [like(x.shape)] * 2
    )(index, x, gains)


def qkv_call(x, w_query, query_start, w_key_value, cosine, sine):
    rows, blocks = x.shape[0], w_query.shape[0]

    def kernel(x_ref, wq_ref, wkv_ref, cos_ref, sin_ref, q_ref, k_ref, v_ref):
        w = jnp.concatenate([wq_ref[0, query_start:], wkv_ref[0, :256]], axis=0)
        mixed = dot_nt(x_ref[...], w)
        cosine, sine = cos_ref[...], sin_ref[...]
        query, key = mixed[:, :128], mixed[:, 128:256]
        query = query * cosine + swap_halves(query) * sine
        key = key * cosine + swap_halves(key) * sine
        q_ref[0] = query.astype(bf16) * bf16(DH**-0.5)
        k_ref[0] = key.astype(bf16)
        v_ref[0] = mixed[:, 256:].astype(bf16)

    out = like((blocks, rows, 128))
    return call(
        kernel,
        "qkv_projection",
        (blocks,),
        [whole(x), by_block(w_query), by_block(w_key_value), whole(cosine), whole(sine)],
        [by_block(out)] * 3,
        [out] * 3,
    )(x, w_query, w_key_value, cosine, sine)


def pair_specs(array, first, halves):
    rows = array.shape[1]
    return (
        pl.BlockSpec((1, rows // halves, array.shape[2]), lambda z, i: (first + z, i, 0)),
        pl.BlockSpec((1, rows, array.shape[2]), lambda z, i: (first + z, 0, 0)),
    )


def weave_call(column, x_near, y_near, x_far, y_far, far_rows):
    blocks, rows, width = column.shape
    half = blocks // 2

    def kernel(col_ref, x_ref, y_ref, x_far_ref, y_far_ref, out_ref):
        z = pl.program_id(0)
        out_ref[0, :, :width] = col_ref[0]
        out_ref[0, :, width : 2 * width] = x_ref[...]
        out_ref[0, :, 2 * width : 3 * width] = y_ref[...]
        start = pl.multiple_of(far_rows + z % half * rows, 16)

        @pl.when(z < half)
        def _():
            out_ref[0, :, 3 * width :] = y_far_ref[pl.ds(start, rows), :]

        @pl.when(z >= half)
        def _():
            out_ref[0, :, 3 * width :] = x_far_ref[pl.ds(start, rows), :]

    near = pl.BlockSpec((rows, width), lambda z: (z, 0))
    out = like((blocks, rows, 4 * width))
    return call(
        kernel,
        "gathered_weight",
        (blocks,),
        [by_block(column), near, near, whole(x_far), whole(y_far)],
        by_block(out),
        out,
    )(column, x_near, y_near, x_far, y_far)


def attend_call(query, key, value, first, count):
    rows = query.shape[1]

    def kernel(q_ref, k_ref, v_ref, out_ref, lse_ref):
        query, key = q_ref[0], k_ref[0]
        value_t = v_ref[0].astype(f32).T.astype(bf16)
        lane = lax.broadcasted_iota(jnp.int32, query.shape, 1)
        outs = []
        for head in range(2):
            query_head = jnp.where(lane // DH == head, query, jnp.zeros_like(query))
            scores = dot_nt(key, query_head)
            peak = jnp.max(scores, axis=0, keepdims=True)
            weights = jnp.exp(scores - peak)
            total = jnp.sum(weights, axis=0, keepdims=True)
            out = dot_nn(value_t[head * DH : (head + 1) * DH], weights.astype(bf16))
            outs.append(out / total)
            lse_ref[0, head : head + 1, :] = peak + jnp.log(total)
        out_ref[0] = jnp.concatenate(outs, axis=0).T.astype(bf16)

    half, full = pair_specs(query, first, 2)
    out_half, _ = pair_specs(query, 0, 2)
    lse = pl.BlockSpec((1, 2, rows // 2), lambda z, i: (z, 0, i))
    return call(
        kernel,
        "attention_forward",
        (count, 2),
        [half, full, full],
        [out_half, lse],
        [like((count, rows, 128)), like((count, 2, rows), f32)],
    )(query, key, value)


def attend_back_call(query, key, value, grad, out, lse, cosine, sine, first, count):
    rows = query.shape[1]

    def kernel(
        q_ref, k_ref, v_ref, grad_ref, out_ref, lse_ref, cos_ref, sin_ref, dq_ref, dkv_ref,
        key_total, value_total,
    ):
        step = pl.program_id(1)
        query, key, value, grad = q_ref[0], k_ref[0], v_ref[0], grad_ref[0]
        key_t = key.astype(f32).T.astype(bf16)
        product_t = (grad.astype(f32) * out_ref[0].astype(f32)).T
        lane = lax.broadcasted_iota(jnp.int32, query.shape, 1)
        grad_key = jnp.zeros((rows, 128), f32)
        grad_value = jnp.zeros((rows, 128), f32)
        grad_queries = []
        for head in range(2):
            mine = lane // DH == head
            query_head = jnp.where(mine, query, jnp.zeros_like(query))
            grad_head = jnp.where(mine, grad, jnp.zeros_like(grad))
            delta = jnp.sum(product_t[head * DH : (head + 1) * DH], axis=0, keepdims=True)
            weights = jnp.exp(dot_nt(key, query_head) - lse_ref[0, head : head + 1, :])
            grad_soft = dot_nt(value, grad_head)
            grad_scores = (weights * (grad_soft - delta)).astype(bf16)
            grad_value += dot_nn(weights.astype(bf16), grad_head)
            grad_key += dot_nn(grad_scores, query_head)
            grad_queries.append(dot_nn(key_t[head * DH : (head + 1) * DH], grad_scores))
        half = query.shape[0]
        grad_query = jnp.concatenate(grad_queries, axis=0).T * (DH**-0.5)
        start = pl.multiple_of(step * half, half)
        cosine, sine = cos_ref[pl.ds(start, half), :], sin_ref[pl.ds(start, half), :]
        dq_ref[0] = (grad_query * cosine - swap_halves(grad_query) * sine).astype(bf16)

        @pl.when(step == 0)
        def _():
            key_total[...] = grad_key
            value_total[...] = grad_value

        @pl.when(step == 1)
        def _():
            total = key_total[...] + grad_key
            back = total * cos_ref[...] - swap_halves(total) * sin_ref[...]
            dkv_ref[0, :, :128] = back.astype(bf16)
            dkv_ref[0, :, 128:] = (value_total[...] + grad_value).astype(bf16)

    half, full = pair_specs(query, first, 2)
    out_half, _ = pair_specs(query, 0, 2)
    lse_spec = pl.BlockSpec((1, 2, rows // 2), lambda z, i: (z, 0, i))
    table = pl.BlockSpec(cosine.shape, lambda z, i: (0, 0))
    return call(
        kernel,
        "attention_backward",
        (count, 2),
        [half, full, full, half, out_half, lse_spec, table, table],
        [out_half, pl.BlockSpec((1, rows, 256), lambda z, i: (z, 0, 0))],
        [like((count, rows, 128)), like((count, rows, 256))],
        [pltpu.VMEM((rows, 128), f32)] * 2,
    )(*in_hbm(query, key, value, grad, out, lse, cosine, sine))


def lanes_of(refs):
    return jnp.concatenate([r[j] for r in refs for j in range(r.shape[0])], axis=1)


def blocks_by_rows(array, steps):
    return pl.BlockSpec(
        (array.shape[0], array.shape[1] // steps, array.shape[2]), lambda i: (0, i, 0)
    )


def rows_of(ref, start, stop):
    if start == 0 and stop == ref.shape[1]:
        return ref[...].reshape(-1, ref.shape[2])
    return jnp.concatenate([ref[z, start:stop] for z in range(ref.shape[0])], axis=0)


def attention_output_call(att, w, start):
    rows = att[0].shape[1]

    def kernel(*refs):
        *att_refs, w_ref, out_ref = refs
        out_ref[...] = dot_nn(lanes_of(att_refs), rows_of(w_ref, start, w_ref.shape[1])).astype(bf16)

    out = like((rows, w.shape[2]))
    return call(
        kernel,
        "attention_output",
        (2,),
        [blocks_by_rows(a, 2) for a in att] + [whole(w)],
        by_rows(out, 2),
        out,
    )(*att, w)


def swapped_rows(array):
    return pl.BlockSpec((array.shape[0] // 4, array.shape[1]), lambda i: ((i + 2) % 4, 0))


def middle_call(x, part, got, gains):
    def kernel(x_ref, part_ref, got_ref, gain_ref, mid_ref, out_ref):
        middle = x_ref[...].astype(f32) + (part_ref[...].astype(f32) + got_ref[...].astype(f32))
        mid_ref[...] = middle
        hats, _ = normalize(middle)
        out_ref[...] = (hats * gain_ref[1:2, :]).astype(bf16)

    tile = by_rows(x, 4)
    return call(
        kernel,
        "second_norm",
        (4,),
        [tile, tile, swapped_rows(got), whole(gains)],
        [tile, tile],
        [like(x.shape, f32), like(x.shape)],
    )(x, part, got, gains)


def lift_call(x, up, gate):
    hidden = up.shape[0] * up.shape[1]

    def kernel(x_ref, up_ref, gate_ref, hid_ref, to_in_ref, to_gate_ref):
        x = x_ref[...]
        w_up, w_gate = (r[...].reshape(hidden, -1) for r in (up_ref, gate_ref))
        for start in range(0, hidden, 512):
            part = slice(start, min(start + 512, hidden))
            lifted = dot_nt(x, w_up[part])
            gate = dot_nt(x, w_gate[part])
            phi = 0.5 * (1.0 + lax.erf(lifted * (0.5**0.5)))
            gelu = lifted * phi
            slope = phi + lifted * jnp.exp(-0.5 * lifted * lifted) * 0.3989422804014327
            hid_ref[:, part] = (gelu * gate).astype(bf16)
            to_in_ref[:, part] = (gate * slope).astype(bf16)
            to_gate_ref[:, part] = gelu.astype(bf16)

    out = like((x.shape[0], hidden))
    return call(
        kernel,
        "expand",
        (2,),
        [by_rows(x, 2), whole(up), whole(gate)],
        [by_rows(out, 2)] * 3,
        [out] * 3,
    )(x, up, gate)


def lower_call(hidden, w, middle):
    rows, width = middle.shape

    def kernel(hid_ref, w_ref, mid_ref, own_ref, oth_ref):
        total = dot_nn(hid_ref[...], w_ref[...].reshape(-1, width))

        @pl.when(pl.program_id(0) == 1)
        def _():
            own_ref[...] = mid_ref[...] + total

        @pl.when(pl.program_id(0) == 0)
        def _():
            oth_ref[...] = total.astype(bf16)

    first = pl.BlockSpec((rows // 2, width), lambda i: (0, 0))
    return call(
        kernel,
        "contract",
        (2,),
        [pl.BlockSpec((rows // 2, hidden.shape[1]), lambda i: (1 - i, 0)), whole(w), first],
        [first, first],
        [like((rows // 2, width), f32), like((rows // 2, width))],
    )(hidden, w, middle)


def output_call(own, got, index):
    def kernel(index_ref, own_ref, got_ref, out_ref):
        out_ref[...] = (pick(own_ref, index_ref) + pick(got_ref, index_ref).astype(f32)).astype(bf16)

    tile = by_rows(own, 2)
    return call(kernel, "layer_output", (2,), [scalars, tile, tile], tile, like(own.shape))(
        index, own, got
    )


def weight_gradient_call(lefts, right, blocks, split, extra=None):
    flat = lefts[0].ndim == 2
    columns = lefts[0].shape[1] // blocks if flat else lefts[0].shape[2]
    more = [] if extra is None else [extra]
    lead = sum(e.shape[0] for e in more)
    height = lead + columns
    width = right.shape[1]
    half = blocks // 2

    def kernel(*refs):
        left_refs = refs[: len(lefts)]
        right_ref = refs[len(lefts)]
        extra_refs = refs[len(lefts) + 1 : len(lefts) + 1 + len(more)]
        outs = refs[len(lefts) + 1 + len(more) :]
        left = left_refs[0][...] if flat else lanes_of(left_refs)

        def put(ref, place, values, part):
            ref[place, lead:] = values
            for e in extra_refs:
                ref[place, :lead] = e[:, part]

        for start in range(0, width, 512):
            grads = dot_tn(left, right_ref[:, start : start + 512]).astype(bf16)
            for z in range(blocks):
                block = grads[z * columns : (z + 1) * columns]
                if not split:
                    put(outs[0], (z, slice(start, start + 512)), block, None)
                    continue
                mine, x_rest, y_rest, to_x, to_y = outs
                for j in range(start // 256, start // 256 + 2):
                    part = slice(256 * j, 256 * j + 256)
                    values = block[:, 256 * j - start : 256 * j - start + 256]
                    if j == 0:
                        put(mine, z, values, part)
                    elif j == 1:
                        put(*((to_x, half + z) if z < half else (x_rest, z - half)), values, part)
                    elif j == 2:
                        put(*((y_rest, z) if z < half else (to_y, z)), values, part)
                    else:
                        put(*((to_x, z) if z < half else (to_y, z - half)), values, part)

    if split:
        out_shape = [like((n, height, width // 4)) for n in (blocks, half, half, blocks, blocks)]
    else:
        out_shape = [like((blocks, height, width))]

        def kernel(*refs):
            left_refs = refs[: len(lefts)]
            right_ref, out_ref = refs[len(lefts)], refs[-1]
            left = left_refs[0][...] if flat else lanes_of(left_refs)
            grads = dot_tn(left, right_ref[...]).astype(bf16)
            for z in range(blocks):
                out_ref[z, lead:] = grads[z * columns : (z + 1) * columns]
                if more:
                    out_ref[z, :lead] = refs[len(lefts) + 1][...]

    return call(
        kernel,
        "weight_gradient",
        (1,),
        [whole(a) for a in (*lefts, right, *more)],
        [whole(o) for o in out_shape],
        [kept(o) for o in out_shape],
    )(*lefts, right, *more)


def combine_call(first, second, x_got, y_got, near_rows):
    operands, out_shape = [], []
    if first is not None:
        operands += first[1:]
        out_shape += [like(first[1].shape)] * 2
    if second is not None:
        operands += second
        out_shape += [like(second[0].shape)]

    def kernel(*refs):
        ins, outs = list(refs[2 : 2 + len(operands)]), list(refs[2 + len(operands) :])
        x_ref, y_ref = refs[:2]
        if first is not None:
            x_rest, y_rest, x_out, y_out = ins.pop(0), ins.pop(0), outs.pop(0), outs.pop(0)
            half, rows = x_rest.shape[:2]
            for j in range(half):
                part = slice(j * rows, (j + 1) * rows)
                x_out[j] = (x_rest[j].astype(f32) + y_ref[part].astype(f32)).astype(bf16)
                y_out[j] = (y_rest[j].astype(f32) + x_ref[part].astype(f32)).astype(bf16)
        if second is not None:
            mine, x_near, y_near = ins
            half, rows = mine.shape[0] // 2, mine.shape[1]
            for j in range(half):
                near = slice((half + j) * rows, (half + j + 1) * rows)
                far = slice(near_rows + j * rows, near_rows + (j + 1) * rows)
                for place, near_ref, far_ref in ((j, x_near, y_ref), (half + j, y_near, x_ref)):
                    total = mine[place].astype(f32) + near_ref[near].astype(f32)
                    outs[0][place] = (total + far_ref[far].astype(f32)).astype(bf16)

    results = call(
        kernel,
        "gradient_sums",
        (1,),
        [whole(a) for a in (x_got, y_got, *operands)],
        [whole(o) for o in out_shape],
        out_shape,
    )(x_got, y_got, *operands)
    near = results[:2] if first is not None else None
    return near, results[-1] if second is not None else None


def hidden_back_call(dy, w, to_in, to_gate):
    hidden = to_in.shape[1]

    def kernel(dy_ref, w_ref, to_in_ref, to_gate_ref, in_ref, gate_ref):
        w = w_ref[...].reshape(hidden, -1)
        for start in range(0, hidden, 512):
            part = slice(start, min(start + 512, hidden))
            grad = dot_nt(dy_ref[...], w[part])
            in_ref[:, part] = (grad * to_in_ref[:, part].astype(f32)).astype(bf16)
            gate_ref[:, part] = (grad * to_gate_ref[:, part].astype(f32)).astype(bf16)

    tile = by_rows(to_in, 2)
    return call(
        kernel,
        "grad_lifted",
        (2,),
        [by_rows(dy, 2), whole(w), tile, tile],
        [tile, tile],
        [like(to_in.shape)] * 2,
    )(dy, w, to_in, to_gate)


def two_part_call(grad_in, grad_gate, up, gate):
    width = up.shape[2]

    def kernel(in_ref, gate_ref, up_ref, w_gate_ref, out_ref):
        total = dot_nn(in_ref[...], up_ref[...].reshape(-1, width))
        total += dot_nn(gate_ref[...], w_gate_ref[...].reshape(-1, width))
        out_ref[...] = total.astype(bf16)

    out = like((grad_in.shape[0], width))
    return call(
        kernel,
        "grad_normed_two",
        (2,),
        [by_rows(grad_in, 2), by_rows(grad_gate, 2), whole(up), whole(gate)],
        by_rows(out, 2),
        out,
    )(grad_in, grad_gate, up, gate)


def two_back_call(part, got, middle, dy, gains):
    rows, width = middle.shape

    def kernel(part_ref, got_ref, mid_ref, dy_ref, gain_ref, grad_ref, low_ref, gain_grad_ref):
        i = pl.program_id(0)
        grads = part_ref[...].astype(f32) + got_ref[...].astype(f32)
        back, gain_grad = unnormalize(grads, mid_ref[...], gain_ref[1:2, :])
        grad = dy_ref[...].astype(f32) + back
        low_ref[...] = grad.astype(bf16)

        @pl.when(i == 0)
        def _():
            gain_grad_ref[...] = jnp.zeros_like(gain_grad_ref)

        @pl.when(i < 2)
        def _():
            grad_ref[...] = grad
            gain_grad_ref[...] += jnp.broadcast_to(gain_grad, gain_grad_ref.shape)

    tile = by_rows(middle, 4)
    row = like((8, width), f32)
    return call(
        kernel,
        "second_norm_gradient",
        (4,),
        [tile, swapped_rows(got), tile, tile, whole(gains)],
        [
            pl.BlockSpec((rows // 4, width), lambda i: (jnp.minimum(i, 1), 0)),
            tile,
            whole(row),
        ],
        [like((rows // 2, width), f32), like(middle.shape), row],
    )(part, got, middle, dy, gains)


def att_grad_call(grad, w, start):
    blocks = w.shape[0]
    columns = w.shape[1] - start

    def kernel(g_ref, w_ref, out_ref):
        out = dot_nt(g_ref[...], rows_of(w_ref, start, w_ref.shape[1])).astype(bf16)
        for z in range(blocks):
            out_ref[z] = out[:, z * columns : (z + 1) * columns]

    out = like((blocks, grad.shape[0], columns))
    return call(
        kernel,
        "grad_attended",
        (2,),
        [by_rows(grad, 2), whole(w)],
        blocks_by_rows(out, 2),
        out,
    )(grad, w)


def one_part_call(queries, keys_values, w_query, query_start, w_key_value):
    rows, width = queries[0].shape[1], w_query.shape[2]
    count = len(queries)

    def kernel(*refs):
        left_refs = refs[: 2 * count]
        wq_ref, wkv_ref, own_ref, oth_ref = refs[2 * count :]
        left = lanes_of(left_refs)
        w = jnp.concatenate(
            [rows_of(wq_ref, query_start, wq_ref.shape[1]), rows_of(wkv_ref, 0, 256)], axis=0
        )
        total = dot_nn(left, w)

        @pl.when(pl.program_id(0) == 1)
        def _():
            own_ref[...] = total

        @pl.when(pl.program_id(0) == 0)
        def _():
            oth_ref[...] = total.astype(bf16)

    def half(array):
        shape = (array.shape[0], rows // 2, array.shape[2])
        return pl.BlockSpec(shape, lambda i: (0, 1 - i, 0))

    first = pl.BlockSpec((rows // 2, width), lambda i: (0, 0))
    return call(
        kernel,
        "grad_normed_one",
        (2,),
        [half(a) for a in (*queries, *keys_values)] + [whole(w_query), whole(w_key_value)],
        [first, first],
        [like((rows // 2, width), f32), like((rows // 2, width))],
    )(*in_hbm(*queries, *keys_values, w_query, w_key_value))


def one_back_call(own, got, x, grad_middle, gains, gain_two, index):
    rows, width = own.shape

    def kernel(
        index_ref, own_ref, got_ref, x_ref, mid_ref, gain_ref, gain_two_ref, grad_ref, gain_grad_ref,
        total_ref, low_ref,
    ):
        i = pl.program_id(0)
        grads = own_ref[...] + got_ref[...].astype(f32)
        back, gain_grad = unnormalize(grads, x_ref[...].astype(f32), gain_ref[0:1, :])
        low_ref[...] = (mid_ref[...] + back).astype(bf16)
        grad_ref[...] = pick(low_ref, index_ref)

        @pl.when(i == 0)
        def _():
            total_ref[...] = gain_grad

        @pl.when(i == 1)
        def _():
            total = total_ref[...] + gain_grad
            row = lax.broadcasted_iota(jnp.int32, gain_grad_ref.shape, 0)
            both = jnp.where(row == 0, total, jnp.where(row == 1, gain_two_ref[0:1, :], 0.0))
            gain_grad_ref[...] = both.astype(bf16)

    tile = by_rows(own, 2)
    x_tile = pl.BlockSpec((rows // 2, width), lambda i: (i, 0))
    gain_grads = like((16, width))
    return call(
        kernel,
        "first_norm_gradient",
        (2,),
        [scalars, tile, tile, x_tile, tile, whole(gains), whole(gain_two)],
        [tile, whole(gain_grads)],
        [like(own.shape), gain_grads],
        [pltpu.VMEM((1, width), f32), pltpu.VMEM((rows // 2, width), bf16)],
    )(index, own, got, x, grad_middle, gains, gain_two)


(
    X_IN,
    COT,
    BOTH,
    PAIR,
    LOW,
    INNER,
    COLUMN,
    W,
    NEAR,
    GRAD,
    TABLES,
    X0,
    X_OWN,
    GAINS,
    X,
    NORMED,
    QKV,
    ATT,
    LSE,
    Y0,
    PART,
    Y_OWN,
    MIDDLE,
    NORMED_TWO,
    HIDDEN,
    TO_IN,
    TO_GATE,
    DY,
    G,
    F,
    N,
    SUM,
    G_GATE,
    OUT,
    DQ,
    DKV,
    G_ATT,
    GRAD_MID,
    MID_LOW,
    GAIN_TWO,
    OUT1,
    OWN,
    OTHER,
    OUT0,
    GAIN_GRADS,
    DX,
    DX1,
    DX0,
    UPDATED,
) = range(49)


def make_per_device(dp, tensor):
    count = dp * tensor
    chips = dp // 2
    chip_bits = chips.bit_length() - 1
    square = chip_bits == 2
    half = tensor // 2

    def permute(value, pairs):
        return lax.ppermute(value, AXES, pairs)

    def exchange(value, mask):
        return permute(value, [(i, i ^ mask) for i in range(count)])

    def over_chip(value, bit):
        return exchange(value, (2 * tensor) << bit)

    def over_core(value, pieces=1):
        rows = value.shape[0] // pieces
        got = [exchange(value[i * rows : (i + 1) * rows], tensor) for i in range(pieces)]
        return got[0] if pieces == 1 else jnp.concatenate(got, axis=0)

    def spread_pairs(r):
        pairs = []
        for i in range(count):
            z = i % tensor
            core = (i // tensor) % 2
            chip = i // (2 * tensor)
            pairs.append((i, (chip * 2 + z % 2) * tensor + (r ^ (z // 2)) * 2 + core))
        return pairs

    def by_column(blocks, me_z):
        for bit in range(tensor.bit_length() - 1):
            odd = (me_z >> bit) % 2 == 1
            blocks = [jnp.where(odd, blocks[k ^ (1 << bit)], blocks[k]) for k in range(tensor)]
        return blocks

    inner = [(i, i ^ 3) for i in range(count) if i % tensor in (1, 2)]
    outward = [(i, i ^ 1) for i in range(count) if i % tensor in (1, 2)]

    def gather_near_z(rows, me_z):
        got = exchange(rows, 1)
        low = me_z % 2 == 0
        return jnp.stack([jnp.where(low, rows, got), jnp.where(low, got, rows)])

    def gather_far_z(pair, got, me_z):
        sent = permute(got, outward)
        other = jnp.where((me_z == 0) | (me_z == 3), sent, got)
        low = me_z < 2
        return jnp.concatenate([jnp.where(low, pair, other), jnp.where(low, other, pair)], axis=0)

    def gather_plane(columns):
        current = columns[None]
        for bit in range(chip_bits):
            current = jnp.concatenate([current, over_chip(current, bit)], axis=0)
        return current.transpose(1, 2, 0, 3).reshape(columns.shape[:2] + (-1,))

    def low_sum(*values):
        return sum(v.astype(f32) for v in values).astype(bf16)

    def reduce_plane(parts):
        current = parts
        for bit in reversed(range(chip_bits)):
            middle = current.shape[0] // 2
            current = low_sum(current[:middle], over_chip(current[middle:], bit))
        return current[0]

    def reduce_column(blocks):
        result = blocks[0].astype(f32)
        for k in range(1, tensor):
            result = result + exchange(blocks[k], k).astype(f32)
        return result

    def per_device(
        inputs,
        cotangent,
        attention_in,
        attention_out,
        expand_weight,
        contract_weight,
        norm_gains,
        attention_in_first,
        attention_in_second,
        attention_out_first,
        attention_out_second,
        expand_first,
        expand_second,
        contract_first,
        contract_second,
        gains_first,
        gains_second,
    ):
        block = attention_in.shape[0]
        head_columns = attention_in.shape[2]
        hidden_local = expand_weight.shape[2]
        local_rows = inputs.shape[2]
        me_dp = lax.axis_index("dp")
        me_z = lax.axis_index("tensor")
        core = me_dp % 2
        z_high = me_z // 2

        me_chip = me_dp // 2
        index = me_chip ^ jnp.arange(chips, dtype=jnp.int32)
        aligned = block % 128 == 0
        kernel_index = index if aligned else jnp.zeros((1,), jnp.int32)

        def outside(values):
            if aligned:
                return values
            shaped = values.reshape(values.shape[0], chips, 2 * block)
            return jnp.take(shaped, index, axis=1).reshape(values.shape)

        def spread(values, r):
            part = lax.dynamic_index_in_dim(values[:, 0], r ^ z_high, 0, keepdims=False)
            return permute(part, spread_pairs(r))

        def collect(values, r):
            part = values[r * local_rows : (r + 1) * local_rows]
            return permute(part, [(b, a) for a, b in spread_pairs(r)])

        def assemble(first, second):
            odd = z_high == 1
            return jnp.stack([jnp.where(odd, second, first), jnp.where(odd, first, second)])[:, None]

        def rotary_tables():
            row_starts = [
                ((r ^ z_high) * 2 + (core ^ c)) * local_rows for c in range(2) for r in range(2)
            ]
            positions = jnp.concatenate([s + jnp.arange(local_rows) for s in row_starts]).astype(f32)
            exponents = jnp.arange(0, DH, 2).astype(f32) / DH
            angles = positions[:, None] * jnp.power(rope_theta, -exponents)[None, :]
            cosine, sine = jnp.cos(angles), jnp.sin(angles)
            cosine = jnp.concatenate([cosine] * 4, axis=-1)
            sine = jnp.concatenate([-sine, sine] * 2, axis=-1)
            return cosine, sine

        cut = (hidden_local // 2 + 15) // 16 * 16
        spare = 2 * cut - hidden_local
        head_cut = head_columns // 2
        low_in = attention_in.astype(bf16).reshape(block, 3, 2, head_cut).transpose(2, 1, 3, 0)
        low_out = attention_out.astype(bf16).reshape(block, 2, head_cut).transpose(1, 2, 0)
        low_expand = jnp.pad(expand_weight.astype(bf16).transpose(1, 2, 0), ((0, 0), (0, spare), (0, 0)))
        low_expand = low_expand.reshape(2, 2, cut, block).transpose(1, 0, 2, 3)
        low_contract = jnp.pad(contract_weight.astype(bf16).T, ((0, spare), (0, 0)))
        low_contract = low_contract.reshape(2, cut, block)
        low_gains = jnp.pad(norm_gains.astype(bf16), ((0, 14), (0, 0)))
        lead = low_gains.shape[0]
        both = jnp.concatenate(
            [
                jnp.stack([low_gains, low_gains]),
                low_in.reshape(2, -1, block),
                low_out,
                low_expand.reshape(2, -1, block),
                low_contract,
            ],
            axis=1,
        )
        sizes = [lead + head_cut, 3 * head_cut, cut, cut, cut]
        starts = [sum(sizes[:k]) for k in range(len(sizes) + 1)]
        last = len(sizes)
        first_core = core == 0

        def side_by_side(mine, got):
            return jnp.concatenate(
                [jnp.where(first_core, mine, got), jnp.where(first_core, got, mine)], axis=-1
            )

        state = {X_IN: inputs, COT: cotangent, BOTH: both}
        held = []
        again = []

        def run(work):
            nonlocal state
            new = {}
            late = held[:]
            held[:] = again
            again.clear()
            work(state, new)
            for values in late:
                new.update(values)
            state.update(new)
            names = list(state)
            state = dict(zip(names, lax.optimization_barrier([state[n] for n in names])))

        def column_a(s, new, k):
            stop = starts[k + 1] if k < 3 else starts[last]
            new[PAIR, k] = gather_near_z(s[LOW][starts[k] : stop], me_z)

        def column_b(s, new, k):
            new[INNER, k] = permute(s[PAIR, k], inner)

        def column_c(s, new, k):
            column = gather_far_z(s.pop((PAIR, k)), s.pop((INNER, k)), me_z)
            if k < 3:
                new[COLUMN, k] = column
            else:
                new[COLUMN, 3], new[COLUMN, 4] = column[:, : sizes[3]], column[:, sizes[3] :]

        def plane(s, new, k):
            if not square:
                if k < last:
                    new[W, k] = gather_plane(s.pop((COLUMN, k)))
                return
            sends, first_rows = ([], []), 0
            if k < last:
                column = s[COLUMN, k]
                first_rows = column.shape[0] * column.shape[1]
                for way in range(2):
                    sends[way].append(column.reshape(first_rows, -1))
            if k > 0:
                got = s[NEAR, k - 1]
                rows = half * sizes[k - 1]
                sends[0].append(got[1][rows : 2 * rows])
                sends[1].append(got[0][:rows])
            got = tuple(over_chip(jnp.concatenate(sends[way], axis=0), way) for way in range(2))
            if k < last:
                new[NEAR, k] = got
            if k > 0:
                new[W, k - 1] = weave_call(
                    s.pop((COLUMN, k - 1)), *s.pop((NEAR, k - 1)), *got, first_rows
                )

        step_rates = (
            2.5 * D ** (-0.5),
            2.5 * max(1, 4 * H * DH // SEQ) ** (-0.5),
            2.5 * D ** (-0.5),
            2.5 * FF ** (-0.5),
            0.25,
        )

        def joined(s, k, rows):
            return jnp.concatenate(s[GRAD, k], axis=0)[:rows]

        def joined_heads(s):
            key_value = [g.reshape(2, head_cut, block) for g in s[GRAD, 4]]
            query = [g[lead:] for g in s[GRAD, 5]]
            grads = jnp.stack(
                [jnp.concatenate(query, axis=0)]
                + [jnp.concatenate([g[i] for g in key_value], axis=0) for i in range(2)]
            )
            return lax.optimization_barrier(grads.transpose(2, 0, 1))

        def first_updates(s):
            grad_down, grad_up, grad_gate = (joined(s, k, hidden_local) for k in range(3))
            grad_expand = jnp.stack([grad_up, grad_gate]).transpose(2, 0, 1)
            grad_out, grad_expand, grad_down = lax.optimization_barrier(
                (joined(s, 3, head_columns).T, grad_expand, grad_down.T)
            )
            return (
                adamw_update(
                    attention_out, attention_out_first, attention_out_second, grad_out, step_rates[1]
                ),
                adamw_update(expand_weight, expand_first, expand_second, grad_expand, step_rates[2]),
                adamw_update(
                    contract_weight, contract_first, contract_second, grad_down, step_rates[3]
                ),
            )

        def f0(s, new):
            pair = s.pop(BOTH)
            mine = jnp.where(first_core, pair[0], pair[1])
            got = over_core(jnp.where(first_core, pair[1], pair[0]))
            new[LOW] = side_by_side(mine, got)

        run(f0)

        def f1(s, new):
            column_a(s, new, 0)

        run(f1)

        def f2(s, new):
            column_b(s, new, 0)
            column_a(s, new, 1)

        run(f2)

        def f3(s, new):
            column_c(s, new, 0)
            column_b(s, new, 1)
            column_a(s, new, 2)
            new[TABLES] = rotary_tables()

        run(f3)

        def f4(s, new):
            plane(s, new, 0)
            column_c(s, new, 1)
            column_b(s, new, 2)
            column_a(s, new, 3)

        run(f4)

        def f5(s, new):
            plane(s, new, 1)
            column_c(s, new, 2)
            column_b(s, new, 3)
            new[X0] = spread(s[X_IN], 0)

        run(f5)

        def f6(s, new):
            plane(s, new, 2)
            column_c(s, new, 3)
            new[X_OWN] = jnp.concatenate([s.pop(X0), spread(s.pop(X_IN), 1)], axis=0)

        run(f6)

        def f7(s, new):
            plane(s, new, 3)
            rows = s.pop(X_OWN)
            x_raw = jnp.concatenate([rows, over_core(rows, 2)], axis=0)
            new[GAINS] = s[W, 0][0, :lead].astype(f32)
            new[X], new[NORMED] = norm_call(outside(x_raw), new[GAINS], kernel_index)
            query, key, value = qkv_call(new[NORMED], s[W, 0], lead, s[W, 1], *s[TABLES])
            new[QKV] = (query, key, value)
            new[ATT, 0], new[LSE, 0] = attend_call(query, key, value, 0, tensor // 2)
            new[Y0] = spread(s[COT], 0)

        run(f7)

        def f8(s, new):
            plane(s, new, 4)
            new[ATT, 1], new[LSE, 1] = attend_call(*s[QKV], tensor // 2, tensor // 2)
            new[PART] = attention_output_call((s[ATT, 0], new[ATT, 1]), s[W, 1], 2 * head_cut)
            new[Y_OWN] = jnp.concatenate([s.pop(Y0), spread(s.pop(COT), 1)], axis=0)

        run(f8)

        def f9(s, new):
            plane(s, new, 5)
            part, rows = s.pop(PART), s.pop(Y_OWN)
            new[MIDDLE], new[NORMED_TWO] = middle_call(
                s[X], part, over_core(part, 4), s[GAINS]
            )
            new[HIDDEN], new[TO_IN], new[TO_GATE] = lift_call(
                new[NORMED_TWO], s[W, 2], s[W, 3]
            )
            y_raw = jnp.concatenate([rows, over_core(rows)], axis=0)
            new[DY] = order_call(outside(y_raw), kernel_index)
            made(new, 0, [new[HIDDEN]], new[DY])

        def made(new, k, lefts, right, extra=None):
            grads = weight_gradient_call(lefts, right, tensor, square and aligned, extra)
            if not square or not aligned:
                (full,) = grads
                grads = full.reshape(full.shape[:2] + (chips, -1)).transpose(2, 0, 1, 3)
            new[G, k] = grads

        def plane_back(s, new, k):
            if not square:
                if (G, k) in s:
                    new[F, k] = [b for b in reduce_plane(s.pop((G, k)))]
                return
            flat = lambda a: a.reshape(-1, a.shape[-1])
            to_x, to_y, rows = [], [], 0
            if (G, k) in s:
                mine, x_rest, y_rest, x_out, y_out = s.pop((G, k))
                rows = x_out.shape[0] * x_out.shape[1]
                to_x.append(flat(x_out))
                to_y.append(flat(y_out))
            if (N, k - 1) in s:
                x_last, y_last, mine_last, x_near, y_near = s.pop((N, k - 1))
                to_x.append(flat(x_last))
                to_y.append(flat(y_last))
            x_got = over_chip(jnp.concatenate(to_x, axis=0), 0)
            y_got = over_chip(jnp.concatenate(to_y, axis=0), 1)
            first = (mine, x_rest, y_rest) if rows else None
            second = (mine_last, x_near, y_near) if len(to_x) > 1 or not rows else None
            near, far = combine_call(first, second, x_got, y_got, rows)
            if first is not None:
                new[N, k] = (*near, mine, x_got, y_got)
            if second is not None:
                new[F, k - 1] = far

        def whole_blocks(blocks):
            return blocks if square else jnp.stack(blocks)

        def scatter(s, k):
            total = lax.psum_scatter(
                whole_blocks(s.pop((F, k))), "tensor", scatter_dimension=0, tiled=False
            )
            held.append({(SUM, k): total})

        def column(s, new, *chunks):
            blocks = [by_column(s.pop((F, k)), me_z) for k in chunks]
            total = reduce_column([jnp.concatenate(b, axis=0) for b in zip(*blocks)])
            start = 0
            for k, b in zip(chunks, blocks):
                new[SUM, k] = total[start : start + b[0].shape[0]].astype(bf16)
                start += b[0].shape[0]

        def trade(s, new, *chunks):
            sums = [s.pop((SUM, k)) for k in chunks]
            total = jnp.concatenate(sums, axis=0)
            mine = jnp.where(first_core, total[:, :block], total[:, block:])
            got = over_core(jnp.where(first_core, total[:, block:], total[:, :block]))
            start = 0
            for k, rows in zip(chunks, [a.shape[0] for a in sums]):
                a, b = mine[start : start + rows], got[start : start + rows]
                new[GRAD, k] = (
                    jnp.where(first_core, a, b).astype(f32),
                    jnp.where(first_core, b, a).astype(f32),
                )
                start += rows

        run(f9)

        def s1(s, new):
            plane_back(s, new, 0)
            own, other = lower_call(s.pop(HIDDEN), s[W, 4], s[MIDDLE])
            g_in, g_gate = hidden_back_call(
                s[DY], s.pop((W, 4)), s.pop(TO_IN), s.pop(TO_GATE)
            )
            new[G_GATE] = g_gate
            new[PART] = two_part_call(g_in, g_gate, s.pop((W, 2)), s.pop((W, 3)))
            made(new, 1, [g_in], s[NORMED_TWO])
            new[OUT] = outside(output_call(own, over_core(other), kernel_index))

        run(s1)

        def attention_back(s, new, p):
            new[DQ, p], new[DKV, p] = attend_back_call(
                *s[QKV], s[G_ATT], s[ATT, p], s.pop((LSE, p)), *s[TABLES],
                p * (tensor // 2), tensor // 2,
            )

        def s2(s, new):
            plane_back(s, new, 1)
            part = s.pop(PART)
            new[GRAD_MID], new[MID_LOW], new[GAIN_TWO] = two_back_call(
                part, over_core(part, 4), s.pop(MIDDLE), s.pop(DY), s[GAINS]
            )
            made(new, 2, [s.pop(G_GATE)], s.pop(NORMED_TWO))
            s[G_ATT] = new[G_ATT] = att_grad_call(new[MID_LOW], s[W, 1], 2 * head_cut)
            attention_back(s, new, 0)
            new[OUT1] = collect(s[OUT], 1)

        run(s2)

        def s3(s, new):
            scatter(s, 0)
            plane_back(s, new, 2)
            attention_back(s, new, 1)
            made(new, 3, [s[ATT, 0], s[ATT, 1]], s[MID_LOW])
            new[OWN], new[OTHER] = one_part_call(
                (s[DQ, 0], new[DQ, 1]), (s[DKV, 0], new[DKV, 1]), s[W, 0], lead, s[W, 1]
            )
            new[OUT0] = collect(s[OUT], 0)

        run(s3)

        def s4(s, new):
            scatter(s, 1)
            plane_back(s, new, 3)
            dx, new[GAIN_GRADS] = one_back_call(
                s.pop(OWN), over_core(s.pop(OTHER), 2), s.pop(X), s.pop(GRAD_MID),
                s[GAINS], s.pop(GAIN_TWO), kernel_index,
            )
            new[DX] = outside(dx)
            made(new, 4, [s[DKV, 0], s[DKV, 1]], s[NORMED])
            new[DX1] = collect(new[DX], 1)

        run(s4)

        def s5(s, new):
            scatter(s, 2)
            plane_back(s, new, 4)
            made(new, 5, [s[DQ, 0], s[DQ, 1]], s[NORMED], s.pop(GAIN_GRADS))
            new[DX0] = collect(s[DX], 0)

        run(s5)

        def s6(s, new):
            plane_back(s, new, 5)
            column(s, new, 3)

        run(s6)

        def s7(s, new):
            plane_back(s, new, 6)
            column(s, new, 4)
            trade(s, new, 0, 1, 2, 3)

        run(s7)

        def s8(s, new):
            column(s, new, 5)
            new[UPDATED] = first_updates(s)

        run(s8)

        def s9(s, new):
            trade(s, new, 4, 5)

        run(s9)

        layer_output = assemble(state[OUT0], state[OUT1])
        input_gradient = assemble(state[DX0], state[DX1])
        grad_qkv = joined_heads(state)
        gain_total = sum(g[:2] for g in state[GRAD, 5])
        qkv_new = adamw_update(
            attention_in, attention_in_first, attention_in_second, grad_qkv, step_rates[0]
        )
        gains_new = adamw_update(norm_gains, gains_first, gains_second, gain_total, step_rates[4])
        out_new, expand_new, contract_new = state[UPDATED]
        return (
            layer_output,
            input_gradient,
            *qkv_new,
            *out_new,
            *expand_new,
            *contract_new,
            *gains_new,
        )

    return per_device


def solution(mesh):
    activation = P(None, "dp", "tensor", None)
    cube = P("dp", None, "tensor")
    flat = P("dp", "tensor")
    gain = P(None, "dp")
    return jax.shard_map(
        make_per_device(mesh.shape["dp"], mesh.shape["tensor"]),
        mesh=mesh,
        in_specs=(
            activation, activation, cube, flat, cube, flat, gain,
            cube, cube, flat, flat, cube, cube, flat, flat, gain, gain,
        ),
        out_specs=(
            activation, activation, cube, cube, cube, flat, flat, flat,
            cube, cube, cube, flat, flat, flat, gain, gain, gain,
        ),
        check_vma=False,
    )
```

```python
import jax
import jax.numpy as jnp
from jax import lax
from jax.experimental import pallas as pl
from jax.experimental.pallas import tpu as pltpu
from jax.sharding import PartitionSpec as P

D = 1024
H = 16
DH = 64
FF = 2624
SEQ = 1024
STEP = 10

epsilon_norm = 1e-05
rope_theta = 160000.0
beta_first = 0.9
beta_second = 0.98
epsilon_adam = 1e-06
weight_decay = 1e-05

AXES = ("dp", "tensor")
bf16 = jnp.bfloat16
f32 = jnp.float32


def dot_nt(left, right):
    return lax.dot_general(left, right, (((1,), (1,)), ((), ())), preferred_element_type=f32)


def dot_tn(left, right):
    return lax.dot_general(left, right, (((0,), (0,)), ((), ())), preferred_element_type=f32)


def dot_nn(left, right):
    return jnp.dot(left, right, preferred_element_type=f32)


def adamw_update(weight, first_moment, second_moment, gradient, step_rate):
    first_new = beta_first * first_moment + (1.0 - beta_first) * gradient
    second_new = beta_second * second_moment + (1.0 - beta_second) * gradient * gradient
    first_hat = first_new / (1.0 - beta_first**STEP)
    second_hat = second_new / (1.0 - beta_second**STEP)
    weight_new = weight - step_rate * (
        first_hat / (jnp.sqrt(second_hat) + epsilon_adam) + weight_decay * weight
    )
    return (weight_new, first_new, second_new)


def whole(array):
    return pl.BlockSpec(
        array.shape, lambda i, rank=array.ndim: (0,) * rank, pipeline_mode=pl.Buffered(1)
    )


def by_block(array):
    return pl.BlockSpec((1,) + array.shape[1:], lambda z: (z, 0, 0))


def by_rows(array, steps):
    return pl.BlockSpec((array.shape[0] // steps, array.shape[1]), lambda i: (i, 0))


def like(shape, dtype=bf16):
    return jax.ShapeDtypeStruct(shape, dtype)


def kept(array):
    return pltpu.HBM(array.shape, array.dtype)


microseconds = dict(
    feature_order=3.0,
    gathered_weight=3.0,
    gradient_sums=3.0,
    first_norm=4.0,
    qkv_projection=6.0,
    attention_forward=9.0,
    attention_output=2.5,
    second_norm=4.0,
    expand=12.0,
    contract=5.0,
    layer_output=2.0,
    weight_gradient=5.0,
    grad_lifted=6.0,
    grad_normed_two=8.0,
    second_norm_gradient=5.0,
    grad_attended=2.5,
    attention_backward=14.0,
    grad_normed_one=6.0,
    first_norm_gradient=3.0,
)


def cost(name):
    return pl.CostEstimate(
        flops=int(microseconds[name] * 0.35e9),
        bytes_accessed=int(microseconds[name] * 1.2e6),
        transcendentals=0,
    )


def call(kernel, name, grid, in_specs, out_specs, out_shape, scratch=()):
    return pl.pallas_call(
        kernel,
        grid=grid,
        in_specs=in_specs,
        out_specs=out_specs,
        out_shape=out_shape,
        scratch_shapes=list(scratch),
        compiler_params=pltpu.CompilerParams(vmem_limit_bytes=20 << 20),
        cost_estimate=cost(name),
        name=name,
    )


def swap_halves(values):
    lane = lax.broadcasted_iota(jnp.int32, values.shape, 1)
    return jnp.where(
        lane % DH < DH // 2,
        pltpu.roll(values, values.shape[1] - DH // 2, 1),
        pltpu.roll(values, DH // 2, 1),
    )


def normalize(values):
    centered = values - jnp.mean(values, axis=1, keepdims=True)
    scale = lax.rsqrt(jnp.mean(centered * centered, axis=1, keepdims=True) + epsilon_norm)
    return centered * scale, scale


def unnormalize(grads, values, gain):
    hats, scale = normalize(values)
    gain_grad = jnp.sum(grads * hats, axis=0, keepdims=True)
    errors = grads * gain
    average = jnp.mean(errors, axis=1, keepdims=True)
    along = jnp.mean(errors * hats, axis=1, keepdims=True)
    return scale * (errors - average - hats * along), gain_grad


def pick(ref, index_ref):
    count = index_ref.shape[0]
    if count == 1:
        return ref[...]
    block = ref.shape[1] // count
    parts = [ref[:, pl.ds(pl.multiple_of(index_ref[j] * block, block), block)] for j in range(count)]
    return jnp.concatenate(parts, axis=1)


def in_hbm(*arrays):
    return tuple(pltpu.with_memory_space_constraint(a, pltpu.HBM) for a in arrays)


scalars = pl.BlockSpec(memory_space=pltpu.SMEM)


def order_call(values, index):
    def kernel(index_ref, in_ref, out_ref):
        out_ref[...] = pick(in_ref, index_ref)

    tile = by_rows(values, 2)
    return call(
        kernel, "feature_order", (2,), [scalars, tile], tile, like(values.shape, values.dtype)
    )(index, values)


def norm_call(x, gains, index):
    def kernel(index_ref, x_ref, gain_ref, x_out_ref, out_ref):
        values = pick(x_ref, index_ref)
        x_out_ref[...] = values
        hats, _ = normalize(values.astype(f32))
        out_ref[...] = (hats * gain_ref[0:1, :]).astype(bf16)

    tile = by_rows(x, 4)
    return call(
        kernel, "first_norm", (4,), [scalars, tile, whole(gains)], [tile] * 2, [like(x.shape)] * 2
    )(index, x, gains)


def qkv_call(x, w, start, cosine, sine):
    rows, blocks = x.shape[0], w.shape[0]

    def kernel(x_ref, w_ref, cos_ref, sin_ref, q_ref, k_ref, v_ref):
        mixed = dot_nt(x_ref[...], w_ref[0, start : start + 384])
        cosine, sine = cos_ref[...], sin_ref[...]
        query, key = mixed[:, :128], mixed[:, 128:256]
        query = query * cosine + swap_halves(query) * sine
        key = key * cosine + swap_halves(key) * sine
        q_ref[0] = query.astype(bf16) * bf16(DH**-0.5)
        k_ref[0] = key.astype(bf16)
        v_ref[0] = mixed[:, 256:].astype(bf16)

    out = like((blocks, rows, 128))
    return call(
        kernel,
        "qkv_projection",
        (blocks,),
        [whole(x), by_block(w), whole(cosine), whole(sine)],
        [by_block(out)] * 3,
        [out] * 3,
    )(x, w, cosine, sine)


def pair_specs(array, first, halves):
    rows = array.shape[1]
    return (
        pl.BlockSpec((1, rows // halves, array.shape[2]), lambda z, i: (first + z, i, 0)),
        pl.BlockSpec((1, rows, array.shape[2]), lambda z, i: (first + z, 0, 0)),
    )


def weave_call(column, x_near, y_near, x_far, y_far, far_rows):
    blocks, rows, width = column.shape
    half = blocks // 2

    def kernel(col_ref, x_ref, y_ref, x_far_ref, y_far_ref, out_ref):
        z = pl.program_id(0)
        out_ref[0, :, :width] = col_ref[0]
        out_ref[0, :, width : 2 * width] = x_ref[...]
        out_ref[0, :, 2 * width : 3 * width] = y_ref[...]
        start = pl.multiple_of(far_rows + z % half * rows, 16)

        @pl.when(z < half)
        def _():
            out_ref[0, :, 3 * width :] = y_far_ref[pl.ds(start, rows), :]

        @pl.when(z >= half)
        def _():
            out_ref[0, :, 3 * width :] = x_far_ref[pl.ds(start, rows), :]

    near = pl.BlockSpec((rows, width), lambda z: (z, 0))
    out = like((blocks, rows, 4 * width))
    return call(
        kernel,
        "gathered_weight",
        (blocks,),
        [by_block(column), near, near, whole(x_far), whole(y_far)],
        by_block(out),
        out,
    )(column, x_near, y_near, x_far, y_far)


def attend_call(query, key, value, first, count):
    rows = query.shape[1]

    def kernel(q_ref, k_ref, v_ref, out_ref, lse_ref):
        query, key = q_ref[0], k_ref[0]
        value_t = v_ref[0].astype(f32).T.astype(bf16)
        lane = lax.broadcasted_iota(jnp.int32, query.shape, 1)
        outs = []
        for head in range(2):
            query_head = jnp.where(lane // DH == head, query, jnp.zeros_like(query))
            scores = dot_nt(key, query_head)
            peak = jnp.max(scores, axis=0, keepdims=True)
            weights = jnp.exp(scores - peak)
            total = jnp.sum(weights, axis=0, keepdims=True)
            out = dot_nn(value_t[head * DH : (head + 1) * DH], weights.astype(bf16))
            outs.append(out / total)
            lse_ref[0, head : head + 1, :] = peak + jnp.log(total)
        out_ref[0] = jnp.concatenate(outs, axis=0).T.astype(bf16)

    half, full = pair_specs(query, first, 2)
    out_half, _ = pair_specs(query, 0, 2)
    lse = pl.BlockSpec((1, 2, rows // 2), lambda z, i: (z, 0, i))
    return call(
        kernel,
        "attention_forward",
        (count, 2),
        [half, full, full],
        [out_half, lse],
        [like((count, rows, 128)), like((count, 2, rows), f32)],
    )(query, key, value)


def attend_back_call(query, key, value, grad, out, lse, cosine, sine, first, count):
    rows = query.shape[1]

    def kernel(
        q_ref, k_ref, v_ref, grad_ref, out_ref, lse_ref, cos_ref, sin_ref, dq_ref, dkv_ref,
        key_total, value_total,
    ):
        step = pl.program_id(1)
        query, key, value, grad = q_ref[0], k_ref[0], v_ref[0], grad_ref[0]
        key_t = key.astype(f32).T.astype(bf16)
        product_t = (grad.astype(f32) * out_ref[0].astype(f32)).T
        lane = lax.broadcasted_iota(jnp.int32, query.shape, 1)
        grad_key = jnp.zeros((rows, 128), f32)
        grad_value = jnp.zeros((rows, 128), f32)
        grad_queries = []
        for head in range(2):
            mine = lane // DH == head
            query_head = jnp.where(mine, query, jnp.zeros_like(query))
            grad_head = jnp.where(mine, grad, jnp.zeros_like(grad))
            delta = jnp.sum(product_t[head * DH : (head + 1) * DH], axis=0, keepdims=True)
            weights = jnp.exp(dot_nt(key, query_head) - lse_ref[0, head : head + 1, :])
            grad_soft = dot_nt(value, grad_head)
            grad_scores = (weights * (grad_soft - delta)).astype(bf16)
            grad_value += dot_nn(weights.astype(bf16), grad_head)
            grad_key += dot_nn(grad_scores, query_head)
            grad_queries.append(dot_nn(key_t[head * DH : (head + 1) * DH], grad_scores))
        half = query.shape[0]
        grad_query = jnp.concatenate(grad_queries, axis=0).T * (DH**-0.5)
        start = pl.multiple_of(step * half, half)
        cosine, sine = cos_ref[pl.ds(start, half), :], sin_ref[pl.ds(start, half), :]
        dq_ref[0] = (grad_query * cosine - swap_halves(grad_query) * sine).astype(bf16)

        @pl.when(step == 0)
        def _():
            key_total[...] = grad_key
            value_total[...] = grad_value

        @pl.when(step == 1)
        def _():
            total = key_total[...] + grad_key
            back = total * cos_ref[...] - swap_halves(total) * sin_ref[...]
            dkv_ref[0, :, :128] = back.astype(bf16)
            dkv_ref[0, :, 128:] = (value_total[...] + grad_value).astype(bf16)

    half, full = pair_specs(query, first, 2)
    out_half, _ = pair_specs(query, 0, 2)
    lse_spec = pl.BlockSpec((1, 2, rows // 2), lambda z, i: (z, 0, i))
    table = pl.BlockSpec(cosine.shape, lambda z, i: (0, 0))
    return call(
        kernel,
        "attention_backward",
        (count, 2),
        [half, full, full, half, out_half, lse_spec, table, table],
        [out_half, pl.BlockSpec((1, rows, 256), lambda z, i: (z, 0, 0))],
        [like((count, rows, 128)), like((count, rows, 256))],
        [pltpu.VMEM((rows, 128), f32)] * 2,
    )(*in_hbm(query, key, value, grad, out, lse, cosine, sine))


def lanes_of(groups):
    return jnp.concatenate([r[j] for g in groups for j in range(g[0].shape[0]) for r in g], axis=1)


def paired(refs, count):
    return [refs[i::count] for i in range(count)]


def blocks_by_rows(array, steps):
    return pl.BlockSpec(
        (array.shape[0], array.shape[1] // steps, array.shape[2]), lambda i: (0, i, 0)
    )


def rows_of(ref, start, stop):
    if start == 0 and stop == ref.shape[1]:
        return ref[...].reshape(-1, ref.shape[2])
    return jnp.concatenate([ref[z, start:stop] for z in range(ref.shape[0])], axis=0)


def attention_output_call(att, w, start):
    rows = att[0].shape[1]

    def kernel(*refs):
        *att_refs, w_ref, out_ref = refs
        att = lanes_of([[r] for r in att_refs])
        out_ref[...] = dot_nn(att, rows_of(w_ref, start, w_ref.shape[1])).astype(bf16)

    out = like((rows, w.shape[2]))
    return call(
        kernel,
        "attention_output",
        (2,),
        [blocks_by_rows(a, 2) for a in att] + [whole(w)],
        by_rows(out, 2),
        out,
    )(*att, w)


def swapped_rows(array):
    return pl.BlockSpec((array.shape[0] // 4, array.shape[1]), lambda i: ((i + 2) % 4, 0))


def middle_call(x, part, got, gains):
    def kernel(x_ref, part_ref, got_ref, gain_ref, mid_ref, out_ref):
        middle = x_ref[...].astype(f32) + (part_ref[...].astype(f32) + got_ref[...].astype(f32))
        mid_ref[...] = middle
        hats, _ = normalize(middle)
        out_ref[...] = (hats * gain_ref[1:2, :]).astype(bf16)

    tile = by_rows(x, 4)
    return call(
        kernel,
        "second_norm",
        (4,),
        [tile, tile, swapped_rows(got), whole(gains)],
        [tile, tile],
        [like(x.shape, f32), like(x.shape)],
    )(x, part, got, gains)


def lift_call(x, up, gate):
    hidden = up.shape[0] * up.shape[1]

    def kernel(x_ref, up_ref, gate_ref, hid_ref, to_in_ref, to_gate_ref):
        x = x_ref[...]
        w_up, w_gate = (r[...].reshape(hidden, -1) for r in (up_ref, gate_ref))
        for start in range(0, hidden, 512):
            part = slice(start, min(start + 512, hidden))
            lifted = dot_nt(x, w_up[part])
            gate = dot_nt(x, w_gate[part])
            phi = 0.5 * (1.0 + lax.erf(lifted * (0.5**0.5)))
            gelu = lifted * phi
            slope = phi + lifted * jnp.exp(-0.5 * lifted * lifted) * 0.3989422804014327
            hid_ref[:, part] = (gelu * gate).astype(bf16)
            to_in_ref[:, part] = (gate * slope).astype(bf16)
            to_gate_ref[:, part] = gelu.astype(bf16)

    out = like((x.shape[0], hidden))
    return call(
        kernel,
        "expand",
        (2,),
        [by_rows(x, 2), whole(up), whole(gate)],
        [by_rows(out, 2)] * 3,
        [out] * 3,
    )(x, up, gate)


def lower_call(hidden, w, middle):
    rows, width = middle.shape

    def kernel(hid_ref, w_ref, mid_ref, own_ref, oth_ref):
        total = dot_nn(hid_ref[...], w_ref[...].reshape(-1, width))

        @pl.when(pl.program_id(0) == 1)
        def _():
            own_ref[...] = mid_ref[...] + total

        @pl.when(pl.program_id(0) == 0)
        def _():
            oth_ref[...] = total.astype(bf16)

    first = pl.BlockSpec((rows // 2, width), lambda i: (0, 0))
    return call(
        kernel,
        "contract",
        (2,),
        [pl.BlockSpec((rows // 2, hidden.shape[1]), lambda i: (1 - i, 0)), whole(w), first],
        [first, first],
        [like((rows // 2, width), f32), like((rows // 2, width))],
    )(hidden, w, middle)


def output_call(own, got, index):
    def kernel(index_ref, own_ref, got_ref, out_ref):
        out_ref[...] = (pick(own_ref, index_ref) + pick(got_ref, index_ref).astype(f32)).astype(bf16)

    tile = by_rows(own, 2)
    return call(kernel, "layer_output", (2,), [scalars, tile, tile], tile, like(own.shape))(
        index, own, got
    )


def weight_gradient_call(lefts, right, blocks, split, extra=None, groups=1):
    flat = lefts[0].ndim == 2
    columns = lefts[0].shape[1] // blocks if flat else sum(a.shape[2] for a in lefts[::groups])
    more = [] if extra is None else [extra]
    lead = sum(e.shape[0] for e in more)
    height = lead + columns
    width = right.shape[1]
    half = blocks // 2

    def kernel(*refs):
        left_refs = refs[: len(lefts)]
        right_ref = refs[len(lefts)]
        extra_refs = refs[len(lefts) + 1 : len(lefts) + 1 + len(more)]
        outs = refs[len(lefts) + 1 + len(more) :]
        left = left_refs[0][...] if flat else lanes_of(paired(left_refs, groups))

        def put(ref, place, values, part):
            ref[place, lead:] = values
            for e in extra_refs:
                ref[place, :lead] = e[:, part]

        for start in range(0, width, 512):
            grads = dot_tn(left, right_ref[:, start : start + 512]).astype(bf16)
            for z in range(blocks):
                block = grads[z * columns : (z + 1) * columns]
                if not split:
                    put(outs[0], (z, slice(start, start + 512)), block, None)
                    continue
                mine, x_rest, y_rest, to_x, to_y = outs
                for j in range(start // 256, start // 256 + 2):
                    part = slice(256 * j, 256 * j + 256)
                    values = block[:, 256 * j - start : 256 * j - start + 256]
                    if j == 0:
                        put(mine, z, values, part)
                    elif j == 1:
                        put(*((to_x, half + z) if z < half else (x_rest, z - half)), values, part)
                    elif j == 2:
                        put(*((y_rest, z) if z < half else (to_y, z)), values, part)
                    else:
                        put(*((to_x, z) if z < half else (to_y, z - half)), values, part)

    if split:
        out_shape = [like((n, height, width // 4)) for n in (blocks, half, half, blocks, blocks)]
    else:
        out_shape = [like((blocks, height, width))]

        def kernel(*refs):
            left_refs = refs[: len(lefts)]
            right_ref, out_ref = refs[len(lefts)], refs[-1]
            left = left_refs[0][...] if flat else lanes_of(paired(left_refs, groups))
            grads = dot_tn(left, right_ref[...]).astype(bf16)
            for z in range(blocks):
                out_ref[z, lead:] = grads[z * columns : (z + 1) * columns]
                if more:
                    out_ref[z, :lead] = refs[len(lefts) + 1][...]

    return call(
        kernel,
        "weight_gradient",
        (1,),
        [whole(a) for a in (*lefts, right, *more)],
        [whole(o) for o in out_shape],
        [kept(o) for o in out_shape],
    )(*lefts, right, *more)


def combine_call(first, second, x_got, y_got, near_rows):
    operands, out_shape = [], []
    if first is not None:
        operands += first[1:]
        out_shape += [like(first[1].shape)] * 2
    if second is not None:
        operands += second
        out_shape += [like(second[0].shape)]

    def kernel(*refs):
        ins, outs = list(refs[2 : 2 + len(operands)]), list(refs[2 + len(operands) :])
        x_ref, y_ref = refs[:2]
        if first is not None:
            x_rest, y_rest, x_out, y_out = ins.pop(0), ins.pop(0), outs.pop(0), outs.pop(0)
            half, rows = x_rest.shape[:2]
            for j in range(half):
                part = slice(j * rows, (j + 1) * rows)
                x_out[j] = (x_rest[j].astype(f32) + y_ref[part].astype(f32)).astype(bf16)
                y_out[j] = (y_rest[j].astype(f32) + x_ref[part].astype(f32)).astype(bf16)
        if second is not None:
            mine, x_near, y_near = ins
            half, rows = mine.shape[0] // 2, mine.shape[1]
            for j in range(half):
                near = slice((half + j) * rows, (half + j + 1) * rows)
                far = slice(near_rows + j * rows, near_rows + (j + 1) * rows)
                for place, near_ref, far_ref in ((j, x_near, y_ref), (half + j, y_near, x_ref)):
                    total = mine[place].astype(f32) + near_ref[near].astype(f32)
                    outs[0][place] = (total + far_ref[far].astype(f32)).astype(bf16)

    results = call(
        kernel,
        "gradient_sums",
        (1,),
        [whole(a) for a in (x_got, y_got, *operands)],
        [whole(o) for o in out_shape],
        out_shape,
    )(x_got, y_got, *operands)
    near = results[:2] if first is not None else None
    return near, results[-1] if second is not None else None


def hidden_back_call(dy, w, to_in, to_gate):
    hidden = to_in.shape[1]

    def kernel(dy_ref, w_ref, to_in_ref, to_gate_ref, in_ref, gate_ref):
        w = w_ref[...].reshape(hidden, -1)
        for start in range(0, hidden, 512):
            part = slice(start, min(start + 512, hidden))
            grad = dot_nt(dy_ref[...], w[part])
            in_ref[:, part] = (grad * to_in_ref[:, part].astype(f32)).astype(bf16)
            gate_ref[:, part] = (grad * to_gate_ref[:, part].astype(f32)).astype(bf16)

    tile = by_rows(to_in, 2)
    return call(
        kernel,
        "grad_lifted",
        (2,),
        [by_rows(dy, 2), whole(w), tile, tile],
        [tile, tile],
        [like(to_in.shape)] * 2,
    )(dy, w, to_in, to_gate)


def two_part_call(grad_in, grad_gate, up, gate):
    width = up.shape[2]

    def kernel(in_ref, gate_ref, up_ref, w_gate_ref, out_ref):
        total = dot_nn(in_ref[...], up_ref[...].reshape(-1, width))
        total += dot_nn(gate_ref[...], w_gate_ref[...].reshape(-1, width))
        out_ref[...] = total.astype(bf16)

    out = like((grad_in.shape[0], width))
    return call(
        kernel,
        "grad_normed_two",
        (2,),
        [by_rows(grad_in, 2), by_rows(grad_gate, 2), whole(up), whole(gate)],
        by_rows(out, 2),
        out,
    )(grad_in, grad_gate, up, gate)


def two_back_call(part, got, middle, dy, gains):
    rows, width = middle.shape

    def kernel(part_ref, got_ref, mid_ref, dy_ref, gain_ref, grad_ref, low_ref, gain_grad_ref):
        i = pl.program_id(0)
        grads = part_ref[...].astype(f32) + got_ref[...].astype(f32)
        back, gain_grad = unnormalize(grads, mid_ref[...], gain_ref[1:2, :])
        grad = dy_ref[...].astype(f32) + back
        low_ref[...] = grad.astype(bf16)

        @pl.when(i == 0)
        def _():
            gain_grad_ref[...] = jnp.zeros_like(gain_grad_ref)

        @pl.when(i < 2)
        def _():
            grad_ref[...] = grad
            gain_grad_ref[...] += jnp.broadcast_to(gain_grad, gain_grad_ref.shape)

    tile = by_rows(middle, 4)
    row = like((8, width), f32)
    return call(
        kernel,
        "second_norm_gradient",
        (4,),
        [tile, swapped_rows(got), tile, tile, whole(gains)],
        [
            pl.BlockSpec((rows // 4, width), lambda i: (jnp.minimum(i, 1), 0)),
            tile,
            whole(row),
        ],
        [like((rows // 2, width), f32), like(middle.shape), row],
    )(part, got, middle, dy, gains)


def att_grad_call(grad, w, start):
    blocks = w.shape[0]
    columns = w.shape[1] - start

    def kernel(g_ref, w_ref, out_ref):
        out = dot_nt(g_ref[...], rows_of(w_ref, start, w_ref.shape[1])).astype(bf16)
        for z in range(blocks):
            out_ref[z] = out[:, z * columns : (z + 1) * columns]

    out = like((blocks, grad.shape[0], columns))
    return call(
        kernel,
        "grad_attended",
        (2,),
        [by_rows(grad, 2), whole(w)],
        blocks_by_rows(out, 2),
        out,
    )(grad, w)


def one_part_call(queries, keys_values, w, start):
    rows, width = queries[0].shape[1], w.shape[2]
    count = len(queries)

    def kernel(*refs):
        *left_refs, w_ref, own_ref, oth_ref = refs
        total = dot_nn(lanes_of(paired(left_refs, count)), rows_of(w_ref, start, start + 384))

        @pl.when(pl.program_id(0) == 1)
        def _():
            own_ref[...] = total

        @pl.when(pl.program_id(0) == 0)
        def _():
            oth_ref[...] = total.astype(bf16)

    def half(array):
        shape = (array.shape[0], rows // 2, array.shape[2])
        return pl.BlockSpec(shape, lambda i: (0, 1 - i, 0))

    first = pl.BlockSpec((rows // 2, width), lambda i: (0, 0))
    return call(
        kernel,
        "grad_normed_one",
        (2,),
        [half(a) for a in (*queries, *keys_values)] + [whole(w)],
        [first, first],
        [like((rows // 2, width), f32), like((rows // 2, width))],
    )(*in_hbm(*queries, *keys_values, w))


def one_back_call(own, got, x, grad_middle, gains, gain_two, index):
    rows, width = own.shape

    def kernel(
        index_ref, own_ref, got_ref, x_ref, mid_ref, gain_ref, gain_two_ref, grad_ref, gain_grad_ref,
        total_ref, low_ref,
    ):
        i = pl.program_id(0)
        grads = own_ref[...] + got_ref[...].astype(f32)
        back, gain_grad = unnormalize(grads, x_ref[...].astype(f32), gain_ref[0:1, :])
        low_ref[...] = (mid_ref[...] + back).astype(bf16)
        grad_ref[...] = pick(low_ref, index_ref)

        @pl.when(i == 0)
        def _():
            total_ref[...] = gain_grad

        @pl.when(i == 1)
        def _():
            total = total_ref[...] + gain_grad
            row = lax.broadcasted_iota(jnp.int32, gain_grad_ref.shape, 0)
            both = jnp.where(row == 0, total, jnp.where(row == 1, gain_two_ref[0:1, :], 0.0))
            gain_grad_ref[...] = both.astype(bf16)

    tile = by_rows(own, 2)
    x_tile = pl.BlockSpec((rows // 2, width), lambda i: (i, 0))
    gain_grads = like((16, width))
    return call(
        kernel,
        "first_norm_gradient",
        (2,),
        [scalars, tile, tile, x_tile, tile, whole(gains), whole(gain_two)],
        [tile, whole(gain_grads)],
        [like(own.shape), gain_grads],
        [pltpu.VMEM((1, width), f32), pltpu.VMEM((rows // 2, width), bf16)],
    )(index, own, got, x, grad_middle, gains, gain_two)


(
    X_IN,
    COT,
    BOTH,
    LOW,
    COLUMN,
    W,
    NEAR,
    GRAD,
    PAIR,
    TABLES,
    REST,
    X_OWN,
    GAINS,
    X,
    NORMED,
    QKV,
    ATT,
    LSE,
    Y1,
    PART,
    Y_OWN,
    MIDDLE,
    NORMED_TWO,
    HIDDEN,
    TO_IN,
    TO_GATE,
    DY,
    G,
    F,
    N,
    SUM,
    G_GATE,
    OUT,
    DQ,
    DKV,
    G_ATT,
    GRAD_MID,
    MID_LOW,
    GAIN_TWO,
    OUT1,
    OWN,
    OTHER,
    OUT0,
    DX,
    DX0,
    DX1,
    OUTPUTS,
    INPUT_GRADS,
    UPDATED,
) = range(49)


def make_per_device(dp, tensor):
    count = dp * tensor
    chips = dp // 2
    chip_bits = chips.bit_length() - 1
    square = chip_bits == 2
    half = tensor // 2

    def permute(value, pairs):
        return lax.ppermute(value, AXES, pairs)

    def exchange(value, mask):
        return permute(value, [(i, i ^ mask) for i in range(count)])

    def over_chip(value, bit):
        return exchange(value, (2 * tensor) << bit)

    def over_core(value, pieces=1):
        rows = value.shape[0] // pieces
        got = [exchange(value[i * rows : (i + 1) * rows], tensor) for i in range(pieces)]
        return got[0] if pieces == 1 else jnp.concatenate(got, axis=0)

    def spread_pairs(r):
        pairs = []
        for i in range(count):
            z = i % tensor
            core = (i // tensor) % 2
            chip = i // (2 * tensor)
            pairs.append((i, (chip * 2 + z % 2) * tensor + (r ^ (z // 2)) * 2 + core))
        return pairs

    def by_column(blocks, me_z):
        for bit in range(tensor.bit_length() - 1):
            odd = (me_z >> bit) % 2 == 1
            blocks = [jnp.where(odd, blocks[k ^ (1 << bit)], blocks[k]) for k in range(tensor)]
        return blocks

    inner = [(i, i ^ 3) for i in range(count) if i % tensor in (1, 2)]
    outward = [(i, i ^ 1) for i in range(count) if i % tensor in (1, 2)]

    def gather_near_z(rows, me_z):
        got = exchange(rows, 1)
        low = me_z % 2 == 0
        return jnp.stack([jnp.where(low, rows, got), jnp.where(low, got, rows)])

    def gather_far_z(pair, got, me_z):
        sent = permute(got, outward)
        other = jnp.where((me_z == 0) | (me_z == 3), sent, got)
        low = me_z < 2
        return jnp.concatenate([jnp.where(low, pair, other), jnp.where(low, other, pair)], axis=0)

    def gather_plane(columns):
        current = columns[None]
        for bit in range(chip_bits):
            current = jnp.concatenate([current, over_chip(current, bit)], axis=0)
        return current.transpose(1, 2, 0, 3).reshape(columns.shape[:2] + (-1,))

    def low_sum(*values):
        return sum(v.astype(f32) for v in values).astype(bf16)

    def reduce_plane(parts):
        current = parts
        for bit in reversed(range(chip_bits)):
            middle = current.shape[0] // 2
            current = low_sum(current[:middle], over_chip(current[middle:], bit))
        return current[0]

    def reduce_column(blocks):
        result = blocks[0].astype(f32)
        for k in range(1, tensor):
            result = result + exchange(blocks[k], k).astype(f32)
        return result

    def per_device(
        inputs,
        cotangent,
        attention_in,
        attention_out,
        expand_weight,
        contract_weight,
        norm_gains,
        attention_in_first,
        attention_in_second,
        attention_out_first,
        attention_out_second,
        expand_first,
        expand_second,
        contract_first,
        contract_second,
        gains_first,
        gains_second,
    ):
        block = attention_in.shape[0]
        head_columns = attention_in.shape[2]
        hidden_local = expand_weight.shape[2]
        local_rows = inputs.shape[2]
        me_dp = lax.axis_index("dp")
        me_z = lax.axis_index("tensor")
        core = me_dp % 2
        z_high = me_z // 2

        me_chip = me_dp // 2
        index = me_chip ^ jnp.arange(chips, dtype=jnp.int32)
        aligned = block % 128 == 0
        kernel_index = index if aligned else jnp.zeros((1,), jnp.int32)

        def outside(values):
            if aligned:
                return values
            shaped = values.reshape(values.shape[0], chips, 2 * block)
            return jnp.take(shaped, index, axis=1).reshape(values.shape)

        def spread(values, r):
            part = lax.dynamic_index_in_dim(values[:, 0], r ^ z_high, 0, keepdims=False)
            return permute(part, spread_pairs(r))

        def collect(values, r):
            part = values[r * local_rows : (r + 1) * local_rows]
            return permute(part, [(b, a) for a, b in spread_pairs(r)])

        def assemble(first, second):
            odd = z_high == 1
            return jnp.stack([jnp.where(odd, second, first), jnp.where(odd, first, second)])[:, None]

        def rotary_tables():
            row_starts = [
                ((r ^ z_high) * 2 + (core ^ c)) * local_rows for c in range(2) for r in range(2)
            ]
            positions = jnp.concatenate([s + jnp.arange(local_rows) for s in row_starts]).astype(f32)
            exponents = jnp.arange(0, DH, 2).astype(f32) / DH
            angles = positions[:, None] * jnp.power(rope_theta, -exponents)[None, :]
            cosine, sine = jnp.cos(angles), jnp.sin(angles)
            cosine = jnp.concatenate([cosine] * 4, axis=-1)
            sine = jnp.concatenate([-sine, sine] * 2, axis=-1)
            return cosine, sine

        cut = (hidden_local // 2 + 15) // 16 * 16
        spare = 2 * cut - hidden_local
        head_cut = head_columns // 2
        low_in = attention_in.astype(bf16).reshape(block, 3, 2, head_cut).transpose(2, 1, 3, 0)
        low_out = attention_out.astype(bf16).reshape(block, 2, head_cut).transpose(1, 2, 0)
        low_expand = jnp.pad(expand_weight.astype(bf16).transpose(1, 2, 0), ((0, 0), (0, spare), (0, 0)))
        low_expand = low_expand.reshape(2, 2, cut, block).transpose(1, 0, 2, 3)
        low_contract = jnp.pad(contract_weight.astype(bf16).T, ((0, spare), (0, 0)))
        low_contract = low_contract.reshape(2, cut, block)
        low_gains = jnp.pad(norm_gains.astype(bf16), ((0, 14), (0, 0)))
        lead = low_gains.shape[0]
        both = jnp.concatenate(
            [
                jnp.stack([low_gains, low_gains]),
                low_in.reshape(2, -1, block),
                low_out,
                low_expand.reshape(2, -1, block),
                low_contract,
            ],
            axis=1,
        )
        out_start = lead + 3 * head_cut
        sizes = [out_start + head_cut, cut, cut, cut]
        starts = [sum(sizes[:k]) for k in range(len(sizes) + 1)]
        last = len(sizes)
        first_core = core == 0

        def side_by_side(mine, got):
            return jnp.concatenate(
                [jnp.where(first_core, mine, got), jnp.where(first_core, got, mine)], axis=-1
            )

        state = {X_IN: inputs, COT: cotangent, BOTH: both}
        held = []
        again = []

        def run(work):
            nonlocal state
            new = {}
            late = held[:]
            held[:] = again
            again.clear()
            work(state, new)
            for values in late:
                new.update(values)
            state.update(new)
            names = list(state)
            state = dict(zip(names, lax.optimization_barrier([state[n] for n in names])))

        def column_direct(s, new, k):
            rows = s[LOW][starts[k] : starts[k + 1]]
            blocks = [rows] + [exchange(rows, j) for j in range(1, tensor)]
            new[COLUMN, k] = jnp.stack(by_column(blocks, me_z))

        def plane(s, new, k):
            if not square:
                if k < last:
                    new[W, k] = gather_plane(s.pop((COLUMN, k)))
                return
            sends, first_rows = ([], []), 0
            if k < last:
                column = s[COLUMN, k]
                first_rows = column.shape[0] * column.shape[1]
                for way in range(2):
                    sends[way].append(column.reshape(first_rows, -1))
            if k > 0:
                got = s[NEAR, k - 1]
                rows = half * sizes[k - 1]
                sends[0].append(got[1][rows : 2 * rows])
                sends[1].append(got[0][:rows])
            got = tuple(over_chip(jnp.concatenate(sends[way], axis=0), way) for way in range(2))
            if k < last:
                new[NEAR, k] = got
            if k > 0:
                new[W, k - 1] = weave_call(
                    s.pop((COLUMN, k - 1)), *s.pop((NEAR, k - 1)), *got, first_rows
                )

        step_rates = (
            2.5 * D ** (-0.5),
            2.5 * max(1, 4 * H * DH // SEQ) ** (-0.5),
            2.5 * D ** (-0.5),
            2.5 * FF ** (-0.5),
            0.25,
        )

        def joined(s, k, rows):
            return jnp.concatenate(s[GRAD, k], axis=0)[:rows]

        def joined_heads(s):
            parts = [g[lead:].reshape(3, head_cut, block) for g in s[GRAD, 4]]
            return lax.optimization_barrier(jnp.concatenate(parts, axis=1).transpose(2, 0, 1))

        def first_updates(s):
            grad_out, grad_down = lax.optimization_barrier(
                (joined(s, 3, head_columns).T, joined(s, 0, hidden_local).T)
            )
            return (
                adamw_update(
                    attention_out, attention_out_first, attention_out_second, grad_out, step_rates[1]
                ),
                adamw_update(
                    contract_weight, contract_first, contract_second, grad_down, step_rates[3]
                ),
            )

        def f0(s, new):
            pair = s.pop(BOTH)
            mine = jnp.where(first_core, pair[0], pair[1])
            got = over_core(jnp.where(first_core, pair[1], pair[0]))
            new[LOW] = side_by_side(mine, got)

        run(f0)

        def f1(s, new):
            column_direct(s, new, 0)
            new[PAIR] = gather_near_z(s[LOW][starts[1] :], me_z)
            new[TABLES] = rotary_tables()

        run(f1)

        def f2(s, new):
            plane(s, new, 0)
            pair = s.pop(PAIR)
            up, rest = pair[:, :cut], pair[:, cut:]
            new[COLUMN, 1] = gather_far_z(up, permute(up, inner), me_z)
            new[REST] = (rest, permute(rest, inner))

        run(f2)

        def f3(s, new):
            plane(s, new, 1)
            rest = gather_far_z(*s.pop(REST), me_z)
            new[COLUMN, 2], new[COLUMN, 3] = rest[:, :cut], rest[:, cut:]
            new[X_OWN] = jnp.concatenate([spread(s[X_IN], 0), spread(s.pop(X_IN), 1)], axis=0)

        run(f3)

        def f4(s, new):
            plane(s, new, 2)
            rows = s.pop(X_OWN)
            x_raw = jnp.concatenate([rows, over_core(rows, 2)], axis=0)
            new[GAINS] = s[W, 0][0, :lead].astype(f32)
            new[X], new[NORMED] = norm_call(outside(x_raw), new[GAINS], kernel_index)
            query, key, value = qkv_call(new[NORMED], s[W, 0], lead, *s[TABLES])
            new[QKV] = (query, key, value)
            new[ATT, 0], new[LSE, 0] = attend_call(query, key, value, 0, tensor // 2)
            new[Y1] = spread(s[COT], 1)

        run(f4)

        def f5(s, new):
            plane(s, new, 3)
            new[ATT, 1], new[LSE, 1] = attend_call(*s[QKV], tensor // 2, tensor // 2)
            new[PART] = attention_output_call((s[ATT, 0], new[ATT, 1]), s[W, 0], out_start)
            new[Y_OWN] = jnp.concatenate([spread(s.pop(COT), 0), s.pop(Y1)], axis=0)

        run(f5)

        def f6(s, new):
            plane(s, new, 4)
            part, rows = s.pop(PART), s.pop(Y_OWN)
            new[MIDDLE], new[NORMED_TWO] = middle_call(
                s[X], part, over_core(part, 4), s[GAINS]
            )
            new[HIDDEN], new[TO_IN], new[TO_GATE] = lift_call(
                new[NORMED_TWO], s[W, 1], s[W, 2]
            )
            y_raw = jnp.concatenate([rows, over_core(rows)], axis=0)
            new[DY] = order_call(outside(y_raw), kernel_index)
            made(new, 0, [new[HIDDEN]], new[DY])

        def made(new, k, lefts, right, extra=None, groups=1):
            split = square and aligned
            grads = weight_gradient_call(lefts, right, tensor, split, extra, groups)
            if not split:
                (full,) = grads
                grads = full.reshape(full.shape[:2] + (chips, -1)).transpose(2, 0, 1, 3)
            new[G, k] = grads

        def plane_back(s, new, k):
            if not square:
                if (G, k) in s:
                    new[F, k] = [b for b in reduce_plane(s.pop((G, k)))]
                return
            flat = lambda a: a.reshape(-1, a.shape[-1])
            to_x, to_y, rows = [], [], 0
            if (G, k) in s:
                mine, x_rest, y_rest, x_out, y_out = s.pop((G, k))
                rows = x_out.shape[0] * x_out.shape[1]
                to_x.append(flat(x_out))
                to_y.append(flat(y_out))
            if (N, k - 1) in s:
                x_last, y_last, mine_last, x_near, y_near = s.pop((N, k - 1))
                to_x.append(flat(x_last))
                to_y.append(flat(y_last))
            x_got = over_chip(jnp.concatenate(to_x, axis=0), 0)
            y_got = over_chip(jnp.concatenate(to_y, axis=0), 1)
            first = (mine, x_rest, y_rest) if rows else None
            second = (mine_last, x_near, y_near) if len(to_x) > 1 or not rows else None
            near, far = combine_call(first, second, x_got, y_got, rows)
            if first is not None:
                new[N, k] = (*near, mine, x_got, y_got)
            if second is not None:
                new[F, k - 1] = far

        def whole_blocks(blocks):
            return blocks if square else jnp.stack(blocks)

        def scatter(s, k):
            total = lax.psum_scatter(
                whole_blocks(s.pop((F, k))), "tensor", scatter_dimension=0, tiled=False
            )
            held.append({(SUM, k): total})

        def column(s, new, *chunks):
            blocks = [by_column(s.pop((F, k)), me_z) for k in chunks]
            total = reduce_column([jnp.concatenate(b, axis=0) for b in zip(*blocks)])
            start = 0
            for k, b in zip(chunks, blocks):
                new[SUM, k] = total[start : start + b[0].shape[0]].astype(bf16)
                start += b[0].shape[0]

        def trade(s, new, *chunks):
            sums = [s.pop((SUM, k)) for k in chunks]
            total = jnp.concatenate(sums, axis=0)
            mine = jnp.where(first_core, total[:, :block], total[:, block:])
            got = over_core(jnp.where(first_core, total[:, block:], total[:, :block]))
            start = 0
            for k, rows in zip(chunks, [a.shape[0] for a in sums]):
                a, b = mine[start : start + rows], got[start : start + rows]
                new[GRAD, k] = (
                    jnp.where(first_core, a, b).astype(f32),
                    jnp.where(first_core, b, a).astype(f32),
                )
                start += rows

        run(f6)

        def s1(s, new):
            plane_back(s, new, 0)
            own, other = lower_call(s.pop(HIDDEN), s[W, 3], s[MIDDLE])
            g_in, g_gate = hidden_back_call(
                s[DY], s.pop((W, 3)), s.pop(TO_IN), s.pop(TO_GATE)
            )
            new[G_GATE] = g_gate
            new[PART] = two_part_call(g_in, g_gate, s.pop((W, 1)), s.pop((W, 2)))
            made(new, 1, [g_in], s[NORMED_TWO])
            new[OUT] = outside(output_call(own, over_core(other), kernel_index))

        run(s1)

        def attention_back(s, new, p):
            new[DQ, p], new[DKV, p] = attend_back_call(
                *s[QKV], s[G_ATT], s[ATT, p], s.pop((LSE, p)), *s[TABLES],
                p * (tensor // 2), tensor // 2,
            )

        def s2(s, new):
            plane_back(s, new, 1)
            part = s.pop(PART)
            new[GRAD_MID], new[MID_LOW], new[GAIN_TWO] = two_back_call(
                part, over_core(part, 4), s.pop(MIDDLE), s.pop(DY), s[GAINS]
            )
            made(new, 2, [s.pop(G_GATE)], s.pop(NORMED_TWO))
            s[G_ATT] = new[G_ATT] = att_grad_call(new[MID_LOW], s[W, 0], out_start)
            attention_back(s, new, 0)
            new[OUT1] = collect(s[OUT], 1)

        run(s2)

        def s3(s, new):
            scatter(s, 0)
            plane_back(s, new, 2)
            attention_back(s, new, 1)
            made(new, 3, [s[ATT, 0], s[ATT, 1]], s[MID_LOW], None, 2)
            new[OWN], new[OTHER] = one_part_call(
                (s[DQ, 0], new[DQ, 1]), (s[DKV, 0], new[DKV, 1]), s[W, 0], lead
            )
            new[OUT0] = collect(s[OUT], 0)

        run(s3)

        def s4(s, new):
            scatter(s, 1)
            plane_back(s, new, 3)
            dx, gain_grads = one_back_call(
                s.pop(OWN), over_core(s.pop(OTHER), 2), s.pop(X), s.pop(GRAD_MID),
                s[GAINS], s.pop(GAIN_TWO), kernel_index,
            )
            new[DX] = outside(dx)
            lefts = [s[DQ, 0], s[DQ, 1], s[DKV, 0], s[DKV, 1]]
            made(new, 4, lefts, s[NORMED], gain_grads, 2)
            new[DX0] = collect(new[DX], 0)

        run(s4)

        def s5(s, new):
            plane_back(s, new, 4)
            new[DX1] = collect(s[DX], 1)
            new[OUTPUTS] = assemble(s.pop(OUT0), s.pop(OUT1))

        run(s5)

        def s6(s, new):
            scatter(s, 2)
            plane_back(s, new, 5)
            column(s, new, 3)
            new[INPUT_GRADS] = assemble(s.pop(DX0), s.pop(DX1))

        run(s6)

        def s7(s, new):
            column(s, new, 4)
            trade(s, new, 0, 1, 3)

        run(s7)

        def s8(s, new):
            trade(s, new, 2, 4)
            new[UPDATED] = first_updates(s)

        run(s8)

        layer_output, input_gradient = state[OUTPUTS], state[INPUT_GRADS]
        grad_qkv = joined_heads(state)
        gain_total = sum(g[:2] for g in state[GRAD, 4])
        qkv_new = adamw_update(
            attention_in, attention_in_first, attention_in_second, grad_qkv, step_rates[0]
        )
        gains_new = adamw_update(norm_gains, gains_first, gains_second, gain_total, step_rates[4])
        out_new, contract_new = state[UPDATED]
        grad_expand = jnp.stack([joined(state, k, hidden_local) for k in (1, 2)]).transpose(2, 0, 1)
        grad_expand = lax.optimization_barrier(grad_expand)
        expand_new = adamw_update(
            expand_weight, expand_first, expand_second, grad_expand, step_rates[2]
        )
        return (
            layer_output,
            input_gradient,
            *qkv_new,
            *out_new,
            *expand_new,
            *contract_new,
            *gains_new,
        )

    return per_device


def solution(mesh):
    activation = P(None, "dp", "tensor", None)
    cube = P("dp", None, "tensor")
    flat = P("dp", "tensor")
    gain = P(None, "dp")
    return jax.shard_map(
        make_per_device(mesh.shape["dp"], mesh.shape["tensor"]),
        mesh=mesh,
        in_specs=(
            activation, activation, cube, flat, cube, flat, gain,
            cube, cube, flat, flat, cube, cube, flat, flat, gain, gain,
        ),
        out_specs=(
            activation, activation, cube, cube, cube, flat, flat, flat,
            cube, cube, cube, flat, flat, flat, gain, gain, gain,
        ),
        check_vma=False,
    )
```

```python
import jax
import jax.numpy as jnp
from jax import lax
from jax.experimental import pallas as pl
from jax.experimental.pallas import tpu as pltpu
from jax.sharding import PartitionSpec as P

D = 1024
H = 16
DH = 64
FF = 2624
SEQ = 1024
STEP = 10

epsilon_norm = 1e-05
rope_theta = 160000.0
beta_first = 0.9
beta_second = 0.98
epsilon_adam = 1e-06
weight_decay = 1e-05

AXES = ("dp", "tensor")
bf16 = jnp.bfloat16
f32 = jnp.float32


def dot_nt(left, right):
    return lax.dot_general(left, right, (((1,), (1,)), ((), ())), preferred_element_type=f32)


def dot_tn(left, right):
    return lax.dot_general(left, right, (((0,), (0,)), ((), ())), preferred_element_type=f32)


def dot_nn(left, right):
    return jnp.dot(left, right, preferred_element_type=f32)


def adamw_update(weight, first_moment, second_moment, gradient, step_rate):
    first_new = beta_first * first_moment + (1.0 - beta_first) * gradient
    second_new = beta_second * second_moment + (1.0 - beta_second) * gradient * gradient
    first_hat = first_new / (1.0 - beta_first**STEP)
    second_hat = second_new / (1.0 - beta_second**STEP)
    weight_new = weight - step_rate * (
        first_hat / (jnp.sqrt(second_hat) + epsilon_adam) + weight_decay * weight
    )
    return (weight_new, first_new, second_new)


def whole(array):
    return pl.BlockSpec(
        array.shape, lambda i, rank=array.ndim: (0,) * rank, pipeline_mode=pl.Buffered(1)
    )


def by_block(array):
    return pl.BlockSpec((1,) + array.shape[1:], lambda z: (z, 0, 0))


def by_rows(array, steps):
    return pl.BlockSpec((array.shape[0] // steps, array.shape[1]), lambda i: (i, 0))


def like(shape, dtype=bf16):
    return jax.ShapeDtypeStruct(shape, dtype)


def kept(array):
    return pltpu.HBM(array.shape, array.dtype)


microseconds = dict(
    feature_order=3.0,
    gathered_weight=3.0,
    gradient_sums=3.0,
    first_norm=4.0,
    qkv_projection=6.0,
    attention_forward=9.0,
    attention_output=2.5,
    second_norm=4.0,
    expand=12.0,
    contract=5.0,
    layer_output=2.0,
    weight_gradient=5.0,
    grad_lifted=6.0,
    grad_normed_two=8.0,
    second_norm_gradient=5.0,
    grad_attended=2.5,
    attention_backward=14.0,
    grad_normed_one=6.0,
    first_norm_gradient=3.0,
)


def cost(name):
    return pl.CostEstimate(
        flops=int(microseconds[name] * 0.35e9),
        bytes_accessed=int(microseconds[name] * 1.2e6),
        transcendentals=0,
    )


def call(kernel, name, grid, in_specs, out_specs, out_shape, scratch=()):
    return pl.pallas_call(
        kernel,
        grid=grid,
        in_specs=in_specs,
        out_specs=out_specs,
        out_shape=out_shape,
        scratch_shapes=list(scratch),
        compiler_params=pltpu.CompilerParams(vmem_limit_bytes=20 << 20),
        cost_estimate=cost(name),
        name=name,
    )


def swap_halves(values):
    lane = lax.broadcasted_iota(jnp.int32, values.shape, 1)
    return jnp.where(
        lane % DH < DH // 2,
        pltpu.roll(values, values.shape[1] - DH // 2, 1),
        pltpu.roll(values, DH // 2, 1),
    )


def normalize(values):
    centered = values - jnp.mean(values, axis=1, keepdims=True)
    scale = lax.rsqrt(jnp.mean(centered * centered, axis=1, keepdims=True) + epsilon_norm)
    return centered * scale, scale


def unnormalize(grads, values, gain):
    hats, scale = normalize(values)
    gain_grad = jnp.sum(grads * hats, axis=0, keepdims=True)
    errors = grads * gain
    average = jnp.mean(errors, axis=1, keepdims=True)
    along = jnp.mean(errors * hats, axis=1, keepdims=True)
    return scale * (errors - average - hats * along), gain_grad


def pick(ref, index_ref):
    count = index_ref.shape[0]
    if count == 1:
        return ref[...]
    block = ref.shape[1] // count
    parts = [ref[:, pl.ds(pl.multiple_of(index_ref[j] * block, block), block)] for j in range(count)]
    return jnp.concatenate(parts, axis=1)


def in_hbm(*arrays):
    return tuple(pltpu.with_memory_space_constraint(a, pltpu.HBM) for a in arrays)


scalars = pl.BlockSpec(memory_space=pltpu.SMEM)


def order_call(values, index):
    def kernel(index_ref, in_ref, out_ref):
        out_ref[...] = pick(in_ref, index_ref)

    tile = by_rows(values, 2)
    return call(
        kernel, "feature_order", (2,), [scalars, tile], tile, like(values.shape, values.dtype)
    )(index, values)


def norm_call(x, gains, index):
    def kernel(index_ref, x_ref, gain_ref, x_out_ref, out_ref):
        values = pick(x_ref, index_ref)
        x_out_ref[...] = values
        hats, _ = normalize(values.astype(f32))
        out_ref[...] = (hats * gain_ref[0:1, :]).astype(bf16)

    tile = by_rows(x, 4)
    return call(
        kernel, "first_norm", (4,), [scalars, tile, whole(gains)], [tile] * 2, [like(x.shape)] * 2
    )(index, x, gains)


def qkv_call(x, w, start, cosine, sine):
    rows, blocks = x.shape[0], w.shape[0]

    def kernel(x_ref, w_ref, cos_ref, sin_ref, q_ref, k_ref, v_ref):
        mixed = dot_nt(x_ref[...], w_ref[0, start : start + 384])
        cosine, sine = cos_ref[...], sin_ref[...]
        query, key = mixed[:, :128], mixed[:, 128:256]
        query = query * cosine + swap_halves(query) * sine
        key = key * cosine + swap_halves(key) * sine
        q_ref[0] = query.astype(bf16) * bf16(DH**-0.5)
        k_ref[0] = key.astype(bf16)
        v_ref[0] = mixed[:, 256:].astype(bf16)

    out = like((blocks, rows, 128))
    return call(
        kernel,
        "qkv_projection",
        (blocks,),
        [whole(x), by_block(w), whole(cosine), whole(sine)],
        [by_block(out)] * 3,
        [out] * 3,
    )(x, w, cosine, sine)


def pair_specs(array, first, halves):
    rows = array.shape[1]
    return (
        pl.BlockSpec((1, rows // halves, array.shape[2]), lambda z, i: (first + z, i, 0)),
        pl.BlockSpec((1, rows, array.shape[2]), lambda z, i: (first + z, 0, 0)),
    )


def weave_call(column, x_near, y_near, x_far, y_far, far_rows):
    blocks, rows, width = column.shape
    half = blocks // 2

    def kernel(col_ref, x_ref, y_ref, x_far_ref, y_far_ref, out_ref):
        z = pl.program_id(0)
        out_ref[0, :, :width] = col_ref[0]
        out_ref[0, :, width : 2 * width] = x_ref[...]
        out_ref[0, :, 2 * width : 3 * width] = y_ref[...]
        start = pl.multiple_of(far_rows + z % half * rows, 16)

        @pl.when(z < half)
        def _():
            out_ref[0, :, 3 * width :] = y_far_ref[pl.ds(start, rows), :]

        @pl.when(z >= half)
        def _():
            out_ref[0, :, 3 * width :] = x_far_ref[pl.ds(start, rows), :]

    near = pl.BlockSpec((rows, width), lambda z: (z, 0))
    out = like((blocks, rows, 4 * width))
    return call(
        kernel,
        "gathered_weight",
        (blocks,),
        [by_block(column), near, near, whole(x_far), whole(y_far)],
        by_block(out),
        out,
    )(column, x_near, y_near, x_far, y_far)


def attend_call(query, key, value, first, count):
    rows = query.shape[1]

    def kernel(q_ref, k_ref, v_ref, out_ref, lse_ref):
        query, key = q_ref[0], k_ref[0]
        value_t = v_ref[0].astype(f32).T.astype(bf16)
        lane = lax.broadcasted_iota(jnp.int32, query.shape, 1)
        outs = []
        for head in range(2):
            query_head = jnp.where(lane // DH == head, query, jnp.zeros_like(query))
            scores = dot_nt(key, query_head)
            peak = jnp.max(scores, axis=0, keepdims=True)
            weights = jnp.exp(scores - peak)
            total = jnp.sum(weights, axis=0, keepdims=True)
            out = dot_nn(value_t[head * DH : (head + 1) * DH], weights.astype(bf16))
            outs.append(out / total)
            lse_ref[0, head : head + 1, :] = peak + jnp.log(total)
        out_ref[0] = jnp.concatenate(outs, axis=0).T.astype(bf16)

    half, full = pair_specs(query, first, 2)
    out_half, _ = pair_specs(query, 0, 2)
    lse = pl.BlockSpec((1, 2, rows // 2), lambda z, i: (z, 0, i))
    return call(
        kernel,
        "attention_forward",
        (count, 2),
        [half, full, full],
        [out_half, lse],
        [like((count, rows, 128)), like((count, 2, rows), f32)],
    )(query, key, value)


def attend_back_call(query, key, value, grad, out, lse, cosine, sine, first, count):
    rows = query.shape[1]

    def kernel(
        q_ref, k_ref, v_ref, grad_ref, out_ref, lse_ref, cos_ref, sin_ref, dq_ref, dkv_ref,
        key_total, value_total,
    ):
        step = pl.program_id(1)
        query, key, value, grad = q_ref[0], k_ref[0], v_ref[0], grad_ref[0]
        key_t = key.astype(f32).T.astype(bf16)
        product_t = (grad.astype(f32) * out_ref[0].astype(f32)).T
        lane = lax.broadcasted_iota(jnp.int32, query.shape, 1)
        grad_key = jnp.zeros((rows, 128), f32)
        grad_value = jnp.zeros((rows, 128), f32)
        grad_queries = []
        for head in range(2):
            mine = lane // DH == head
            query_head = jnp.where(mine, query, jnp.zeros_like(query))
            grad_head = jnp.where(mine, grad, jnp.zeros_like(grad))
            delta = jnp.sum(product_t[head * DH : (head + 1) * DH], axis=0, keepdims=True)
            weights = jnp.exp(dot_nt(key, query_head) - lse_ref[0, head : head + 1, :])
            grad_soft = dot_nt(value, grad_head)
            grad_scores = (weights * (grad_soft - delta)).astype(bf16)
            grad_value += dot_nn(weights.astype(bf16), grad_head)
            grad_key += dot_nn(grad_scores, query_head)
            grad_queries.append(dot_nn(key_t[head * DH : (head + 1) * DH], grad_scores))
        half = query.shape[0]
        grad_query = jnp.concatenate(grad_queries, axis=0).T * (DH**-0.5)
        start = pl.multiple_of(step * half, half)
        cosine, sine = cos_ref[pl.ds(start, half), :], sin_ref[pl.ds(start, half), :]
        dq_ref[0] = (grad_query * cosine - swap_halves(grad_query) * sine).astype(bf16)

        @pl.when(step == 0)
        def _():
            key_total[...] = grad_key
            value_total[...] = grad_value

        @pl.when(step == 1)
        def _():
            total = key_total[...] + grad_key
            back = total * cos_ref[...] - swap_halves(total) * sin_ref[...]
            dkv_ref[0, :, :128] = back.astype(bf16)
            dkv_ref[0, :, 128:] = (value_total[...] + grad_value).astype(bf16)

    half, full = pair_specs(query, first, 2)
    out_half, _ = pair_specs(query, 0, 2)
    lse_spec = pl.BlockSpec((1, 2, rows // 2), lambda z, i: (z, 0, i))
    table = pl.BlockSpec(cosine.shape, lambda z, i: (0, 0))
    return call(
        kernel,
        "attention_backward",
        (count, 2),
        [half, full, full, half, out_half, lse_spec, table, table],
        [out_half, pl.BlockSpec((1, rows, 256), lambda z, i: (z, 0, 0))],
        [like((count, rows, 128)), like((count, rows, 256))],
        [pltpu.VMEM((rows, 128), f32)] * 2,
    )(*in_hbm(query, key, value, grad, out, lse, cosine, sine))


def lanes_of(groups):
    return jnp.concatenate([r[j] for g in groups for j in range(g[0].shape[0]) for r in g], axis=1)


def paired(refs, count):
    return [refs[i::count] for i in range(count)]


def blocks_by_rows(array, steps):
    return pl.BlockSpec(
        (array.shape[0], array.shape[1] // steps, array.shape[2]), lambda i: (0, i, 0)
    )


def rows_of(ref, start, stop):
    if start == 0 and stop == ref.shape[1]:
        return ref[...].reshape(-1, ref.shape[2])
    return jnp.concatenate([ref[z, start:stop] for z in range(ref.shape[0])], axis=0)


def attention_output_call(att, w, start):
    rows = att[0].shape[1]

    def kernel(*refs):
        *att_refs, w_ref, out_ref = refs
        att = lanes_of([[r] for r in att_refs])
        out_ref[...] = dot_nn(att, rows_of(w_ref, start, w_ref.shape[1])).astype(bf16)

    out = like((rows, w.shape[2]))
    return call(
        kernel,
        "attention_output",
        (2,),
        [blocks_by_rows(a, 2) for a in att] + [whole(w)],
        by_rows(out, 2),
        out,
    )(*att, w)


def swapped_rows(array):
    return pl.BlockSpec((array.shape[0] // 4, array.shape[1]), lambda i: ((i + 2) % 4, 0))


def middle_call(x, part, got, gains):
    def kernel(x_ref, part_ref, got_ref, gain_ref, mid_ref, out_ref):
        middle = x_ref[...].astype(f32) + (part_ref[...].astype(f32) + got_ref[...].astype(f32))
        mid_ref[...] = middle
        hats, _ = normalize(middle)
        out_ref[...] = (hats * gain_ref[1:2, :]).astype(bf16)

    tile = by_rows(x, 4)
    return call(
        kernel,
        "second_norm",
        (4,),
        [tile, tile, swapped_rows(got), whole(gains)],
        [tile, tile],
        [like(x.shape, f32), like(x.shape)],
    )(x, part, got, gains)


def lift_call(x, up, gate):
    hidden = up.shape[0] * up.shape[1]

    def kernel(x_ref, up_ref, gate_ref, hid_ref, to_in_ref, to_gate_ref):
        x = x_ref[...]
        w_up, w_gate = (r[...].reshape(hidden, -1) for r in (up_ref, gate_ref))
        for start in range(0, hidden, 512):
            part = slice(start, min(start + 512, hidden))
            lifted = dot_nt(x, w_up[part])
            gate = dot_nt(x, w_gate[part])
            phi = 0.5 * (1.0 + lax.erf(lifted * (0.5**0.5)))
            gelu = lifted * phi
            slope = phi + lifted * jnp.exp(-0.5 * lifted * lifted) * 0.3989422804014327
            hid_ref[:, part] = (gelu * gate).astype(bf16)
            to_in_ref[:, part] = (gate * slope).astype(bf16)
            to_gate_ref[:, part] = gelu.astype(bf16)

    out = like((x.shape[0], hidden))
    return call(
        kernel,
        "expand",
        (2,),
        [by_rows(x, 2), whole(up), whole(gate)],
        [by_rows(out, 2)] * 3,
        [out] * 3,
    )(x, up, gate)


def lower_call(hidden, w, middle):
    rows, width = middle.shape

    def kernel(hid_ref, w_ref, mid_ref, own_ref, oth_ref):
        total = dot_nn(hid_ref[...], w_ref[...].reshape(-1, width))

        @pl.when(pl.program_id(0) == 1)
        def _():
            own_ref[...] = mid_ref[...] + total

        @pl.when(pl.program_id(0) == 0)
        def _():
            oth_ref[...] = total.astype(bf16)

    first = pl.BlockSpec((rows // 2, width), lambda i: (0, 0))
    return call(
        kernel,
        "contract",
        (2,),
        [pl.BlockSpec((rows // 2, hidden.shape[1]), lambda i: (1 - i, 0)), whole(w), first],
        [first, first],
        [like((rows // 2, width), f32), like((rows // 2, width))],
    )(hidden, w, middle)


def output_call(own, got, index):
    def kernel(index_ref, own_ref, got_ref, out_ref):
        out_ref[...] = (pick(own_ref, index_ref) + pick(got_ref, index_ref).astype(f32)).astype(bf16)

    tile = by_rows(own, 2)
    return call(kernel, "layer_output", (2,), [scalars, tile, tile], tile, like(own.shape))(
        index, own, got
    )


def weight_gradient_call(lefts, right, blocks, split, extra=None, groups=1):
    flat = lefts[0].ndim == 2
    columns = lefts[0].shape[1] // blocks if flat else sum(a.shape[2] for a in lefts[::groups])
    more = [] if extra is None else [extra]
    lead = sum(e.shape[0] for e in more)
    height = lead + columns
    width = right.shape[1]
    half = blocks // 2

    def kernel(*refs):
        left_refs = refs[: len(lefts)]
        right_ref = refs[len(lefts)]
        extra_refs = refs[len(lefts) + 1 : len(lefts) + 1 + len(more)]
        outs = refs[len(lefts) + 1 + len(more) :]
        left = left_refs[0][...] if flat else lanes_of(paired(left_refs, groups))

        def put(ref, place, values, part):
            ref[place, lead:] = values
            for e in extra_refs:
                ref[place, :lead] = e[:, part]

        for start in range(0, width, 512):
            grads = dot_tn(left, right_ref[:, start : start + 512]).astype(bf16)
            for z in range(blocks):
                block = grads[z * columns : (z + 1) * columns]
                if not split:
                    put(outs[0], (z, slice(start, start + 512)), block, None)
                    continue
                mine, x_rest, y_rest, to_x, to_y = outs
                for j in range(start // 256, start // 256 + 2):
                    part = slice(256 * j, 256 * j + 256)
                    values = block[:, 256 * j - start : 256 * j - start + 256]
                    if j == 0:
                        put(mine, z, values, part)
                    elif j == 1:
                        put(*((to_x, half + z) if z < half else (x_rest, z - half)), values, part)
                    elif j == 2:
                        put(*((y_rest, z) if z < half else (to_y, z)), values, part)
                    else:
                        put(*((to_x, z) if z < half else (to_y, z - half)), values, part)

    if split:
        out_shape = [like((n, height, width // 4)) for n in (blocks, half, half, blocks, blocks)]
    else:
        out_shape = [like((blocks, height, width))]

        def kernel(*refs):
            left_refs = refs[: len(lefts)]
            right_ref, out_ref = refs[len(lefts)], refs[-1]
            left = left_refs[0][...] if flat else lanes_of(paired(left_refs, groups))
            grads = dot_tn(left, right_ref[...]).astype(bf16)
            for z in range(blocks):
                out_ref[z, lead:] = grads[z * columns : (z + 1) * columns]
                if more:
                    out_ref[z, :lead] = refs[len(lefts) + 1][...]

    return call(
        kernel,
        "weight_gradient",
        (1,),
        [whole(a) for a in (*lefts, right, *more)],
        [whole(o) for o in out_shape],
        [kept(o) for o in out_shape],
    )(*(in_hbm(*lefts, right) if groups > 1 else (*lefts, right)), *more)


def combine_call(first, second, x_got, y_got, near_rows):
    operands, out_shape = [], []
    if first is not None:
        operands += first[1:]
        out_shape += [like(first[1].shape)] * 2
    if second is not None:
        operands += second
        out_shape += [like(second[0].shape)]

    def kernel(*refs):
        ins, outs = list(refs[2 : 2 + len(operands)]), list(refs[2 + len(operands) :])
        x_ref, y_ref = refs[:2]
        if first is not None:
            x_rest, y_rest, x_out, y_out = ins.pop(0), ins.pop(0), outs.pop(0), outs.pop(0)
            half, rows = x_rest.shape[:2]
            for j in range(half):
                part = slice(j * rows, (j + 1) * rows)
                x_out[j] = (x_rest[j].astype(f32) + y_ref[part].astype(f32)).astype(bf16)
                y_out[j] = (y_rest[j].astype(f32) + x_ref[part].astype(f32)).astype(bf16)
        if second is not None:
            mine, x_near, y_near = ins
            half, rows = mine.shape[0] // 2, mine.shape[1]
            for j in range(half):
                near = slice((half + j) * rows, (half + j + 1) * rows)
                far = slice(near_rows + j * rows, near_rows + (j + 1) * rows)
                for place, near_ref, far_ref in ((j, x_near, y_ref), (half + j, y_near, x_ref)):
                    total = mine[place].astype(f32) + near_ref[near].astype(f32)
                    outs[0][place] = (total + far_ref[far].astype(f32)).astype(bf16)

    results = call(
        kernel,
        "gradient_sums",
        (1,),
        [whole(a) for a in (x_got, y_got, *operands)],
        [whole(o) for o in out_shape],
        out_shape,
    )(x_got, y_got, *operands)
    near = results[:2] if first is not None else None
    return near, results[-1] if second is not None else None


def hidden_back_call(dy, w, to_in, to_gate):
    hidden = to_in.shape[1]

    def kernel(dy_ref, w_ref, to_in_ref, to_gate_ref, in_ref, gate_ref):
        w = w_ref[...].reshape(hidden, -1)
        for start in range(0, hidden, 512):
            part = slice(start, min(start + 512, hidden))
            grad = dot_nt(dy_ref[...], w[part])
            in_ref[:, part] = (grad * to_in_ref[:, part].astype(f32)).astype(bf16)
            gate_ref[:, part] = (grad * to_gate_ref[:, part].astype(f32)).astype(bf16)

    tile = by_rows(to_in, 2)
    return call(
        kernel,
        "grad_lifted",
        (2,),
        [by_rows(dy, 2), whole(w), tile, tile],
        [tile, tile],
        [like(to_in.shape)] * 2,
    )(dy, w, to_in, to_gate)


def two_part_call(grad_in, grad_gate, up, gate):
    width = up.shape[2]

    def kernel(in_ref, gate_ref, up_ref, w_gate_ref, out_ref):
        total = dot_nn(in_ref[...], up_ref[...].reshape(-1, width))
        total += dot_nn(gate_ref[...], w_gate_ref[...].reshape(-1, width))
        out_ref[...] = total.astype(bf16)

    out = like((grad_in.shape[0], width))
    return call(
        kernel,
        "grad_normed_two",
        (2,),
        [by_rows(grad_in, 2), by_rows(grad_gate, 2), whole(up), whole(gate)],
        by_rows(out, 2),
        out,
    )(grad_in, grad_gate, up, gate)


def two_back_call(part, got, middle, dy, gains):
    rows, width = middle.shape

    def kernel(part_ref, got_ref, mid_ref, dy_ref, gain_ref, grad_ref, low_ref, gain_grad_ref):
        i = pl.program_id(0)
        grads = part_ref[...].astype(f32) + got_ref[...].astype(f32)
        back, gain_grad = unnormalize(grads, mid_ref[...], gain_ref[1:2, :])
        grad = dy_ref[...].astype(f32) + back
        low_ref[...] = grad.astype(bf16)

        @pl.when(i == 0)
        def _():
            gain_grad_ref[...] = jnp.zeros_like(gain_grad_ref)

        @pl.when(i < 2)
        def _():
            grad_ref[...] = grad
            gain_grad_ref[...] += jnp.broadcast_to(gain_grad, gain_grad_ref.shape)

    tile = by_rows(middle, 4)
    row = like((8, width), f32)
    return call(
        kernel,
        "second_norm_gradient",
        (4,),
        [tile, swapped_rows(got), tile, tile, whole(gains)],
        [
            pl.BlockSpec((rows // 4, width), lambda i: (jnp.minimum(i, 1), 0)),
            tile,
            whole(row),
        ],
        [like((rows // 2, width), f32), like(middle.shape), row],
    )(part, got, middle, dy, gains)


def att_grad_call(grad, w, start):
    blocks = w.shape[0]
    columns = w.shape[1] - start

    def kernel(g_ref, w_ref, out_ref):
        out = dot_nt(g_ref[...], rows_of(w_ref, start, w_ref.shape[1])).astype(bf16)
        for z in range(blocks):
            out_ref[z] = out[:, z * columns : (z + 1) * columns]

    out = like((blocks, grad.shape[0], columns))
    return call(
        kernel,
        "grad_attended",
        (2,),
        [by_rows(grad, 2), whole(w)],
        blocks_by_rows(out, 2),
        out,
    )(grad, w)


def one_part_call(queries, keys_values, w, start):
    rows, width = queries[0].shape[1], w.shape[2]
    count = len(queries)

    def kernel(*refs):
        *left_refs, w_ref, own_ref, oth_ref = refs
        total = dot_nn(lanes_of(paired(left_refs, count)), rows_of(w_ref, start, start + 384))

        @pl.when(pl.program_id(0) == 1)
        def _():
            own_ref[...] = total

        @pl.when(pl.program_id(0) == 0)
        def _():
            oth_ref[...] = total.astype(bf16)

    def half(array):
        shape = (array.shape[0], rows // 2, array.shape[2])
        return pl.BlockSpec(shape, lambda i: (0, 1 - i, 0))

    first = pl.BlockSpec((rows // 2, width), lambda i: (0, 0))
    return call(
        kernel,
        "grad_normed_one",
        (2,),
        [half(a) for a in (*queries, *keys_values)] + [whole(w)],
        [first, first],
        [like((rows // 2, width), f32), like((rows // 2, width))],
    )(*in_hbm(*queries, *keys_values, w))


def one_back_call(own, got, x, grad_middle, gains, gain_two, index):
    rows, width = own.shape

    def kernel(
        index_ref, own_ref, got_ref, x_ref, mid_ref, gain_ref, gain_two_ref, grad_ref, gain_grad_ref,
        total_ref, low_ref,
    ):
        i = pl.program_id(0)
        grads = own_ref[...] + got_ref[...].astype(f32)
        back, gain_grad = unnormalize(grads, x_ref[...].astype(f32), gain_ref[0:1, :])
        low_ref[...] = (mid_ref[...] + back).astype(bf16)
        grad_ref[...] = pick(low_ref, index_ref)

        @pl.when(i == 0)
        def _():
            total_ref[...] = gain_grad

        @pl.when(i == 1)
        def _():
            total = total_ref[...] + gain_grad
            row = lax.broadcasted_iota(jnp.int32, gain_grad_ref.shape, 0)
            both = jnp.where(row == 0, total, jnp.where(row == 1, gain_two_ref[0:1, :], 0.0))
            gain_grad_ref[...] = both.astype(bf16)

    tile = by_rows(own, 2)
    x_tile = pl.BlockSpec((rows // 2, width), lambda i: (i, 0))
    gain_grads = like((16, width))
    return call(
        kernel,
        "first_norm_gradient",
        (2,),
        [scalars, tile, tile, x_tile, tile, whole(gains), whole(gain_two)],
        [tile, whole(gain_grads)],
        [like(own.shape), gain_grads],
        [pltpu.VMEM((1, width), f32), pltpu.VMEM((rows // 2, width), bf16)],
    )(index, own, got, x, grad_middle, gains, gain_two)


(
    X_IN,
    COT,
    BOTH,
    LOW,
    COLUMN,
    W,
    NEAR,
    GRAD,
    PAIR,
    TABLES,
    REST,
    X0,
    X_OWN,
    GAINS,
    X,
    NORMED,
    QKV,
    ATT,
    LSE,
    Y1,
    PART,
    Y_OWN,
    MIDDLE,
    NORMED_TWO,
    HIDDEN,
    TO_IN,
    TO_GATE,
    DY,
    G,
    F,
    N,
    SUM,
    G_GATE,
    OUT,
    DQ,
    DKV,
    G_ATT,
    GRAD_MID,
    MID_LOW,
    GAIN_TWO,
    OUT1,
    OWN,
    OTHER,
    DX,
    OUT0,
    DX1,
    DX0,
    INPUT_GRADS,
    OUTPUTS,
    UPDATED,
) = range(50)


def make_per_device(dp, tensor):
    count = dp * tensor
    chips = dp // 2
    chip_bits = chips.bit_length() - 1
    square = chip_bits == 2
    half = tensor // 2

    def permute(value, pairs):
        return lax.ppermute(value, AXES, pairs)

    def exchange(value, mask):
        return permute(value, [(i, i ^ mask) for i in range(count)])

    def over_chip(value, bit):
        return exchange(value, (2 * tensor) << bit)

    def over_core(value, pieces=1):
        rows = value.shape[0] // pieces
        got = [exchange(value[i * rows : (i + 1) * rows], tensor) for i in range(pieces)]
        return got[0] if pieces == 1 else jnp.concatenate(got, axis=0)

    def spread_pairs(r):
        pairs = []
        for i in range(count):
            z = i % tensor
            core = (i // tensor) % 2
            chip = i // (2 * tensor)
            pairs.append((i, (chip * 2 + z % 2) * tensor + (r ^ (z // 2)) * 2 + core))
        return pairs

    def by_column(blocks, me_z):
        for bit in range(tensor.bit_length() - 1):
            odd = (me_z >> bit) % 2 == 1
            blocks = [jnp.where(odd, blocks[k ^ (1 << bit)], blocks[k]) for k in range(tensor)]
        return blocks

    inner = [(i, i ^ 3) for i in range(count) if i % tensor in (1, 2)]
    outward = [(i, i ^ 1) for i in range(count) if i % tensor in (1, 2)]

    def gather_near_z(rows, me_z):
        got = exchange(rows, 1)
        low = me_z % 2 == 0
        return jnp.stack([jnp.where(low, rows, got), jnp.where(low, got, rows)])

    def gather_far_z(pair, got, me_z):
        sent = permute(got, outward)
        other = jnp.where((me_z == 0) | (me_z == 3), sent, got)
        low = me_z < 2
        return jnp.concatenate([jnp.where(low, pair, other), jnp.where(low, other, pair)], axis=0)

    def gather_plane(columns):
        current = columns[None]
        for bit in range(chip_bits):
            current = jnp.concatenate([current, over_chip(current, bit)], axis=0)
        return current.transpose(1, 2, 0, 3).reshape(columns.shape[:2] + (-1,))

    def low_sum(*values):
        return sum(v.astype(f32) for v in values).astype(bf16)

    def reduce_plane(parts):
        current = parts
        for bit in reversed(range(chip_bits)):
            middle = current.shape[0] // 2
            current = low_sum(current[:middle], over_chip(current[middle:], bit))
        return current[0]

    def reduce_column(blocks):
        result = blocks[0].astype(f32)
        for k in range(1, tensor):
            result = result + exchange(blocks[k], k).astype(f32)
        return result

    def per_device(
        inputs,
        cotangent,
        attention_in,
        attention_out,
        expand_weight,
        contract_weight,
        norm_gains,
        attention_in_first,
        attention_in_second,
        attention_out_first,
        attention_out_second,
        expand_first,
        expand_second,
        contract_first,
        contract_second,
        gains_first,
        gains_second,
    ):
        block = attention_in.shape[0]
        head_columns = attention_in.shape[2]
        hidden_local = expand_weight.shape[2]
        local_rows = inputs.shape[2]
        me_dp = lax.axis_index("dp")
        me_z = lax.axis_index("tensor")
        core = me_dp % 2
        z_high = me_z // 2

        me_chip = me_dp // 2
        index = me_chip ^ jnp.arange(chips, dtype=jnp.int32)
        aligned = block % 128 == 0
        kernel_index = index if aligned else jnp.zeros((1,), jnp.int32)

        def outside(values):
            if aligned:
                return values
            shaped = values.reshape(values.shape[0], chips, 2 * block)
            return jnp.take(shaped, index, axis=1).reshape(values.shape)

        def spread(values, r):
            part = lax.dynamic_index_in_dim(values[:, 0], r ^ z_high, 0, keepdims=False)
            return permute(part, spread_pairs(r))

        def collect(values, r):
            part = values[r * local_rows : (r + 1) * local_rows]
            return permute(part, [(b, a) for a, b in spread_pairs(r)])

        def assemble(first, second):
            odd = z_high == 1
            return jnp.stack([jnp.where(odd, second, first), jnp.where(odd, first, second)])[:, None]

        def rotary_tables():
            row_starts = [
                ((r ^ z_high) * 2 + (core ^ c)) * local_rows for c in range(2) for r in range(2)
            ]
            positions = jnp.concatenate([s + jnp.arange(local_rows) for s in row_starts]).astype(f32)
            exponents = jnp.arange(0, DH, 2).astype(f32) / DH
            angles = positions[:, None] * jnp.power(rope_theta, -exponents)[None, :]
            cosine, sine = jnp.cos(angles), jnp.sin(angles)
            cosine = jnp.concatenate([cosine] * 4, axis=-1)
            sine = jnp.concatenate([-sine, sine] * 2, axis=-1)
            return cosine, sine

        cut = (hidden_local // 2 + 15) // 16 * 16
        spare = 2 * cut - hidden_local
        head_cut = head_columns // 2
        low_in = attention_in.astype(bf16).reshape(block, 3, 2, head_cut).transpose(2, 1, 3, 0)
        low_out = attention_out.astype(bf16).reshape(block, 2, head_cut).transpose(1, 2, 0)
        low_expand = jnp.pad(expand_weight.astype(bf16).transpose(1, 2, 0), ((0, 0), (0, spare), (0, 0)))
        low_expand = low_expand.reshape(2, 2, cut, block).transpose(1, 0, 2, 3)
        low_contract = jnp.pad(contract_weight.astype(bf16).T, ((0, spare), (0, 0)))
        low_contract = low_contract.reshape(2, cut, block)
        low_gains = jnp.pad(norm_gains.astype(bf16), ((0, 14), (0, 0)))
        lead = low_gains.shape[0]
        both = jnp.concatenate(
            [
                jnp.stack([low_gains, low_gains]),
                low_in.reshape(2, -1, block),
                low_out,
                low_expand.reshape(2, -1, block),
                low_contract,
            ],
            axis=1,
        )
        out_start = lead + 3 * head_cut
        sizes = [out_start + head_cut, cut, cut, cut]
        starts = [sum(sizes[:k]) for k in range(len(sizes) + 1)]
        last = len(sizes)
        first_core = core == 0

        def side_by_side(mine, got):
            return jnp.concatenate(
                [jnp.where(first_core, mine, got), jnp.where(first_core, got, mine)], axis=-1
            )

        state = {X_IN: inputs, COT: cotangent, BOTH: both}
        held = []
        state_late = []
        again = []

        def run(work):
            nonlocal state
            new = {}
            late = held[:]
            held[:] = again
            again.clear()
            work(state, new)
            for values in late:
                new.update(values)
            state.update(new)
            names = list(state)
            state = dict(zip(names, lax.optimization_barrier([state[n] for n in names])))

        def column_direct(s, new, k):
            rows = s[LOW][starts[k] : starts[k + 1]]
            blocks = [rows] + [exchange(rows, j) for j in range(1, tensor)]
            new[COLUMN, k] = jnp.stack(by_column(blocks, me_z))

        def plane(s, new, k):
            if not square:
                if k < last:
                    new[W, k] = gather_plane(s.pop((COLUMN, k)))
                return
            sends, first_rows = ([], []), 0
            if k < last:
                column = s[COLUMN, k]
                first_rows = column.shape[0] * column.shape[1]
                for way in range(2):
                    sends[way].append(column.reshape(first_rows, -1))
            if k > 0:
                got = s[NEAR, k - 1]
                rows = half * sizes[k - 1]
                sends[0].append(got[1][rows : 2 * rows])
                sends[1].append(got[0][:rows])
            got = tuple(over_chip(jnp.concatenate(sends[way], axis=0), way) for way in range(2))
            if k < last:
                new[NEAR, k] = got
            if k > 0:
                new[W, k - 1] = weave_call(
                    s.pop((COLUMN, k - 1)), *s.pop((NEAR, k - 1)), *got, first_rows
                )

        step_rates = (
            2.5 * D ** (-0.5),
            2.5 * max(1, 4 * H * DH // SEQ) ** (-0.5),
            2.5 * D ** (-0.5),
            2.5 * FF ** (-0.5),
            0.25,
        )

        def joined(s, k, rows):
            return jnp.concatenate(s[GRAD, k], axis=0)[:rows]

        def joined_heads(s):
            parts = [g[lead:].reshape(3, head_cut, block) for g in s[GRAD, 4]]
            return lax.optimization_barrier(jnp.concatenate(parts, axis=1).transpose(2, 0, 1))

        def first_updates(s):
            grad_down, grad_up, grad_gate = (joined(s, k, hidden_local) for k in range(3))
            grad_expand = jnp.stack([grad_up, grad_gate]).transpose(2, 0, 1)
            grad_out, grad_expand, grad_down = lax.optimization_barrier(
                (joined(s, 3, head_columns).T, grad_expand, grad_down.T)
            )
            return (
                adamw_update(
                    attention_out, attention_out_first, attention_out_second, grad_out, step_rates[1]
                ),
                adamw_update(expand_weight, expand_first, expand_second, grad_expand, step_rates[2]),
                adamw_update(
                    contract_weight, contract_first, contract_second, grad_down, step_rates[3]
                ),
            )

        def f0(s, new):
            pair = s.pop(BOTH)
            mine = jnp.where(first_core, pair[0], pair[1])
            got = over_core(jnp.where(first_core, pair[1], pair[0]))
            new[LOW] = side_by_side(mine, got)

        run(f0)

        def f1(s, new):
            column_direct(s, new, 0)
            new[PAIR] = gather_near_z(s[LOW][starts[1] : starts[2]], me_z)
            new[TABLES] = rotary_tables()

        run(f1)

        def f2(s, new):
            plane(s, new, 0)
            up = s.pop(PAIR)
            rest = gather_near_z(s[LOW][starts[2] :], me_z)
            new[COLUMN, 1] = gather_far_z(up, permute(up, inner), me_z)
            new[REST] = (rest, permute(rest, inner))
            new[X0] = spread(s[X_IN], 0)

        run(f2)

        def f3(s, new):
            plane(s, new, 1)
            rest = gather_far_z(*s.pop(REST), me_z)
            new[COLUMN, 2], new[COLUMN, 3] = rest[:, :cut], rest[:, cut:]
            new[X_OWN] = jnp.concatenate([s.pop(X0), spread(s.pop(X_IN), 1)], axis=0)

        run(f3)

        def f4(s, new):
            plane(s, new, 2)
            rows = s.pop(X_OWN)
            x_raw = jnp.concatenate([rows, over_core(rows, 2)], axis=0)
            new[GAINS] = s[W, 0][0, :lead].astype(f32)
            new[X], new[NORMED] = norm_call(outside(x_raw), new[GAINS], kernel_index)
            query, key, value = qkv_call(new[NORMED], s[W, 0], lead, *s[TABLES])
            new[QKV] = (query, key, value)
            new[ATT, 0], new[LSE, 0] = attend_call(query, key, value, 0, tensor // 2)
            new[Y1] = spread(s[COT], 1)

        run(f4)

        def f5(s, new):
            plane(s, new, 3)
            new[ATT, 1], new[LSE, 1] = attend_call(*s[QKV], tensor // 2, tensor // 2)
            new[PART] = attention_output_call((s[ATT, 0], new[ATT, 1]), s[W, 0], out_start)
            new[Y_OWN] = jnp.concatenate([spread(s.pop(COT), 0), s.pop(Y1)], axis=0)

        run(f5)

        def f6(s, new):
            plane(s, new, 4)
            part, rows = s.pop(PART), s.pop(Y_OWN)
            new[MIDDLE], new[NORMED_TWO] = middle_call(
                s[X], part, over_core(part, 4), s[GAINS]
            )
            new[HIDDEN], new[TO_IN], new[TO_GATE] = lift_call(
                new[NORMED_TWO], s[W, 1], s[W, 2]
            )
            y_raw = jnp.concatenate([rows, over_core(rows)], axis=0)
            new[DY] = order_call(outside(y_raw), kernel_index)
            made(new, 0, [new[HIDDEN]], new[DY])

        def made(new, k, lefts, right, extra=None, groups=1):
            split = square and aligned
            grads = weight_gradient_call(lefts, right, tensor, split, extra, groups)
            if not split:
                (full,) = grads
                grads = full.reshape(full.shape[:2] + (chips, -1)).transpose(2, 0, 1, 3)
            new[G, k] = grads

        def plane_back(s, new, k):
            if not square:
                if (G, k) in s:
                    new[F, k] = [b for b in reduce_plane(s.pop((G, k)))]
                return
            flat = lambda a: a.reshape(-1, a.shape[-1])
            to_x, to_y, rows = [], [], 0
            if (G, k) in s:
                mine, x_rest, y_rest, x_out, y_out = s.pop((G, k))
                rows = x_out.shape[0] * x_out.shape[1]
                to_x.append(flat(x_out))
                to_y.append(flat(y_out))
            if (N, k - 1) in s:
                x_last, y_last, mine_last, x_near, y_near = s.pop((N, k - 1))
                to_x.append(flat(x_last))
                to_y.append(flat(y_last))
            x_got = over_chip(jnp.concatenate(to_x, axis=0), 0)
            y_got = over_chip(jnp.concatenate(to_y, axis=0), 1)
            first = (mine, x_rest, y_rest) if rows else None
            second = (mine_last, x_near, y_near) if len(to_x) > 1 or not rows else None
            near, far = combine_call(first, second, x_got, y_got, rows)
            if first is not None:
                new[N, k] = (*near, mine, x_got, y_got)
            if second is not None:
                new[F, k - 1] = far

        def whole_blocks(blocks):
            return blocks if square else jnp.stack(blocks)

        def scatter(s, k):
            total = lax.psum_scatter(
                whole_blocks(s.pop((F, k))), "tensor", scatter_dimension=0, tiled=False
            )
            held.append({(SUM, k): total})

        def column(s, new, *chunks):
            blocks = [by_column(s.pop((F, k)), me_z) for k in chunks]
            total = reduce_column([jnp.concatenate(b, axis=0) for b in zip(*blocks)])
            start = 0
            for k, b in zip(chunks, blocks):
                new[SUM, k] = total[start : start + b[0].shape[0]].astype(bf16)
                start += b[0].shape[0]

        def trade(s, new, *chunks):
            sums = [s.pop((SUM, k)) for k in chunks]
            total = jnp.concatenate(sums, axis=0)
            mine = jnp.where(first_core, total[:, :block], total[:, block:])
            got = over_core(jnp.where(first_core, total[:, block:], total[:, :block]))
            start = 0
            for k, rows in zip(chunks, [a.shape[0] for a in sums]):
                a, b = mine[start : start + rows], got[start : start + rows]
                new[GRAD, k] = (
                    jnp.where(first_core, a, b).astype(f32),
                    jnp.where(first_core, b, a).astype(f32),
                )
                start += rows

        run(f6)

        def s1(s, new):
            plane_back(s, new, 0)
            own, other = lower_call(s.pop(HIDDEN), s[W, 3], s[MIDDLE])
            g_in, g_gate = hidden_back_call(
                s[DY], s.pop((W, 3)), s.pop(TO_IN), s.pop(TO_GATE)
            )
            new[G_GATE] = g_gate
            new[PART] = two_part_call(g_in, g_gate, s.pop((W, 1)), s.pop((W, 2)))
            made(new, 1, [g_in], s[NORMED_TWO])
            new[OUT] = outside(output_call(own, over_core(other), kernel_index))

        run(s1)

        def attention_back(s, new, p):
            new[DQ, p], new[DKV, p] = attend_back_call(
                *s[QKV], s[G_ATT], s[ATT, p], s.pop((LSE, p)), *s[TABLES],
                p * (tensor // 2), tensor // 2,
            )

        def s2(s, new):
            plane_back(s, new, 1)
            part = s.pop(PART)
            new[GRAD_MID], new[MID_LOW], new[GAIN_TWO] = two_back_call(
                part, over_core(part, 4), s.pop(MIDDLE), s.pop(DY), s[GAINS]
            )
            made(new, 2, [s.pop(G_GATE)], s.pop(NORMED_TWO))
            s[G_ATT] = new[G_ATT] = att_grad_call(new[MID_LOW], s[W, 0], out_start)
            attention_back(s, new, 0)
            new[OUT1] = collect(s[OUT], 1)

        run(s2)

        def s3(s, new):
            scatter(s, 0)
            plane_back(s, new, 2)
            attention_back(s, new, 1)
            made(new, 3, [s[ATT, 0], s[ATT, 1]], s[MID_LOW], None, 2)
            new[OWN], new[OTHER] = one_part_call(
                (s[DQ, 0], new[DQ, 1]), (s[DKV, 0], new[DKV, 1]), s[W, 0], lead
            )

        run(s3)

        def s4(s, new):
            scatter(s, 1)
            plane_back(s, new, 3)
            dx, gain_grads = one_back_call(
                s.pop(OWN), over_core(s.pop(OTHER), 2), s.pop(X), s.pop(GRAD_MID),
                s[GAINS], s.pop(GAIN_TWO), kernel_index,
            )
            new[DX] = outside(dx)
            lefts = [s[DQ, 0], s[DQ, 1], s[DKV, 0], s[DKV, 1]]
            made(new, 4, lefts, s[NORMED], gain_grads, 2)
            new[OUT0] = collect(s[OUT], 0)

        run(s4)

        def s5(s, new):
            plane_back(s, new, 4)
            new[DX1] = collect(s[DX], 1)
            new[DX0] = collect(s[DX], 0)

        run(s5)

        def s6(s, new):
            scatter(s, 2)
            late = held.pop()
            plane_back(s, new, 5)
            column(s, new, 3)
            state_late.append(late)
            new[INPUT_GRADS] = assemble(s.pop(DX0), s.pop(DX1))
            new[OUTPUTS] = assemble(s.pop(OUT0), s.pop(OUT1))

        run(s6)

        def s7(s, new):
            column(s, new, 4)
            s.update(state_late.pop())
            trade(s, new, 0, 1, 2, 3)
            new[UPDATED] = first_updates(new)

        run(s7)

        def s8(s, new):
            trade(s, new, 4)

        run(s8)

        layer_output, input_gradient = state[OUTPUTS], state[INPUT_GRADS]
        grad_qkv = joined_heads(state)
        gain_total = sum(g[:2] for g in state[GRAD, 4])
        qkv_new = adamw_update(
            attention_in, attention_in_first, attention_in_second, grad_qkv, step_rates[0]
        )
        gains_new = adamw_update(norm_gains, gains_first, gains_second, gain_total, step_rates[4])
        out_new, expand_new, contract_new = state[UPDATED]
        return (
            layer_output,
            input_gradient,
            *qkv_new,
            *out_new,
            *expand_new,
            *contract_new,
            *gains_new,
        )

    return per_device


def solution(mesh):
    activation = P(None, "dp", "tensor", None)
    cube = P("dp", None, "tensor")
    flat = P("dp", "tensor")
    gain = P(None, "dp")
    return jax.shard_map(
        make_per_device(mesh.shape["dp"], mesh.shape["tensor"]),
        mesh=mesh,
        in_specs=(
            activation, activation, cube, flat, cube, flat, gain,
            cube, cube, flat, flat, cube, cube, flat, flat, gain, gain,
        ),
        out_specs=(
            activation, activation, cube, cube, cube, flat, flat, flat,
            cube, cube, cube, flat, flat, flat, gain, gain, gain,
        ),
        check_vma=False,
    )
```

```python
import jax
import jax.numpy as jnp
from jax import lax
from jax.experimental import pallas as pl
from jax.experimental.pallas import tpu as pltpu
from jax.sharding import PartitionSpec as P

D = 1024
H = 16
DH = 64
FF = 2624
SEQ = 1024
STEP = 10

epsilon_norm = 1e-05
rope_theta = 160000.0
beta_first = 0.9
beta_second = 0.98
epsilon_adam = 1e-06
weight_decay = 1e-05

AXES = ("dp", "tensor")
bf16 = jnp.bfloat16
f32 = jnp.float32


def dot_nt(left, right):
    return lax.dot_general(left, right, (((1,), (1,)), ((), ())), preferred_element_type=f32)


def dot_tn(left, right):
    return lax.dot_general(left, right, (((0,), (0,)), ((), ())), preferred_element_type=f32)


def dot_nn(left, right):
    return jnp.dot(left, right, preferred_element_type=f32)


def adamw_update(weight, first_moment, second_moment, gradient, step_rate):
    first_new = beta_first * first_moment + (1.0 - beta_first) * gradient
    second_new = beta_second * second_moment + (1.0 - beta_second) * gradient * gradient
    first_hat = first_new / (1.0 - beta_first**STEP)
    second_hat = second_new / (1.0 - beta_second**STEP)
    weight_new = weight - step_rate * (
        first_hat / (jnp.sqrt(second_hat) + epsilon_adam) + weight_decay * weight
    )
    return (weight_new, first_new, second_new)


def whole(array):
    return pl.BlockSpec(
        array.shape, lambda i, rank=array.ndim: (0,) * rank, pipeline_mode=pl.Buffered(1)
    )


def by_block(array):
    return pl.BlockSpec((1,) + array.shape[1:], lambda z: (z, 0, 0))


def by_rows(array, steps):
    return pl.BlockSpec((array.shape[0] // steps, array.shape[1]), lambda i: (i, 0))


def like(shape, dtype=bf16):
    return jax.ShapeDtypeStruct(shape, dtype)


def kept(array):
    return pltpu.HBM(array.shape, array.dtype)


microseconds = dict(
    feature_order=3.0,
    gathered_weight=3.0,
    gradient_sums=3.0,
    first_norm=4.0,
    qkv_projection=6.0,
    attention_forward=9.0,
    attention_output=2.5,
    second_norm=4.0,
    expand=12.0,
    contract=5.0,
    layer_output=2.0,
    weight_gradient=5.0,
    grad_lifted=6.0,
    grad_normed_two=8.0,
    second_norm_gradient=5.0,
    grad_attended=2.5,
    attention_backward=14.0,
    grad_normed_one=6.0,
    first_norm_gradient=3.0,
)


def cost(name):
    return pl.CostEstimate(
        flops=int(microseconds[name] * 0.35e9),
        bytes_accessed=int(microseconds[name] * 1.2e6),
        transcendentals=0,
    )


def call(kernel, name, grid, in_specs, out_specs, out_shape, scratch=()):
    return pl.pallas_call(
        kernel,
        grid=grid,
        in_specs=in_specs,
        out_specs=out_specs,
        out_shape=out_shape,
        scratch_shapes=list(scratch),
        compiler_params=pltpu.CompilerParams(vmem_limit_bytes=20 << 20),
        cost_estimate=cost(name),
        name=name,
    )


def swap_halves(values):
    lane = lax.broadcasted_iota(jnp.int32, values.shape, 1)
    return jnp.where(
        lane % DH < DH // 2,
        pltpu.roll(values, values.shape[1] - DH // 2, 1),
        pltpu.roll(values, DH // 2, 1),
    )


def normalize(values):
    centered = values - jnp.mean(values, axis=1, keepdims=True)
    scale = lax.rsqrt(jnp.mean(centered * centered, axis=1, keepdims=True) + epsilon_norm)
    return centered * scale, scale


def unnormalize(grads, values, gain):
    hats, scale = normalize(values)
    gain_grad = jnp.sum(grads * hats, axis=0, keepdims=True)
    errors = grads * gain
    average = jnp.mean(errors, axis=1, keepdims=True)
    along = jnp.mean(errors * hats, axis=1, keepdims=True)
    return scale * (errors - average - hats * along), gain_grad


def pick(ref, index_ref):
    count = index_ref.shape[0]
    if count == 1:
        return ref[...]
    block = ref.shape[1] // count
    parts = [ref[:, pl.ds(pl.multiple_of(index_ref[j] * block, block), block)] for j in range(count)]
    return jnp.concatenate(parts, axis=1)


def in_hbm(*arrays):
    return tuple(pltpu.with_memory_space_constraint(a, pltpu.HBM) for a in arrays)


scalars = pl.BlockSpec(memory_space=pltpu.SMEM)


def order_call(values, index):
    def kernel(index_ref, in_ref, out_ref):
        out_ref[...] = pick(in_ref, index_ref)

    tile = by_rows(values, 2)
    return call(
        kernel, "feature_order", (2,), [scalars, tile], tile, like(values.shape, values.dtype)
    )(index, values)


def norm_call(x, gains, index):
    def kernel(index_ref, x_ref, gain_ref, x_out_ref, out_ref):
        values = pick(x_ref, index_ref)
        x_out_ref[...] = values
        hats, _ = normalize(values.astype(f32))
        out_ref[...] = (hats * gain_ref[0:1, :]).astype(bf16)

    tile = by_rows(x, 4)
    return call(
        kernel, "first_norm", (4,), [scalars, tile, whole(gains)], [tile] * 2, [like(x.shape)] * 2
    )(index, x, gains)


def qkv_call(x, w, start, cosine, sine):
    rows, blocks = x.shape[0], w.shape[0]

    def kernel(x_ref, w_ref, cos_ref, sin_ref, q_ref, k_ref, v_ref):
        mixed = dot_nt(x_ref[...], w_ref[0, start : start + 384])
        cosine, sine = cos_ref[...], sin_ref[...]
        query, key = mixed[:, :128], mixed[:, 128:256]
        query = query * cosine + swap_halves(query) * sine
        key = key * cosine + swap_halves(key) * sine
        q_ref[0] = query.astype(bf16) * bf16(DH**-0.5)
        k_ref[0] = key.astype(bf16)
        v_ref[0] = mixed[:, 256:].astype(bf16)

    out = like((blocks, rows, 128))
    return call(
        kernel,
        "qkv_projection",
        (blocks,),
        [whole(x), by_block(w), whole(cosine), whole(sine)],
        [by_block(out)] * 3,
        [out] * 3,
    )(x, w, cosine, sine)


def pair_specs(array, first, halves):
    rows = array.shape[1]
    return (
        pl.BlockSpec((1, rows // halves, array.shape[2]), lambda z, i: (first + z, i, 0)),
        pl.BlockSpec((1, rows, array.shape[2]), lambda z, i: (first + z, 0, 0)),
    )


def weave_call(column, x_near, y_near, x_far, y_far, far_rows):
    blocks, rows, width = column.shape
    half = blocks // 2

    def kernel(col_ref, x_ref, y_ref, x_far_ref, y_far_ref, out_ref):
        z = pl.program_id(0)
        out_ref[0, :, :width] = col_ref[0]
        out_ref[0, :, width : 2 * width] = x_ref[...]
        out_ref[0, :, 2 * width : 3 * width] = y_ref[...]
        start = pl.multiple_of(far_rows + z % half * rows, 16)

        @pl.when(z < half)
        def _():
            out_ref[0, :, 3 * width :] = y_far_ref[pl.ds(start, rows), :]

        @pl.when(z >= half)
        def _():
            out_ref[0, :, 3 * width :] = x_far_ref[pl.ds(start, rows), :]

    near = pl.BlockSpec((rows, width), lambda z: (z, 0))
    out = like((blocks, rows, 4 * width))
    return call(
        kernel,
        "gathered_weight",
        (blocks,),
        [by_block(column), near, near, whole(x_far), whole(y_far)],
        by_block(out),
        out,
    )(column, x_near, y_near, x_far, y_far)


def attend_call(query, key, value, first, count):
    rows = query.shape[1]

    def kernel(q_ref, k_ref, v_ref, out_ref, lse_ref):
        query, key = q_ref[0], k_ref[0]
        value_t = v_ref[0].astype(f32).T.astype(bf16)
        lane = lax.broadcasted_iota(jnp.int32, query.shape, 1)
        outs = []
        for head in range(2):
            query_head = jnp.where(lane // DH == head, query, jnp.zeros_like(query))
            scores = dot_nt(key, query_head)
            peak = jnp.max(scores, axis=0, keepdims=True)
            weights = jnp.exp(scores - peak)
            total = jnp.sum(weights, axis=0, keepdims=True)
            out = dot_nn(value_t[head * DH : (head + 1) * DH], weights.astype(bf16))
            outs.append(out / total)
            lse_ref[0, head : head + 1, :] = peak + jnp.log(total)
        out_ref[0] = jnp.concatenate(outs, axis=0).T.astype(bf16)

    half, full = pair_specs(query, first, 2)
    out_half, _ = pair_specs(query, 0, 2)
    lse = pl.BlockSpec((1, 2, rows // 2), lambda z, i: (z, 0, i))
    return call(
        kernel,
        "attention_forward",
        (count, 2),
        [half, full, full],
        [out_half, lse],
        [like((count, rows, 128)), like((count, 2, rows), f32)],
    )(query, key, value)


def attend_back_call(query, key, value, grad, out, lse, cosine, sine, first, count):
    rows = query.shape[1]

    def kernel(
        q_ref, k_ref, v_ref, grad_ref, out_ref, lse_ref, cos_ref, sin_ref, dq_ref, dkv_ref,
        key_total, value_total,
    ):
        step = pl.program_id(1)
        query, key, value, grad = q_ref[0], k_ref[0], v_ref[0], grad_ref[0]
        key_t = key.astype(f32).T.astype(bf16)
        product_t = (grad.astype(f32) * out_ref[0].astype(f32)).T
        lane = lax.broadcasted_iota(jnp.int32, query.shape, 1)
        grad_key = jnp.zeros((rows, 128), f32)
        grad_value = jnp.zeros((rows, 128), f32)
        grad_queries = []
        for head in range(2):
            mine = lane // DH == head
            query_head = jnp.where(mine, query, jnp.zeros_like(query))
            grad_head = jnp.where(mine, grad, jnp.zeros_like(grad))
            delta = jnp.sum(product_t[head * DH : (head + 1) * DH], axis=0, keepdims=True)
            weights = jnp.exp(dot_nt(key, query_head) - lse_ref[0, head : head + 1, :])
            grad_soft = dot_nt(value, grad_head)
            grad_scores = (weights * (grad_soft - delta)).astype(bf16)
            grad_value += dot_nn(weights.astype(bf16), grad_head)
            grad_key += dot_nn(grad_scores, query_head)
            grad_queries.append(dot_nn(key_t[head * DH : (head + 1) * DH], grad_scores))
        half = query.shape[0]
        grad_query = jnp.concatenate(grad_queries, axis=0).T * (DH**-0.5)
        start = pl.multiple_of(step * half, half)
        cosine, sine = cos_ref[pl.ds(start, half), :], sin_ref[pl.ds(start, half), :]
        dq_ref[0] = (grad_query * cosine - swap_halves(grad_query) * sine).astype(bf16)

        @pl.when(step == 0)
        def _():
            key_total[...] = grad_key
            value_total[...] = grad_value

        @pl.when(step == 1)
        def _():
            total = key_total[...] + grad_key
            back = total * cos_ref[...] - swap_halves(total) * sin_ref[...]
            dkv_ref[0, :, :128] = back.astype(bf16)
            dkv_ref[0, :, 128:] = (value_total[...] + grad_value).astype(bf16)

    half, full = pair_specs(query, first, 2)
    out_half, _ = pair_specs(query, 0, 2)
    lse_spec = pl.BlockSpec((1, 2, rows // 2), lambda z, i: (z, 0, i))
    table = pl.BlockSpec(cosine.shape, lambda z, i: (0, 0))
    return call(
        kernel,
        "attention_backward",
        (count, 2),
        [half, full, full, half, out_half, lse_spec, table, table],
        [out_half, pl.BlockSpec((1, rows, 256), lambda z, i: (z, 0, 0))],
        [like((count, rows, 128)), like((count, rows, 256))],
        [pltpu.VMEM((rows, 128), f32)] * 2,
    )(*in_hbm(query, key, value, grad, out, lse, cosine, sine))


def lanes_of(groups):
    return jnp.concatenate([r[j] for g in groups for j in range(g[0].shape[0]) for r in g], axis=1)


def paired(refs, count):
    return [refs[i::count] for i in range(count)]


def blocks_by_rows(array, steps):
    return pl.BlockSpec(
        (array.shape[0], array.shape[1] // steps, array.shape[2]), lambda i: (0, i, 0)
    )


def rows_of(ref, start, stop):
    if start == 0 and stop == ref.shape[1]:
        return ref[...].reshape(-1, ref.shape[2])
    return jnp.concatenate([ref[z, start:stop] for z in range(ref.shape[0])], axis=0)


def attention_output_call(att, w, start):
    rows = att[0].shape[1]

    def kernel(*refs):
        *att_refs, w_ref, out_ref = refs
        att = lanes_of([[r] for r in att_refs])
        out_ref[...] = dot_nn(att, rows_of(w_ref, start, w_ref.shape[1])).astype(bf16)

    out = like((rows, w.shape[2]))
    return call(
        kernel,
        "attention_output",
        (2,),
        [blocks_by_rows(a, 2) for a in att] + [whole(w)],
        by_rows(out, 2),
        out,
    )(*att, w)


def swapped_rows(array):
    return pl.BlockSpec((array.shape[0] // 4, array.shape[1]), lambda i: ((i + 2) % 4, 0))


def middle_call(x, part, got, gains):
    def kernel(x_ref, part_ref, got_ref, gain_ref, mid_ref, out_ref):
        middle = x_ref[...].astype(f32) + (part_ref[...].astype(f32) + got_ref[...].astype(f32))
        mid_ref[...] = middle
        hats, _ = normalize(middle)
        out_ref[...] = (hats * gain_ref[1:2, :]).astype(bf16)

    tile = by_rows(x, 4)
    return call(
        kernel,
        "second_norm",
        (4,),
        [tile, tile, swapped_rows(got), whole(gains)],
        [tile, tile],
        [like(x.shape, f32), like(x.shape)],
    )(x, part, got, gains)


def lift_call(x, up, gate):
    hidden = up.shape[0] * up.shape[1]

    def kernel(x_ref, up_ref, gate_ref, hid_ref, to_in_ref, to_gate_ref):
        x = x_ref[...]
        w_up, w_gate = (r[...].reshape(hidden, -1) for r in (up_ref, gate_ref))
        for start in range(0, hidden, 512):
            part = slice(start, min(start + 512, hidden))
            lifted = dot_nt(x, w_up[part])
            gate = dot_nt(x, w_gate[part])
            phi = 0.5 * (1.0 + lax.erf(lifted * (0.5**0.5)))
            gelu = lifted * phi
            slope = phi + lifted * jnp.exp(-0.5 * lifted * lifted) * 0.3989422804014327
            hid_ref[:, part] = (gelu * gate).astype(bf16)
            to_in_ref[:, part] = (gate * slope).astype(bf16)
            to_gate_ref[:, part] = gelu.astype(bf16)

    out = like((x.shape[0], hidden))
    return call(
        kernel,
        "expand",
        (2,),
        [by_rows(x, 2), whole(up), whole(gate)],
        [by_rows(out, 2)] * 3,
        [out] * 3,
    )(x, up, gate)


def lower_call(hidden, w, middle):
    rows, width = middle.shape

    def kernel(hid_ref, w_ref, mid_ref, own_ref, oth_ref):
        total = dot_nn(hid_ref[...], w_ref[...].reshape(-1, width))

        @pl.when(pl.program_id(0) == 1)
        def _():
            own_ref[...] = mid_ref[...] + total

        @pl.when(pl.program_id(0) == 0)
        def _():
            oth_ref[...] = total.astype(bf16)

    first = pl.BlockSpec((rows // 2, width), lambda i: (0, 0))
    return call(
        kernel,
        "contract",
        (2,),
        [pl.BlockSpec((rows // 2, hidden.shape[1]), lambda i: (1 - i, 0)), whole(w), first],
        [first, first],
        [like((rows // 2, width), f32), like((rows // 2, width))],
    )(hidden, w, middle)


def output_call(own, got, index):
    def kernel(index_ref, own_ref, got_ref, out_ref):
        out_ref[...] = (pick(own_ref, index_ref) + pick(got_ref, index_ref).astype(f32)).astype(bf16)

    tile = by_rows(own, 2)
    return call(kernel, "layer_output", (2,), [scalars, tile, tile], tile, like(own.shape))(
        index, own, got
    )


def weight_gradient_call(lefts, right, blocks, split, extra=None, groups=1):
    flat = lefts[0].ndim == 2
    columns = lefts[0].shape[1] // blocks if flat else sum(a.shape[2] for a in lefts[::groups])
    more = [] if extra is None else [extra]
    lead = sum(e.shape[0] for e in more)
    height = lead + columns
    width = right.shape[1]
    half = blocks // 2

    def kernel(*refs):
        left_refs = refs[: len(lefts)]
        right_ref = refs[len(lefts)]
        extra_refs = refs[len(lefts) + 1 : len(lefts) + 1 + len(more)]
        outs = refs[len(lefts) + 1 + len(more) :]
        left = left_refs[0][...] if flat else lanes_of(paired(left_refs, groups))

        def put(ref, place, values, part):
            ref[place, lead:] = values
            for e in extra_refs:
                ref[place, :lead] = e[:, part]

        for start in range(0, width, 512):
            grads = dot_tn(left, right_ref[:, start : start + 512]).astype(bf16)
            for z in range(blocks):
                block = grads[z * columns : (z + 1) * columns]
                if not split:
                    put(outs[0], (z, slice(start, start + 512)), block, None)
                    continue
                mine, x_rest, y_rest, to_x, to_y = outs
                for j in range(start // 256, start // 256 + 2):
                    part = slice(256 * j, 256 * j + 256)
                    values = block[:, 256 * j - start : 256 * j - start + 256]
                    if j == 0:
                        put(mine, z, values, part)
                    elif j == 1:
                        put(*((to_x, half + z) if z < half else (x_rest, z - half)), values, part)
                    elif j == 2:
                        put(*((y_rest, z) if z < half else (to_y, z)), values, part)
                    else:
                        put(*((to_x, z) if z < half else (to_y, z - half)), values, part)

    if split:
        out_shape = [like((n, height, width // 4)) for n in (blocks, half, half, blocks, blocks)]
    else:
        out_shape = [like((blocks, height, width))]

        def kernel(*refs):
            left_refs = refs[: len(lefts)]
            right_ref, out_ref = refs[len(lefts)], refs[-1]
            left = left_refs[0][...] if flat else lanes_of(paired(left_refs, groups))
            grads = dot_tn(left, right_ref[...]).astype(bf16)
            for z in range(blocks):
                out_ref[z, lead:] = grads[z * columns : (z + 1) * columns]
                if more:
                    out_ref[z, :lead] = refs[len(lefts) + 1][...]

    return call(
        kernel,
        "weight_gradient",
        (1,),
        [whole(a) for a in (*lefts, right, *more)],
        [whole(o) for o in out_shape],
        [kept(o) for o in out_shape],
    )(*((*in_hbm(*lefts), right) if groups > 1 else (*lefts, right)), *more)


def combine_call(first, second, x_got, y_got, near_rows):
    operands, out_shape = [], []
    if first is not None:
        operands += first[1:]
        out_shape += [like(first[1].shape)] * 2
    if second is not None:
        operands += second
        out_shape += [like(second[0].shape)]

    def kernel(*refs):
        ins, outs = list(refs[2 : 2 + len(operands)]), list(refs[2 + len(operands) :])
        x_ref, y_ref = refs[:2]
        if first is not None:
            x_rest, y_rest, x_out, y_out = ins.pop(0), ins.pop(0), outs.pop(0), outs.pop(0)
            half, rows = x_rest.shape[:2]
            for j in range(half):
                part = slice(j * rows, (j + 1) * rows)
                x_out[j] = (x_rest[j].astype(f32) + y_ref[part].astype(f32)).astype(bf16)
                y_out[j] = (y_rest[j].astype(f32) + x_ref[part].astype(f32)).astype(bf16)
        if second is not None:
            mine, x_near, y_near = ins
            half, rows = mine.shape[0] // 2, mine.shape[1]
            for j in range(half):
                near = slice((half + j) * rows, (half + j + 1) * rows)
                far = slice(near_rows + j * rows, near_rows + (j + 1) * rows)
                for place, near_ref, far_ref in ((j, x_near, y_ref), (half + j, y_near, x_ref)):
                    total = mine[place].astype(f32) + near_ref[near].astype(f32)
                    outs[0][place] = (total + far_ref[far].astype(f32)).astype(bf16)

    results = call(
        kernel,
        "gradient_sums",
        (1,),
        [whole(a) for a in (x_got, y_got, *operands)],
        [whole(o) for o in out_shape],
        [kept(o) for o in out_shape],
    )(x_got, y_got, *operands)
    near = results[:2] if first is not None else None
    return near, results[-1] if second is not None else None


def hidden_back_call(dy, w, to_in, to_gate):
    hidden = to_in.shape[1]

    def kernel(dy_ref, w_ref, to_in_ref, to_gate_ref, in_ref, gate_ref):
        w = w_ref[...].reshape(hidden, -1)
        for start in range(0, hidden, 512):
            part = slice(start, min(start + 512, hidden))
            grad = dot_nt(dy_ref[...], w[part])
            in_ref[:, part] = (grad * to_in_ref[:, part].astype(f32)).astype(bf16)
            gate_ref[:, part] = (grad * to_gate_ref[:, part].astype(f32)).astype(bf16)

    tile = by_rows(to_in, 2)
    return call(
        kernel,
        "grad_lifted",
        (2,),
        [by_rows(dy, 2), whole(w), tile, tile],
        [tile, tile],
        [like(to_in.shape)] * 2,
    )(dy, w, to_in, to_gate)


def two_part_call(grad_in, grad_gate, up, gate):
    width = up.shape[2]

    def kernel(in_ref, gate_ref, up_ref, w_gate_ref, out_ref):
        total = dot_nn(in_ref[...], up_ref[...].reshape(-1, width))
        total += dot_nn(gate_ref[...], w_gate_ref[...].reshape(-1, width))
        out_ref[...] = total.astype(bf16)

    out = like((grad_in.shape[0], width))
    return call(
        kernel,
        "grad_normed_two",
        (2,),
        [by_rows(grad_in, 2), by_rows(grad_gate, 2), whole(up), whole(gate)],
        by_rows(out, 2),
        out,
    )(grad_in, grad_gate, up, gate)


def two_back_call(part, got, middle, dy, gains):
    rows, width = middle.shape

    def kernel(part_ref, got_ref, mid_ref, dy_ref, gain_ref, grad_ref, low_ref, gain_grad_ref):
        i = pl.program_id(0)
        grads = part_ref[...].astype(f32) + got_ref[...].astype(f32)
        back, gain_grad = unnormalize(grads, mid_ref[...], gain_ref[1:2, :])
        grad = dy_ref[...].astype(f32) + back
        low_ref[...] = grad.astype(bf16)

        @pl.when(i == 0)
        def _():
            gain_grad_ref[...] = jnp.zeros_like(gain_grad_ref)

        @pl.when(i < 2)
        def _():
            grad_ref[...] = grad
            gain_grad_ref[...] += jnp.broadcast_to(gain_grad, gain_grad_ref.shape)

    tile = by_rows(middle, 4)
    row = like((8, width), f32)
    return call(
        kernel,
        "second_norm_gradient",
        (4,),
        [tile, swapped_rows(got), tile, tile, whole(gains)],
        [
            pl.BlockSpec((rows // 4, width), lambda i: (jnp.minimum(i, 1), 0)),
            tile,
            whole(row),
        ],
        [like((rows // 2, width), f32), like(middle.shape), row],
    )(part, got, middle, dy, gains)


def att_grad_call(grad, w, start):
    blocks = w.shape[0]
    columns = w.shape[1] - start

    def kernel(g_ref, w_ref, out_ref):
        out = dot_nt(g_ref[...], rows_of(w_ref, start, w_ref.shape[1])).astype(bf16)
        for z in range(blocks):
            out_ref[z] = out[:, z * columns : (z + 1) * columns]

    out = like((blocks, grad.shape[0], columns))
    return call(
        kernel,
        "grad_attended",
        (2,),
        [by_rows(grad, 2), whole(w)],
        blocks_by_rows(out, 2),
        out,
    )(grad, w)


def one_part_call(queries, keys_values, w, start):
    rows, width = queries[0].shape[1], w.shape[2]
    count = len(queries)

    def kernel(*refs):
        *left_refs, w_ref, own_ref, oth_ref = refs
        total = dot_nn(lanes_of(paired(left_refs, count)), rows_of(w_ref, start, start + 384))

        @pl.when(pl.program_id(0) == 1)
        def _():
            own_ref[...] = total

        @pl.when(pl.program_id(0) == 0)
        def _():
            oth_ref[...] = total.astype(bf16)

    def half(array):
        shape = (array.shape[0], rows // 2, array.shape[2])
        return pl.BlockSpec(shape, lambda i: (0, 1 - i, 0))

    first = pl.BlockSpec((rows // 2, width), lambda i: (0, 0))
    return call(
        kernel,
        "grad_normed_one",
        (2,),
        [half(a) for a in (*queries, *keys_values)] + [whole(w)],
        [first, first],
        [like((rows // 2, width), f32), like((rows // 2, width))],
    )(*in_hbm(*queries, *keys_values, w))


def one_back_call(own, got, x, grad_middle, gains, gain_two, index):
    rows, width = own.shape

    def kernel(
        index_ref, own_ref, got_ref, x_ref, mid_ref, gain_ref, gain_two_ref, grad_ref, gain_grad_ref,
        total_ref, low_ref,
    ):
        i = pl.program_id(0)
        grads = own_ref[...] + got_ref[...].astype(f32)
        back, gain_grad = unnormalize(grads, x_ref[...].astype(f32), gain_ref[0:1, :])
        low_ref[...] = (mid_ref[...] + back).astype(bf16)
        grad_ref[...] = pick(low_ref, index_ref)

        @pl.when(i == 0)
        def _():
            total_ref[...] = gain_grad

        @pl.when(i == 1)
        def _():
            total = total_ref[...] + gain_grad
            row = lax.broadcasted_iota(jnp.int32, gain_grad_ref.shape, 0)
            both = jnp.where(row == 0, total, jnp.where(row == 1, gain_two_ref[0:1, :], 0.0))
            gain_grad_ref[...] = both.astype(bf16)

    tile = by_rows(own, 2)
    x_tile = pl.BlockSpec((rows // 2, width), lambda i: (i, 0))
    gain_grads = like((16, width))
    return call(
        kernel,
        "first_norm_gradient",
        (2,),
        [scalars, tile, tile, x_tile, tile, whole(gains), whole(gain_two)],
        [tile, whole(gain_grads)],
        [like(own.shape), gain_grads],
        [pltpu.VMEM((1, width), f32), pltpu.VMEM((rows // 2, width), bf16)],
    )(index, own, got, x, grad_middle, gains, gain_two)


(
    X_IN,
    COT,
    BOTH,
    LOW,
    COLUMN,
    W,
    NEAR,
    GRAD,
    PAIR,
    TABLES,
    REST,
    X0,
    X_OWN,
    GAINS,
    X,
    NORMED,
    QKV,
    ATT,
    LSE,
    Y1,
    PART,
    Y_OWN,
    MIDDLE,
    NORMED_TWO,
    HIDDEN,
    TO_IN,
    TO_GATE,
    DY,
    G,
    F,
    N,
    SUM,
    G_GATE,
    OUT,
    DQ,
    DKV,
    G_ATT,
    GRAD_MID,
    MID_LOW,
    GAIN_TWO,
    OUT1,
    OWN,
    OTHER,
    DX,
    OUT0,
    DX1,
    DX0,
    INPUT_GRADS,
    OUTPUTS,
    UPDATED,
) = range(50)


def make_per_device(dp, tensor):
    count = dp * tensor
    chips = dp // 2
    chip_bits = chips.bit_length() - 1
    square = chip_bits == 2
    half = tensor // 2

    def permute(value, pairs):
        return lax.ppermute(value, AXES, pairs)

    def exchange(value, mask):
        return permute(value, [(i, i ^ mask) for i in range(count)])

    def over_chip(value, bit):
        return exchange(value, (2 * tensor) << bit)

    def over_core(value, pieces=1):
        rows = value.shape[0] // pieces
        got = [exchange(value[i * rows : (i + 1) * rows], tensor) for i in range(pieces)]
        return got[0] if pieces == 1 else jnp.concatenate(got, axis=0)

    def spread_pairs(r):
        pairs = []
        for i in range(count):
            z = i % tensor
            core = (i // tensor) % 2
            chip = i // (2 * tensor)
            pairs.append((i, (chip * 2 + z % 2) * tensor + (r ^ (z // 2)) * 2 + core))
        return pairs

    def by_column(blocks, me_z):
        for bit in range(tensor.bit_length() - 1):
            odd = (me_z >> bit) % 2 == 1
            blocks = [jnp.where(odd, blocks[k ^ (1 << bit)], blocks[k]) for k in range(tensor)]
        return blocks

    inner = [(i, i ^ 3) for i in range(count) if i % tensor in (1, 2)]
    outward = [(i, i ^ 1) for i in range(count) if i % tensor in (1, 2)]

    def gather_near_z(rows, me_z):
        got = exchange(rows, 1)
        low = me_z % 2 == 0
        return jnp.stack([jnp.where(low, rows, got), jnp.where(low, got, rows)])

    def gather_far_z(pair, got, me_z):
        sent = permute(got, outward)
        other = jnp.where((me_z == 0) | (me_z == 3), sent, got)
        low = me_z < 2
        return jnp.concatenate([jnp.where(low, pair, other), jnp.where(low, other, pair)], axis=0)

    def gather_plane(columns):
        current = columns[None]
        for bit in range(chip_bits):
            current = jnp.concatenate([current, over_chip(current, bit)], axis=0)
        return current.transpose(1, 2, 0, 3).reshape(columns.shape[:2] + (-1,))

    def low_sum(*values):
        return sum(v.astype(f32) for v in values).astype(bf16)

    def reduce_plane(parts):
        current = parts
        for bit in reversed(range(chip_bits)):
            middle = current.shape[0] // 2
            current = low_sum(current[:middle], over_chip(current[middle:], bit))
        return current[0]

    def reduce_column(blocks):
        result = blocks[0].astype(f32)
        for k in range(1, tensor):
            result = result + exchange(blocks[k], k).astype(f32)
        return result

    def per_device(
        inputs,
        cotangent,
        attention_in,
        attention_out,
        expand_weight,
        contract_weight,
        norm_gains,
        attention_in_first,
        attention_in_second,
        attention_out_first,
        attention_out_second,
        expand_first,
        expand_second,
        contract_first,
        contract_second,
        gains_first,
        gains_second,
    ):
        block = attention_in.shape[0]
        head_columns = attention_in.shape[2]
        hidden_local = expand_weight.shape[2]
        local_rows = inputs.shape[2]
        me_dp = lax.axis_index("dp")
        me_z = lax.axis_index("tensor")
        core = me_dp % 2
        z_high = me_z // 2

        me_chip = me_dp // 2
        index = me_chip ^ jnp.arange(chips, dtype=jnp.int32)
        aligned = block % 128 == 0
        kernel_index = index if aligned else jnp.zeros((1,), jnp.int32)

        def outside(values):
            if aligned:
                return values
            shaped = values.reshape(values.shape[0], chips, 2 * block)
            return jnp.take(shaped, index, axis=1).reshape(values.shape)

        def spread(values, r):
            part = lax.dynamic_index_in_dim(values[:, 0], r ^ z_high, 0, keepdims=False)
            return permute(part, spread_pairs(r))

        def collect(values, r):
            part = values[r * local_rows : (r + 1) * local_rows]
            return permute(part, [(b, a) for a, b in spread_pairs(r)])

        def assemble(first, second):
            odd = z_high == 1
            return jnp.stack([jnp.where(odd, second, first), jnp.where(odd, first, second)])[:, None]

        def rotary_tables():
            row_starts = [
                ((r ^ z_high) * 2 + (core ^ c)) * local_rows for c in range(2) for r in range(2)
            ]
            positions = jnp.concatenate([s + jnp.arange(local_rows) for s in row_starts]).astype(f32)
            exponents = jnp.arange(0, DH, 2).astype(f32) / DH
            angles = positions[:, None] * jnp.power(rope_theta, -exponents)[None, :]
            cosine, sine = jnp.cos(angles), jnp.sin(angles)
            cosine = jnp.concatenate([cosine] * 4, axis=-1)
            sine = jnp.concatenate([-sine, sine] * 2, axis=-1)
            return cosine, sine

        cut = (hidden_local // 2 + 15) // 16 * 16
        spare = 2 * cut - hidden_local
        head_cut = head_columns // 2
        low_in = attention_in.astype(bf16).reshape(block, 3, 2, head_cut).transpose(2, 1, 3, 0)
        low_out = attention_out.astype(bf16).reshape(block, 2, head_cut).transpose(1, 2, 0)
        low_expand = jnp.pad(expand_weight.astype(bf16).transpose(1, 2, 0), ((0, 0), (0, spare), (0, 0)))
        low_expand = low_expand.reshape(2, 2, cut, block).transpose(1, 0, 2, 3)
        low_contract = jnp.pad(contract_weight.astype(bf16).T, ((0, spare), (0, 0)))
        low_contract = low_contract.reshape(2, cut, block)
        low_gains = jnp.pad(norm_gains.astype(bf16), ((0, 14), (0, 0)))
        lead = low_gains.shape[0]
        both = jnp.concatenate(
            [
                jnp.stack([low_gains, low_gains]),
                low_in.reshape(2, -1, block),
                low_out,
                low_expand.reshape(2, -1, block),
                low_contract,
            ],
            axis=1,
        )
        out_start = lead + 3 * head_cut
        sizes = [out_start + head_cut, cut, cut, cut]
        starts = [sum(sizes[:k]) for k in range(len(sizes) + 1)]
        last = len(sizes)
        first_core = core == 0

        def side_by_side(mine, got):
            return jnp.concatenate(
                [jnp.where(first_core, mine, got), jnp.where(first_core, got, mine)], axis=-1
            )

        state = {X_IN: inputs, COT: cotangent, BOTH: both}
        held = []
        state_late = []
        again = []

        def run(work):
            nonlocal state
            new = {}
            late = held[:]
            held[:] = again
            again.clear()
            work(state, new)
            for values in late:
                new.update(values)
            state.update(new)
            names = list(state)
            state = dict(zip(names, lax.optimization_barrier([state[n] for n in names])))

        def column_direct(s, new, k):
            rows = s[LOW][starts[k] : starts[k + 1]]
            blocks = [rows] + [exchange(rows, j) for j in range(1, tensor)]
            new[COLUMN, k] = jnp.stack(by_column(blocks, me_z))

        def plane(s, new, k):
            if not square:
                if k < last:
                    new[W, k] = gather_plane(s.pop((COLUMN, k)))
                return
            sends, first_rows = ([], []), 0
            if k < last:
                column = s[COLUMN, k]
                first_rows = column.shape[0] * column.shape[1]
                for way in range(2):
                    sends[way].append(column.reshape(first_rows, -1))
            if k > 0:
                got = s[NEAR, k - 1]
                rows = half * sizes[k - 1]
                sends[0].append(got[1][rows : 2 * rows])
                sends[1].append(got[0][:rows])
            got = tuple(over_chip(jnp.concatenate(sends[way], axis=0), way) for way in range(2))
            if k < last:
                new[NEAR, k] = got
            if k > 0:
                new[W, k - 1] = weave_call(
                    s.pop((COLUMN, k - 1)), *s.pop((NEAR, k - 1)), *got, first_rows
                )

        step_rates = (
            2.5 * D ** (-0.5),
            2.5 * max(1, 4 * H * DH // SEQ) ** (-0.5),
            2.5 * D ** (-0.5),
            2.5 * FF ** (-0.5),
            0.25,
        )

        def joined(s, k, rows):
            return jnp.concatenate(s[GRAD, k], axis=0)[:rows]

        def joined_heads(s):
            parts = [g[lead:].reshape(3, head_cut, block) for g in s[GRAD, 4]]
            return lax.optimization_barrier(jnp.concatenate(parts, axis=1).transpose(2, 0, 1))

        def first_updates(s):
            grad_down, grad_up, grad_gate = (joined(s, k, hidden_local) for k in range(3))
            grad_expand = jnp.stack([grad_up, grad_gate]).transpose(2, 0, 1)
            grad_out, grad_expand, grad_down = lax.optimization_barrier(
                (joined(s, 3, head_columns).T, grad_expand, grad_down.T)
            )
            return (
                adamw_update(
                    attention_out, attention_out_first, attention_out_second, grad_out, step_rates[1]
                ),
                adamw_update(expand_weight, expand_first, expand_second, grad_expand, step_rates[2]),
                adamw_update(
                    contract_weight, contract_first, contract_second, grad_down, step_rates[3]
                ),
            )

        def f0(s, new):
            pair = s.pop(BOTH)
            mine = jnp.where(first_core, pair[0], pair[1])
            got = over_core(jnp.where(first_core, pair[1], pair[0]))
            new[LOW] = side_by_side(mine, got)

        run(f0)

        def f1(s, new):
            column_direct(s, new, 0)
            new[PAIR] = gather_near_z(s[LOW][starts[1] : starts[2]], me_z)
            new[TABLES] = rotary_tables()

        run(f1)

        def f2(s, new):
            plane(s, new, 0)
            up = s.pop(PAIR)
            rest = gather_near_z(s[LOW][starts[2] :], me_z)
            new[COLUMN, 1] = gather_far_z(up, permute(up, inner), me_z)
            new[REST] = (rest, permute(rest, inner))
            new[X0] = spread(s[X_IN], 0)

        run(f2)

        def f3(s, new):
            plane(s, new, 1)
            rest = gather_far_z(*s.pop(REST), me_z)
            new[COLUMN, 2], new[COLUMN, 3] = rest[:, :cut], rest[:, cut:]
            new[X_OWN] = jnp.concatenate([s.pop(X0), spread(s.pop(X_IN), 1)], axis=0)

        run(f3)

        def f4(s, new):
            plane(s, new, 2)
            rows = s.pop(X_OWN)
            x_raw = jnp.concatenate([rows, over_core(rows, 2)], axis=0)
            new[GAINS] = s[W, 0][0, :lead].astype(f32)
            new[X], new[NORMED] = norm_call(outside(x_raw), new[GAINS], kernel_index)
            query, key, value = qkv_call(new[NORMED], s[W, 0], lead, *s[TABLES])
            new[QKV] = (query, key, value)
            new[ATT, 0], new[LSE, 0] = attend_call(query, key, value, 0, tensor // 2)
            new[Y1] = spread(s[COT], 1)

        run(f4)

        def f5(s, new):
            plane(s, new, 3)
            new[ATT, 1], new[LSE, 1] = attend_call(*s[QKV], tensor // 2, tensor // 2)
            new[PART] = attention_output_call((s[ATT, 0], new[ATT, 1]), s[W, 0], out_start)
            new[Y_OWN] = jnp.concatenate([spread(s.pop(COT), 0), s.pop(Y1)], axis=0)

        run(f5)

        def f6(s, new):
            plane(s, new, 4)
            part, rows = s.pop(PART), s.pop(Y_OWN)
            new[MIDDLE], new[NORMED_TWO] = middle_call(
                s[X], part, over_core(part, 4), s[GAINS]
            )
            new[HIDDEN], new[TO_IN], new[TO_GATE] = lift_call(
                new[NORMED_TWO], s[W, 1], s[W, 2]
            )
            y_raw = jnp.concatenate([rows, over_core(rows)], axis=0)
            new[DY] = order_call(outside(y_raw), kernel_index)
            made(new, 0, [new[HIDDEN]], new[DY])

        def made(new, k, lefts, right, extra=None, groups=1):
            split = square and aligned
            grads = weight_gradient_call(lefts, right, tensor, split, extra, groups)
            if not split:
                (full,) = grads
                grads = full.reshape(full.shape[:2] + (chips, -1)).transpose(2, 0, 1, 3)
            new[G, k] = grads

        def plane_back(s, new, k):
            if not square:
                if (G, k) in s:
                    new[F, k] = [b for b in reduce_plane(s.pop((G, k)))]
                return
            flat = lambda a: a.reshape(-1, a.shape[-1])
            to_x, to_y, rows = [], [], 0
            if (G, k) in s:
                mine, x_rest, y_rest, x_out, y_out = s.pop((G, k))
                rows = x_out.shape[0] * x_out.shape[1]
                to_x.append(flat(x_out))
                to_y.append(flat(y_out))
            if (N, k - 1) in s:
                x_last, y_last, mine_last, x_near, y_near = s.pop((N, k - 1))
                to_x.append(flat(x_last))
                to_y.append(flat(y_last))
            x_got = over_chip(jnp.concatenate(to_x, axis=0), 0)
            y_got = over_chip(jnp.concatenate(to_y, axis=0), 1)
            first = (mine, x_rest, y_rest) if rows else None
            second = (mine_last, x_near, y_near) if len(to_x) > 1 or not rows else None
            near, far = combine_call(first, second, x_got, y_got, rows)
            if first is not None:
                new[N, k] = (*near, mine, x_got, y_got)
            if second is not None:
                new[F, k - 1] = far

        def whole_blocks(blocks):
            return blocks if square else jnp.stack(blocks)

        def scatter(s, k):
            total = lax.psum_scatter(
                whole_blocks(s.pop((F, k))), "tensor", scatter_dimension=0, tiled=False
            )
            held.append({(SUM, k): total})

        def column(s, new, *chunks):
            blocks = [by_column(s.pop((F, k)), me_z) for k in chunks]
            total = reduce_column([jnp.concatenate(b, axis=0) for b in zip(*blocks)])
            start = 0
            for k, b in zip(chunks, blocks):
                new[SUM, k] = total[start : start + b[0].shape[0]].astype(bf16)
                start += b[0].shape[0]

        def trade(s, new, *chunks):
            sums = [s.pop((SUM, k)) for k in chunks]
            total = jnp.concatenate(sums, axis=0)
            mine = jnp.where(first_core, total[:, :block], total[:, block:])
            got = over_core(jnp.where(first_core, total[:, block:], total[:, :block]))
            start = 0
            for k, rows in zip(chunks, [a.shape[0] for a in sums]):
                a, b = mine[start : start + rows], got[start : start + rows]
                new[GRAD, k] = (
                    jnp.where(first_core, a, b).astype(f32),
                    jnp.where(first_core, b, a).astype(f32),
                )
                start += rows

        run(f6)

        def s1(s, new):
            plane_back(s, new, 0)
            own, other = lower_call(s.pop(HIDDEN), s[W, 3], s[MIDDLE])
            g_in, g_gate = hidden_back_call(
                s[DY], s.pop((W, 3)), s.pop(TO_IN), s.pop(TO_GATE)
            )
            new[G_GATE] = g_gate
            new[PART] = two_part_call(g_in, g_gate, s.pop((W, 1)), s.pop((W, 2)))
            made(new, 1, [g_in], s[NORMED_TWO])
            new[OUT] = outside(output_call(own, over_core(other), kernel_index))

        run(s1)

        def attention_back(s, new, p):
            new[DQ, p], new[DKV, p] = attend_back_call(
                *s[QKV], s[G_ATT], s[ATT, p], s.pop((LSE, p)), *s[TABLES],
                p * (tensor // 2), tensor // 2,
            )

        def s2(s, new):
            plane_back(s, new, 1)
            part = s.pop(PART)
            new[GRAD_MID], new[MID_LOW], new[GAIN_TWO] = two_back_call(
                part, over_core(part, 4), s.pop(MIDDLE), s.pop(DY), s[GAINS]
            )
            made(new, 2, [s.pop(G_GATE)], s.pop(NORMED_TWO))
            s[G_ATT] = new[G_ATT] = att_grad_call(new[MID_LOW], s[W, 0], out_start)
            attention_back(s, new, 0)
            new[OUT1] = collect(s[OUT], 1)

        run(s2)

        def s3(s, new):
            scatter(s, 0)
            plane_back(s, new, 2)
            attention_back(s, new, 1)
            made(new, 3, [s[ATT, 0], s[ATT, 1]], s[MID_LOW], None, 2)
            new[OWN], new[OTHER] = one_part_call(
                (s[DQ, 0], new[DQ, 1]), (s[DKV, 0], new[DKV, 1]), s[W, 0], lead
            )

        run(s3)

        def s4(s, new):
            scatter(s, 1)
            plane_back(s, new, 3)
            dx, gain_grads = one_back_call(
                s.pop(OWN), over_core(s.pop(OTHER), 2), s.pop(X), s.pop(GRAD_MID),
                s[GAINS], s.pop(GAIN_TWO), kernel_index,
            )
            new[DX] = outside(dx)
            lefts = [s[DQ, 0], s[DQ, 1], s[DKV, 0], s[DKV, 1]]
            made(new, 4, lefts, s[NORMED], gain_grads, 2)
            new[OUT0] = collect(s[OUT], 0)

        run(s4)

        def s5(s, new):
            plane_back(s, new, 4)
            new[DX1] = collect(s[DX], 1)
            new[DX0] = collect(s[DX], 0)

        run(s5)

        def s6(s, new):
            scatter(s, 2)
            late = held.pop()
            plane_back(s, new, 5)
            column(s, new, 3)
            state_late.append(late)
            new[INPUT_GRADS] = assemble(s.pop(DX0), s.pop(DX1))
            new[OUTPUTS] = assemble(s.pop(OUT0), s.pop(OUT1))

        run(s6)

        def s7(s, new):
            column(s, new, 4)
            s.update(state_late.pop())
            trade(s, new, 0, 1, 2, 3)
            new[UPDATED] = first_updates(new)

        run(s7)

        def s8(s, new):
            trade(s, new, 4)

        run(s8)

        layer_output, input_gradient = state[OUTPUTS], state[INPUT_GRADS]
        grad_qkv = joined_heads(state)
        gain_total = sum(g[:2] for g in state[GRAD, 4])
        qkv_new = adamw_update(
            attention_in, attention_in_first, attention_in_second, grad_qkv, step_rates[0]
        )
        gains_new = adamw_update(norm_gains, gains_first, gains_second, gain_total, step_rates[4])
        out_new, expand_new, contract_new = state[UPDATED]
        return (
            layer_output,
            input_gradient,
            *qkv_new,
            *out_new,
            *expand_new,
            *contract_new,
            *gains_new,
        )

    return per_device


def solution(mesh):
    activation = P(None, "dp", "tensor", None)
    cube = P("dp", None, "tensor")
    flat = P("dp", "tensor")
    gain = P(None, "dp")
    return jax.shard_map(
        make_per_device(mesh.shape["dp"], mesh.shape["tensor"]),
        mesh=mesh,
        in_specs=(
            activation, activation, cube, flat, cube, flat, gain,
            cube, cube, flat, flat, cube, cube, flat, flat, gain, gain,
        ),
        out_specs=(
            activation, activation, cube, cube, cube, flat, flat, flat,
            cube, cube, cube, flat, flat, flat, gain, gain, gain,
        ),
        check_vma=False,
    )
```
